256 devices in a mesh: tm: 16 (over z_hi, y, core), dp: 16 (over z_lo, x).
Axes of the slice: x: 4, y: 4, z: 8 (z_hi: 2, z_lo: 4; z = z_hi * 4 + z_lo), core: 2. Of those that a mesh axis runs over, the one named last changes fastest.
Arguments:
- tokens: bfloat16 [16, 32, 64, 1152], P('dp', 'tm'), may hold values from -6 to 6
- clip_frames: int32 [16, 4], P('dp'), may hold values from 1 to 16, 32 in all within a row
- teacher_scores: float32 [16, 4, 8], P('dp'), may hold values from -4 to 4
- ln_gain: float32 [1152], replicated, may hold values from 0.25 to 1.75
- w_qkv: bfloat16 [1152, 3456], replicated, may hold values from -1 to 1
- w_out: bfloat16 [1152, 1152], replicated, may hold values from -0.1875 to 0.1875
- out_gain: float32 [1152], replicated, may hold values from 0.25 to 1.75
- reward_head: float32 [1152, 8], replicated, may hold values from -1.8856181 to 1.8856181
Outputs:
- scores: float32 [16, 4, 8], P('dp')
- grad_qkv: float32 [1152, 3456], P('dp')
- grad_out: float32 [1152, 1152], P('dp')
The draws below stay inside these ranges and needn't reach their ends.
Inputs may be any that keep to these rules, and one draw needn't show every extreme that they name: `clip_frames`: each row lists the lengths of 4 clips laid end to end over its 32 frames; the longest clip of every row has exactly 16 frames.
All inputs are finite; a program needn't handle non-finite values.
Results may differ from the reference program's by a relative error of at most 0.033.
Values may be sent and summed in bfloat16 or wider, within the bound.
No kernel may reach another device: no remote copies, remote signals or barrier semaphores. Data moves between devices by JAX's collectives and lax.ppermute only.
A program may use at most 128 MiB of HBM per device.

```python
import math
import jax
import jax.numpy as jnp
import numpy as np
from jax import lax

D = 1152
HEADS = 16
HEAD_DIM = 72
POS = 64
WINDOW = 8
CLIPS = 4
REWARDS = 8
FRAMES = 32
ROWS = 16
MOST = 16
N_TM = 16


def draw_tokens(key, part):
    key = jax.random.fold_in(key, 11)
    first_key = jax.random.fold_in(key, 0)
    full_shape = (ROWS, FRAMES, POS, D)
    values = jax.random.normal(first_key, full_shape, jnp.float32)
    return jnp.clip(values, -6.0, 6.0).astype(jnp.bfloat16)


def draw_w_qkv(key, part):
    key = jax.random.fold_in(key, 12)
    split_keys = jax.random.split(key, 1)
    fan_scale = D ** (-0.5)
    values = jax.random.normal(split_keys[0], (D, 3 * D), jnp.float32) * fan_scale
    return jnp.clip(values, -1.0, 1.0).astype(jnp.bfloat16)


def levels(stream_key, dims, pieces, least, largest):
    loudness, own = 1.0, jax.random.fold_in(stream_key, 6)
    for axis_at, parts in pieces:
        draws = jnp.exp(jax.random.uniform(jax.random.fold_in(own, axis_at), (parts,), jnp.float32, least / len(pieces), largest / len(pieces)))
        loudness = loudness * jnp.repeat(draws, dims[axis_at] // parts).reshape([-1 if axis == axis_at else 1 for axis in range(len(dims))])
    return loudness


def profile(count, total, reach, slope):
    loads = [(1 << 20) // math.isqrt(grade ** slope) + 1 for grade in range(2, count + 1)]
    spare, given = total - reach - (count - 1), [1] * (count - 1)
    while spare > 0:
        movable = [i for i in range(count - 1) if given[i] < reach]
        whole, remaining = sum([loads[i] for i in movable]), spare
        for i in movable:
            extra = min(reach - given[i], max(1, remaining * loads[i] // whole), spare)
            given[i] = given[i] + extra
            spare = spare - extra
    return np.array([reach] + given)


def uneven_parts(rng, number_of, total, reach, lean):
    if number_of == 2:
        one = jax.random.randint(rng, (), max(1, total - reach), min(reach, total - 1) + 1)
        return jnp.stack([one, total - one])
    sizes = jnp.asarray(profile(number_of, total, reach, lean), jnp.int32)
    pairs = (number_of - 1) // 2
    source_of, receiver = sizes[1:1 + 2 * pairs:2], sizes[2:2 + 2 * pairs:2]
    room = jnp.minimum(source_of - 1, reach - receiver)
    shifted = jax.random.randint(jax.random.fold_in(rng, 1), (pairs,), 0, 1 << 20) % (room + 1)
    sizes = sizes.at[1:1 + 2 * pairs:2].set(source_of - shifted).at[2:2 + 2 * pairs:2].set(receiver + shifted)
    return sizes[jax.random.permutation(jax.random.fold_in(rng, 2), number_of)]


def noise(rng, extent, deviation, most, pieces=(), kind=jnp.bfloat16):
    drawn = deviation * jax.random.normal(rng, extent, jnp.float32)
    if pieces:
        drawn = drawn * levels(rng, extent, pieces, -0.22, 0.18)
    return jnp.clip(drawn, -most, most).astype(kind)


def setup_inputs(seed: int = 0) -> dict:
    key_of = jax.random.split(jax.random.key(seed), 9)
    tokens = draw_tokens(jax.random.fold_in(key_of[8], 71), 0)
    clip_frames = jax.vmap(lambda own: uneven_parts(own, CLIPS, FRAMES, MOST, 2))(jax.random.split(key_of[1], ROWS)).reshape((ROWS, CLIPS)).astype(jnp.int32)
    teacher_scores = noise(key_of[2], (ROWS, CLIPS, REWARDS), 1.0, 4.0, ((0, 16),), jnp.float32)
    ln_gain = jnp.clip(1.0 + 0.15 * jax.random.normal(key_of[3], (D,), jnp.float32), 0.25, 1.75)
    w_qkv = draw_w_qkv(jax.random.fold_in(key_of[8], 71), 0)
    w_out = noise(key_of[5], (D, D), D ** -0.5, 0.1875)
    out_gain = jnp.clip(1.0 + 0.15 * jax.random.normal(key_of[6], (D,), jnp.float32), 0.25, 1.75)
    reward_head = noise(key_of[7], (D, REWARDS), (16 * D ** -0.5), 1.8856181, (), jnp.float32)
    return {"tokens": tokens, "clip_frames": clip_frames, "teacher_scores": teacher_scores, "ln_gain": ln_gain, "w_qkv": w_qkv, "w_out": w_out, "out_gain": out_gain, "reward_head": reward_head}


norm_eps = 1e-06
highest = lax.Precision.HIGHEST

def rounded(values):
    return lax.optimization_barrier(values.astype(jnp.bfloat16)).astype(jnp.float32)

def layer_norm(values, gain_vector):
    centre = values - lax.optimization_barrier(jnp.mean(values, axis=-1, keepdims=True))
    inv_std = lax.rsqrt(lax.optimization_barrier(jnp.mean(centre * centre, axis=-1, keepdims=True)) + norm_eps)
    normal_form = centre * inv_std
    return (normal_form * gain_vector, normal_form, inv_std)

def frame_clip(lengths, frame_ids):
    clip_ends = jnp.cumsum(lengths)
    return lax.optimization_barrier(jnp.sum((clip_ends[None, :] <= frame_ids[:, None]).astype(jnp.int32), axis=1)).astype(jnp.int32)

def one_row(row_tokens, lengths, targets, ln_gain, w_qkv, w_out, out_gain, reward_head):
    frames = FRAMES
    model_width = D
    score_scale = 1.0 / math.sqrt(HEAD_DIM)
    behind = WINDOW // 2
    ahead = WINDOW - behind - 1
    inputs = row_tokens.astype(jnp.float32)
    normed_full, _, _ = layer_norm(inputs, ln_gain)
    normed = normed_full.astype(jnp.bfloat16)
    projected = jnp.dot(normed.reshape(frames * POS, model_width), w_qkv, preferred_element_type=jnp.float32)
    projected = rounded(projected).reshape(frames, POS, 3, HEADS, HEAD_DIM)
    queries = projected[:, :, 0]
    key_rows = projected[:, :, 1]
    value_rows = projected[:, :, 2]
    clip_ids = frame_clip(lengths, jnp.arange(frames, dtype=jnp.int32))
    padding = ((behind, ahead), (0, 0), (0, 0), (0, 0))
    key_pad = jnp.pad(key_rows, padding)
    value_pad = jnp.pad(value_rows, padding)
    clip_pad = jnp.pad(clip_ids, (behind, ahead), constant_values=-1)
    key_window = jnp.stack([key_pad[offset:offset + frames] for offset in range(WINDOW)])
    value_window = jnp.stack([value_pad[offset:offset + frames] for offset in range(WINDOW)])
    allowed = jnp.stack([clip_pad[offset:offset + frames] == clip_ids for offset in range(WINDOW)])[:, :, None, None]
    logits = jnp.einsum('fphe,wfphe->wfph', queries, key_window) * score_scale
    masked = jnp.where(allowed, logits, -1e+30)
    row_peak = lax.optimization_barrier(jnp.max(masked, axis=0))
    exp_terms = jnp.exp(masked - row_peak)
    weights = exp_terms / lax.optimization_barrier(jnp.sum(exp_terms, axis=0))
    weights_low = rounded(weights)
    attended = rounded(jnp.einsum('wfph,wfphe->fphe', weights_low, value_window)).reshape(frames, POS, model_width)
    attended_low = attended.astype(jnp.bfloat16)
    mixed = inputs + jnp.dot(attended_low.reshape(frames * POS, model_width), w_out, preferred_element_type=jnp.float32).reshape(frames, POS, model_width)
    final_norm, centred, inv_std = layer_norm(mixed, out_gain)
    per_token = jnp.dot(final_norm.reshape(frames * POS, model_width), reward_head, precision=highest)
    frame_sums = lax.optimization_barrier(jnp.sum(per_token.reshape(frames, POS, REWARDS), axis=1))
    onehot = (clip_ids[:, None] == jnp.arange(CLIPS, dtype=jnp.int32)[None, :]).astype(jnp.float32)
    clip_sums = jnp.dot(onehot.T, frame_sums, precision=highest)
    counts = lengths.astype(jnp.float32) * POS
    scores = clip_sums / counts[:, None]
    residue = (scores - targets) / ROWS
    frame_grad = jnp.dot(jnp.dot(onehot, residue, precision=highest), reward_head.T, precision=highest)
    scaled = frame_grad[:, None, :] * out_gain
    mixed_grad = (scaled - lax.optimization_barrier(jnp.mean(scaled, axis=-1, keepdims=True)) - centred * lax.optimization_barrier(jnp.mean(scaled * centred, axis=-1, keepdims=True))) * inv_std
    mixed_grad_low = mixed_grad.astype(jnp.bfloat16)
    attended_grad = jnp.dot(mixed_grad_low.reshape(frames * POS, model_width), w_out.T, preferred_element_type=jnp.float32)
    attended_grad = rounded(attended_grad).reshape(frames, POS, HEADS, HEAD_DIM)
    weight_grad = jnp.einsum('fphe,wfphe->wfph', attended_grad, value_window)
    logit_grad = rounded(weights * (weight_grad - lax.optimization_barrier(jnp.sum(weights * weight_grad, axis=0))))
    query_grad = jnp.einsum('wfph,wfphe->fphe', logit_grad, key_window) * score_scale
    key_terms = jnp.einsum('wfph,fphe->wfphe', logit_grad, queries) * score_scale
    value_terms = jnp.einsum('wfph,fphe->wfphe', weights_low, attended_grad)
    key_grad_pad = jnp.zeros((frames + WINDOW - 1, POS, HEADS, HEAD_DIM), jnp.float32)
    value_grad_pad = jnp.zeros((frames + WINDOW - 1, POS, HEADS, HEAD_DIM), jnp.float32)
    for offset in range(WINDOW):
        key_grad_pad = key_grad_pad.at[offset:offset + frames].add(key_terms[offset])
        value_grad_pad = value_grad_pad.at[offset:offset + frames].add(value_terms[offset])
    key_grad = key_grad_pad[behind:behind + frames]
    value_grad = value_grad_pad[behind:behind + frames]
    projected_grad = jnp.stack([query_grad, key_grad, value_grad], axis=2).reshape(frames, POS, 3 * model_width)
    projected_grad = rounded(projected_grad)
    normed_blocks = normed.astype(jnp.float32).reshape(N_TM, 2 * POS, model_width)
    grad_blocks = projected_grad.reshape(N_TM, 2 * POS, 3 * model_width)
    qkv_parts = rounded(jnp.einsum('mtd,mte->mde', normed_blocks, grad_blocks))
    part_qkv = lax.optimization_barrier(jnp.sum(qkv_parts, axis=0))
    attended_blocks = attended.reshape(N_TM, 2 * POS, model_width)
    mixed_blocks = mixed_grad_low.astype(jnp.float32).reshape(N_TM, 2 * POS, model_width)
    out_parts = rounded(jnp.einsum('mtd,mte->mde', attended_blocks, mixed_blocks))
    part_out = lax.optimization_barrier(jnp.sum(out_parts, axis=0))
    return (scores, part_qkv, part_out)

def reference(tokens, clip_frames, teacher_scores, ln_gain, w_qkv, w_out, out_gain, reward_head):

    def row_step(totals, row_inputs):
        row_tokens, lengths, targets = row_inputs
        scores, part_qkv, part_out = one_row(row_tokens, lengths, targets, ln_gain, w_qkv, w_out, out_gain, reward_head)
        return ((totals[0] + part_qkv, totals[1] + part_out), scores)
    initial = (jnp.zeros((D, 3 * D), jnp.float32), jnp.zeros((D, D), jnp.float32))
    totals, scores = lax.scan(row_step, initial, (tokens, clip_frames, teacher_scores))
    return (scores, totals[0], totals[1])
```

```python
import math

import jax
import jax.numpy as jnp
from jax import lax
from jax.experimental import pallas as pl
from jax.experimental.pallas import tpu as pltpu
from jax.sharding import PartitionSpec as P

HEADS = 16
HEAD_DIM = 72
WINDOW = 8
D = 1152
TOK = 128
CLIPS = 4
REWARDS = 8
ROWS = 16
CHUNK = 384
PIECE = 18
EPS = 1e-06
SCALE = 1.0 / math.sqrt(HEAD_DIM)

f32 = jnp.float32
bf16 = jnp.bfloat16
HI = lax.Precision.HIGHEST
VMEM = pl.BlockSpec(memory_space=pltpu.VMEM)
SMEM = pl.BlockSpec(memory_space=pltpu.SMEM)
ANY = pl.BlockSpec(memory_space=pl.ANY)


def dot(a, b, ca, cb, precision=None):
    return lax.dot_general(
        a, b, (((ca,), (cb,)), ((), ())), preferred_element_type=f32, precision=precision
    )


def clip_of(lens, frame):
    end, clip = lens[0], jnp.zeros_like(frame)
    for c in range(CLIPS):
        clip += (frame >= end).astype(jnp.int32)
        if c + 1 < CLIPS:
            end = end + lens[c + 1]
    return clip


def span(h):
    low = HEAD_DIM * h
    return low // 128 * 128, -(-(low + HEAD_DIM) // 128) * 128


def lane_mask(h):
    start, end = span(h)
    lane = lax.broadcasted_iota(jnp.int32, (1, end - start), 1) + (start - HEAD_DIM * h)
    return ((lane >= 0) & (lane < HEAD_DIM)).astype(f32).astype(bf16)


def standard(values):
    centre = values - jnp.mean(values, axis=-1, keepdims=True)
    inv_std = lax.rsqrt(jnp.mean(centre * centre, axis=-1, keepdims=True) + EPS)
    return centre * inv_std, inv_std


def place_rows(src, dst, pos, x_first):
    for k in range(64):
        first, second, kz = k // 16, k // 4 % 4, k % 4
        kx, ky = (first, second) if x_first else (second, first)
        dp = ((pos[2] + kz) & 3) * 4 + ((pos[0] + kx) & 3)
        start = dp * 72 + ((pos[1] + ky) & 3) * PIECE
        dst[PIECE * k : PIECE * (k + 1), :] = src[pl.ds(start, PIECE), :]


def forward_kernel(
    lens, pos, x_ref, ln_ref, wq_hbm, wo_hbm, og_ref, rh_ref,
    proj_ref, p_ref, cen_ref, inv_ref, tot_ref, keep_ref, send_ref,
    wq, wo, acc, turned, placed, sems,
):
    count = 3 * D // CHUNK
    copies = []
    for j in range(count):
        cols = pl.ds(j * CHUNK, CHUNK)
        copies.append(pltpu.make_async_copy(wq_hbm.at[:, cols], wq.at[:, cols], sems.at[j]))
    copies.append(pltpu.make_async_copy(wo_hbm, wo, sems.at[count]))
    for copy in copies:
        copy.start()
    x = x_ref[...].astype(f32)
    norm, _ = standard(x)
    normed = (norm * ln_ref[...]).astype(bf16)
    for j in range(count):
        copies[j].wait()
        cols = slice(j * CHUNK, (j + 1) * CHUNK)
        proj_ref[:, cols] = dot(normed, wq[:, cols], 1, 0).astype(bf16)
    row = lax.broadcasted_iota(jnp.int32, (TOK, TOK), 0)
    col = lax.broadcasted_iota(jnp.int32, (TOK, TOK), 1)
    lag = (col >> 2) - (row >> 2)
    allowed = (
        ((row & 3) == (col & 3))
        & (lag >= -(WINDOW // 2))
        & (lag < WINDOW - WINDOW // 2)
        & (clip_of(lens, row >> 2) == clip_of(lens, col >> 2))
    )
    acc[...] = jnp.zeros_like(acc)
    for h in range(HEADS):
        a, b = span(h)
        mask = lane_mask(h)
        logits = dot(proj_ref[:, a:b] * mask, proj_ref[:, D + a : D + b], 1, 1) * SCALE
        masked = jnp.where(allowed, logits, -1e30)
        terms = jnp.exp(masked - jnp.max(masked, axis=1, keepdims=True))
        weights = terms / jnp.sum(terms, axis=1, keepdims=True)
        p_ref[h] = weights
        acc[:, a:b] += dot(
            weights.astype(bf16), proj_ref[:, 2 * D + a : 2 * D + b] * mask, 1, 0
        )
    attended = acc[...].astype(bf16)
    copies[count].wait()
    mixed = x_ref[...].astype(f32) + dot(attended, wo[...], 1, 0)
    centred, inv_std = standard(mixed)
    cen_ref[...] = centred
    inv_ref[...] = jnp.broadcast_to(inv_std, (TOK, 128))
    final = centred * og_ref[...]
    clip_row = lax.broadcasted_iota(jnp.int32, (8, TOK), 0)
    token = lax.broadcasted_iota(jnp.int32, (8, TOK), 1)
    onehot = (clip_of(lens, token >> 2) == clip_row).astype(f32)
    tot_ref[...] = dot(dot(onehot, final, 1, 0, HI), rh_ref[...], 1, 0, HI)
    turned[0] = normed.astype(f32).T
    turned[1] = attended.astype(f32).T
    place_rows(turned.at[0], placed, pos, True)
    keep_ref[0] = placed[...].astype(bf16)
    send_ref[0] = keep_ref[0]
    which = pos[3]
    place_rows(turned.at[which], placed, pos, False)
    keep_ref[1] = placed[...].astype(bf16)
    place_rows(turned.at[1 - which], placed, pos, False)
    send_ref[1] = placed[...].astype(bf16)


def forward(lens, pos, x, ln_gain, w_qkv, w_out, out_gain, reward_head):
    shape = jax.ShapeDtypeStruct
    return pl.pallas_call(
        forward_kernel,
        out_shape=(
            shape((TOK, 3 * D), bf16),
            shape((HEADS, TOK, TOK), f32),
            shape((TOK, D), f32),
            shape((TOK, 128), f32),
            shape((8, REWARDS), f32),
            shape((2, D, TOK), bf16),
            shape((2, D, TOK), bf16),
        ),
        in_specs=[SMEM, SMEM, VMEM, VMEM, ANY, ANY, VMEM, VMEM],
        out_specs=[VMEM] * 7,
        scratch_shapes=[
            pltpu.VMEM((D, 3 * D), bf16),
            pltpu.VMEM((D, D), bf16),
            pltpu.VMEM((TOK, D), f32),
            pltpu.VMEM((2, D, TOK), f32),
            pltpu.VMEM((D, TOK), f32),
            pltpu.SemaphoreType.DMA((3 * D // CHUNK + 1,)),
        ],
        compiler_params=pltpu.CompilerParams(vmem_limit_bytes=40 << 20),
        name="forward",
    )(lens, pos, x, ln_gain, w_qkv, w_out, out_gain, reward_head)


def backward_kernel(
    lens, pos, tot_ref, teacher_ref, og_ref, rh_ref, proj_ref, p_ref, cen_ref, inv_ref, wo_ref,
    scores_ref, keep_ref, send_ref,
    dq, dk, dv, da_ref,
):
    clip_row = lax.broadcasted_iota(jnp.int32, (8, REWARDS), 0)
    count = jnp.ones((8, REWARDS), f32)
    for c in range(CLIPS):
        count = jnp.where(clip_row == c, (lens[c] * 64).astype(f32), count)
    scores = jnp.sum(tot_ref[...], axis=0) / count
    scores_ref[...] = scores
    residue = jnp.where(clip_row < CLIPS, (scores - teacher_ref[...]) / ROWS, 0.0)
    clip_grad = dot(residue, rh_ref[...], 1, 1, HI) * og_ref[...]
    token = lax.broadcasted_iota(jnp.int32, (TOK, 8), 0)
    clip = lax.broadcasted_iota(jnp.int32, (TOK, 8), 1)
    onehot = (clip_of(lens, token >> 2) == clip).astype(f32)
    scaled = dot(onehot, clip_grad, 1, 0, HI)
    centred = cen_ref[...]
    mixed_grad = (
        scaled
        - jnp.mean(scaled, axis=-1, keepdims=True)
        - centred * jnp.mean(scaled * centred, axis=-1, keepdims=True)
    ) * inv_ref[:, 0:1]
    mixed_grad = mixed_grad.astype(bf16)
    da_ref[...] = dot(mixed_grad, wo_ref[...], 1, 1).astype(bf16)
    dq[...] = jnp.zeros_like(dq)
    dk[...] = jnp.zeros_like(dk)
    dv[...] = jnp.zeros_like(dv)
    for h in range(HEADS):
        a, b = span(h)
        mask = lane_mask(h)
        out_grad = da_ref[:, a:b] * mask
        weights = p_ref[h]
        weight_grad = dot(out_grad, proj_ref[:, 2 * D + a : 2 * D + b], 1, 1)
        inner = jnp.sum(weights * weight_grad, axis=1, keepdims=True)
        logit_grad = (weights * (weight_grad - inner)).astype(bf16)
        dq[:, a:b] += dot(logit_grad, proj_ref[:, D + a : D + b] * mask, 1, 0)
        dk[:, a:b] += dot(logit_grad, proj_ref[:, a:b] * mask, 0, 0)
        dv[:, a:b] += dot(weights.astype(bf16), out_grad, 0, 0)

    def store(ref_qk, ref_vo):
        ref_qk[0] = (dq[...] * SCALE).astype(bf16)
        ref_qk[1] = (dk[...] * SCALE).astype(bf16)
        ref_vo[0] = dv[...].astype(bf16)
        ref_vo[1] = mixed_grad

    @pl.when(pos[3] == 0)
    def _():
        store(keep_ref, send_ref)

    @pl.when(pos[3] != 0)
    def _():
        store(send_ref, keep_ref)


def backward(lens, pos, totals, teacher, out_gain, reward_head, proj, p, centred, inv, w_out):
    shape = jax.ShapeDtypeStruct
    return pl.pallas_call(
        backward_kernel,
        out_shape=(
            shape((8, REWARDS), f32),
            shape((2, TOK, D), bf16),
            shape((2, TOK, D), bf16),
        ),
        in_specs=[SMEM, SMEM] + [VMEM] * 9,
        out_specs=[VMEM] * 3,
        scratch_shapes=[pltpu.VMEM((TOK, D), f32)] * 3 + [pltpu.VMEM((TOK, D), bf16)],
        compiler_params=pltpu.CompilerParams(vmem_limit_bytes=32 << 20),
        name="backward",
    )(lens, pos, totals, teacher, out_gain, reward_head, proj, p, centred, inv, w_out)


def gradient_kernel(lk, lr, rk, rr, *outs):
    for i in range(2):
        right = jnp.concatenate([rk[i], rr[i]], axis=0)
        for k in range(4):
            rows = slice(288 * k, 288 * (k + 1))
            left = jnp.concatenate([lk[i, rows], lr[i, rows]], axis=1)
            outs[4 * i + k][...] = dot(left, right, 1, 0).astype(bf16)


def gradient(left_keep, left_recv, right_keep, right_recv):
    return pl.pallas_call(
        gradient_kernel,
        out_shape=(jax.ShapeDtypeStruct((288, D), bf16),) * 8,
        in_specs=[VMEM] * 4,
        out_specs=[VMEM] * 8,
        compiler_params=pltpu.CompilerParams(vmem_limit_bytes=24 << 20),
        name="gradient",
    )(left_keep, left_recv, right_keep, right_recv)


def total(refs):
    result = refs[0][...].astype(f32)
    for ref in refs[1:]:
        result += ref[...].astype(f32)
    return result


def first_sum_kernel(*refs):
    for i in range(2):
        result = total(refs[4 * i : 4 * i + 4])
        for k in range(4):
            refs[8 + 4 * i + k][...] = result[72 * k : 72 * (k + 1)].astype(bf16)


def first_sum(parts):
    return pl.pallas_call(
        first_sum_kernel,
        out_shape=(jax.ShapeDtypeStruct((72, D), bf16),) * 8,
        in_specs=[VMEM] * 8,
        out_specs=[VMEM] * 8,
        compiler_params=pltpu.CompilerParams(vmem_limit_bytes=24 << 20),
        name="first_sum",
    )(*parts)


def second_sum_kernel(*refs):
    sums = [total(refs[0:4]), total(refs[4:8])]
    rest = jnp.zeros((6, D), f32)
    for k in range(4):
        rows = slice(PIECE * k, PIECE * (k + 1))
        refs[8 + k][...] = jnp.concatenate(
            [sums[0][rows], rest, sums[1][rows], rest], axis=0
        ).astype(bf16)


def second_sum(parts):
    return pl.pallas_call(
        second_sum_kernel,
        out_shape=(jax.ShapeDtypeStruct((48, D), bf16),) * 4,
        in_specs=[VMEM] * 8,
        out_specs=[VMEM] * 4,
        name="second_sum",
    )(*parts)


def sum_kernel(*refs):
    refs[-1][...] = total(refs[:-1]).astype(bf16)


def plain_sum(parts):
    return pl.pallas_call(
        sum_kernel,
        out_shape=jax.ShapeDtypeStruct(parts[0].shape, bf16),
        in_specs=[VMEM] * len(parts),
        out_specs=VMEM,
        name="plain_sum",
    )(*parts)


def last_kernel(pos, mine, other, qkv_ref, out_ref, held):
    for k in range(4):
        y = (pos[1] - k) & 3
        held[pos[3], y] = mine[k].astype(f32)
        held[1 - pos[3], y] = other[k].astype(f32)
    for y in range(4):
        rows = slice(PIECE * y, PIECE * (y + 1))
        qkv_ref[rows, 0:D] = held[0, y, 0:PIECE]
        qkv_ref[rows, D : 2 * D] = held[0, y, 24 : 24 + PIECE]
        qkv_ref[rows, 2 * D : 3 * D] = held[1, y, 0:PIECE]
        out_ref[rows, :] = held[1, y, 24 : 24 + PIECE]


def last(pos, mine, other):
    return pl.pallas_call(
        last_kernel,
        out_shape=(
            jax.ShapeDtypeStruct((72, 3 * D), f32),
            jax.ShapeDtypeStruct((72, D), f32),
        ),
        in_specs=[SMEM, VMEM, VMEM],
        out_specs=[VMEM] * 2,
        scratch_shapes=[pltpu.VMEM((2, 4, 48, D), f32)],
        compiler_params=pltpu.CompilerParams(vmem_limit_bytes=16 << 20),
        name="last",
    )(pos, mine, other)


def to_core(block):
    return lax.ppermute(block, "tm", [(i, i ^ 1) for i in range(16)])


def to_far(block):
    return lax.ppermute(block, "tm", [(i, i ^ 8) for i in range(16)])


def along_y(block, k):
    return lax.ppermute(block, "tm", [(i, i & 9 | (i + 2 * k) & 6) for i in range(16)])


def along_x(block, k):
    return lax.ppermute(block, "dp", [(i, i & 12 | (i + k) & 3) for i in range(16)])


def along_z(block, k):
    return lax.ppermute(block, "dp", [(i, (i + 4 * k) & 15) for i in range(16)])


def spread(move, chunks):
    moved = {k: move(chunks[k], k) for k in (1, 3, 2)}
    return [chunks[0]] + [moved[k] for k in (1, 2, 3)]


def on_device(tokens, clip_frames, teacher_scores, ln_gain, w_qkv, w_out, out_gain, reward_head):
    tm, dp = lax.axis_index("tm"), lax.axis_index("dp")
    pos = jnp.stack([dp & 3, (tm >> 1) & 3, dp >> 2, tm & 1]).astype(jnp.int32)
    lens = clip_frames[0]
    out_gain = out_gain[None]
    by_place = tokens[0].reshape(2, 16, 4, D).transpose(1, 0, 2, 3).reshape(16, 8, D)
    x = lax.all_to_all(by_place, "tm", 0, 0, tiled=True).reshape(TOK, D)
    proj, p, centred, inv, partial, left_keep, left_send = forward(
        lens, pos, x, ln_gain[None], w_qkv, w_out, out_gain, reward_head
    )
    left_recv = to_core(left_send)
    totals = lax.all_to_all(
        jnp.broadcast_to(partial, (16, 8, REWARDS)), "tm", 0, 0, tiled=True
    )
    teacher = jnp.pad(teacher_scores[0], ((0, 8 - CLIPS), (0, 0)))
    scores, right_keep, right_send = backward(
        lens, pos, totals, teacher, out_gain, reward_head, proj, p, centred, inv, w_out
    )
    parts = gradient(left_keep, left_recv, right_keep, to_core(right_send))
    a, b = spread(along_x, parts[:4]), spread(along_y, parts[4:])
    parts = first_sum(a + b)
    a, b = spread(along_y, parts[:4]), spread(along_x, parts[4:])
    part = plain_sum(spread(along_z, second_sum(a + b)))
    part = plain_sum([part, to_far(part)])
    mine = jnp.stack(spread(along_y, [part] * 4))
    qkv_total, out_total = last(pos, mine, to_core(mine))
    return (scores[None, :CLIPS], qkv_total, out_total)


def solution(mesh):
    return jax.shard_map(
        on_device,
        mesh=mesh,
        in_specs=(
            P("dp", "tm", None, None),
            P("dp", None),
            P("dp", None, None),
            P(),
            P(),
            P(),
            P(),
            P(),
        ),
        out_specs=(P("dp", None, None), P("dp", None), P("dp", None)),
        check_vma=False,
    )
```

```python
import math

import jax
import jax.numpy as jnp
from jax import lax
from jax.experimental import pallas as pl
from jax.experimental.pallas import tpu as pltpu
from jax.sharding import PartitionSpec as P

HEADS = 16
HEAD_DIM = 72
WINDOW = 8
D = 1152
TOK = 128
CLIPS = 4
REWARDS = 8
ROWS = 16
CHUNK = 384
PIECE = 18
EPS = 1e-06
SCALE = 1.0 / math.sqrt(HEAD_DIM)

f32 = jnp.float32
bf16 = jnp.bfloat16
HI = lax.Precision.HIGHEST
VMEM = pl.BlockSpec(memory_space=pltpu.VMEM)
ANY = pl.BlockSpec(memory_space=pl.ANY)


def dot(a, b, ca, cb, precision=None):
    return lax.dot_general(
        a, b, (((ca,), (cb,)), ((), ())), preferred_element_type=f32, precision=precision
    )


def clip_of(small, frame):
    end, clip = small[10:11, 0:1], jnp.zeros_like(frame)
    for c in range(CLIPS):
        clip += (frame >= end).astype(f32)
        if c + 1 < CLIPS:
            end = end + small[10:11, c + 1 : c + 2]
    return clip


def frames(dims, axis):
    return (lax.broadcasted_iota(jnp.int32, dims, axis) >> 2).astype(f32)


def span(h):
    low = HEAD_DIM * h
    return low // 128 * 128, -(-(low + HEAD_DIM) // 128) * 128


def lane_mask(h):
    start, end = span(h)
    lane = lax.broadcasted_iota(jnp.int32, (1, end - start), 1) + (start - HEAD_DIM * h)
    return ((lane >= 0) & (lane < HEAD_DIM)).astype(f32).astype(bf16)


def standard(values):
    centre = values - jnp.mean(values, axis=-1, keepdims=True)
    inv_std = lax.rsqrt(jnp.mean(centre * centre, axis=-1, keepdims=True) + EPS)
    return centre * inv_std, inv_std


def position():
    tm, dp = lax.axis_index("tm"), lax.axis_index("dp")
    return dp & 3, (tm >> 1) & 3, dp >> 2, tm & 1


def shape(dims, kind):
    return jax.ShapeDtypeStruct(dims, kind)


def call(kernel, out_shape, in_specs, scratch, mib, name, flops=0, moved=0):
    return pl.pallas_call(
        kernel,
        out_shape=out_shape,
        in_specs=in_specs,
        out_specs=jax.tree.map(lambda _: VMEM, out_shape),
        scratch_shapes=scratch,
        compiler_params=pltpu.CompilerParams(vmem_limit_bytes=mib << 20),
        cost_estimate=pl.CostEstimate(flops=flops, bytes_accessed=moved, transcendentals=0),
        name=name,
    )


def regroup_kernel(x_ref, out_ref):
    for q in range(4):
        rows = [x_ref[a, 16 * q : 16 * (q + 1)].astype(f32) for a in range(2)]
        for k in range(4):
            piece = slice(4 * k, 4 * (k + 1))
            out_ref[4 * q + k] = jnp.concatenate([r[piece] for r in rows], axis=0).astype(bf16)


def regroup(tokens):
    return call(
        regroup_kernel, shape((16, 8, D), bf16), [VMEM], [], 4, "regroup", moved=600_000
    )(tokens)


def forward_kernel(
    x_ref, wq_any, wo_any, small,
    normed_ref, attended_ref, proj_ref, p_ref, cen_ref, inv_ref, tot_ref,
    acc, wq_ref, wo_ref, sems,
):
    count = 3 * D // CHUNK
    copies = []
    for j in range(count):
        cols = pl.ds(j * CHUNK, CHUNK)
        copies.append(pltpu.make_async_copy(wq_any.at[:, cols], wq_ref.at[:, cols], sems.at[j]))
    copies.append(pltpu.make_async_copy(wo_any, wo_ref, sems.at[count]))
    for copy in copies:
        copy.start()
    x = x_ref[...].astype(f32)
    norm, _ = standard(x)
    normed = (norm * small[9:10, :]).astype(bf16)
    normed_ref[...] = normed
    for j in range(count):
        copies[j].wait()
        cols = slice(j * CHUNK, (j + 1) * CHUNK)
        proj_ref[:, cols] = dot(normed, wq_ref[:, cols], 1, 0).astype(bf16)
    row = lax.broadcasted_iota(jnp.int32, (TOK, TOK), 0)
    col = lax.broadcasted_iota(jnp.int32, (TOK, TOK), 1)
    lag = (col >> 2) - (row >> 2)
    allowed = (
        ((row & 3) == (col & 3))
        & (lag >= -(WINDOW // 2))
        & (lag < WINDOW - WINDOW // 2)
        & (clip_of(small, frames((TOK, TOK), 0)) == clip_of(small, frames((TOK, TOK), 1)))
    )
    acc[...] = jnp.zeros_like(acc)
    for h in range(HEADS):
        a, b = span(h)
        mask = lane_mask(h)
        logits = dot(proj_ref[:, a:b] * mask, proj_ref[:, D + a : D + b], 1, 1) * SCALE
        masked = jnp.where(allowed, logits, -1e30)
        terms = jnp.exp(masked - jnp.max(masked, axis=1, keepdims=True))
        weights = terms / jnp.sum(terms, axis=1, keepdims=True)
        p_ref[h] = weights
        acc[:, a:b] += dot(
            weights.astype(bf16), proj_ref[:, 2 * D + a : 2 * D + b] * mask, 1, 0
        )
    attended = acc[...].astype(bf16)
    attended_ref[...] = attended
    copies[count].wait()
    mixed = x_ref[...].astype(f32) + dot(attended, wo_ref[...], 1, 0)
    centred, inv_std = standard(mixed)
    cen_ref[...] = centred
    inv_ref[...] = jnp.broadcast_to(inv_std, (TOK, 128))
    final = centred * small[8:9, :]
    clip_row = lax.broadcasted_iota(jnp.int32, (8, TOK), 0).astype(f32)
    onehot = (clip_of(small, frames((8, TOK), 1)) == clip_row).astype(f32)
    tot_ref[...] = dot(dot(onehot, final, 1, 0, HI), small[0:REWARDS, :], 1, 1, HI)


def forward(x, w_qkv, w_out, small):
    return call(
        forward_kernel,
        (
            shape((TOK, D), bf16),
            shape((TOK, D), bf16),
            shape((TOK, 3 * D), bf16),
            shape((HEADS, TOK, TOK), f32),
            shape((TOK, D), f32),
            shape((TOK, 128), f32),
            shape((8, REWARDS), f32),
        ),
        [VMEM, ANY, ANY, VMEM],
        [
            pltpu.VMEM((TOK, D), f32),
            pltpu.VMEM((D, 3 * D), bf16),
            pltpu.VMEM((D, D), bf16),
            pltpu.SemaphoreType.DMA((3 * D // CHUNK + 1,)),
        ],
        48,
        "forward",
        flops=2_000_000_000,
        moved=14_000_000,
    )(x, w_qkv, w_out, small)


def place_rows(src, dst, where, x_first):
    x, y, z, _ = where
    for k in range(64):
        first, second, kz = k // 16, k // 4 % 4, k % 4
        kx, ky = (first, second) if x_first else (second, first)
        dp = ((z + kz) & 3) * 4 + ((x + kx) & 3)
        start = dp * 72 + ((y + ky) & 3) * PIECE
        dst[PIECE * k : PIECE * (k + 1), :] = src[pl.ds(start, PIECE), :]


def turn_kernel(normed_ref, attended_ref, keep_ref, send_ref, turned, placed):
    where = position()
    core = where[3]
    turned[0] = normed_ref[...].astype(f32).T
    turned[1] = attended_ref[...].astype(f32).T
    place_rows(turned.at[0], placed, where, True)
    keep_ref[0] = placed[...].astype(bf16)
    send_ref[0] = keep_ref[0]
    place_rows(turned.at[core], placed, where, False)
    keep_ref[1] = placed[...].astype(bf16)
    place_rows(turned.at[1 - core], placed, where, False)
    send_ref[1] = placed[...].astype(bf16)


def turn(normed, attended):
    return call(
        turn_kernel,
        (shape((2, D, TOK), bf16), shape((2, D, TOK), bf16)),
        [VMEM] * 2,
        [pltpu.VMEM((2, D, TOK), f32), pltpu.VMEM((D, TOK), f32)],
        8,
        "turn",
        moved=4_000_000,
    )(normed, attended)


def backward_kernel(
    t0, t1, t2, t3, small, proj_ref, p_ref, cen_ref, inv_ref, wo_ref,
    scores_ref, keep_ref, send_ref,
    dq, dk, dv, da_ref, res_ref,
):
    clip_row = lax.broadcasted_iota(jnp.int32, (8, REWARDS), 0)
    count = jnp.ones((8, REWARDS), f32)
    for c in range(CLIPS):
        count = jnp.where(clip_row == c, small[10:11, c : c + 1] * 64.0, count)
    scores = ((t0[...] + t2[...]) + (t1[...] + t3[...])) / count
    scores_ref[...] = scores[0:CLIPS]
    res_ref[...] = jnp.zeros_like(res_ref)
    res_ref[0:CLIPS] = (scores[0:CLIPS] - small[12:16, 0:REWARDS]) / ROWS
    clip_grad = dot(res_ref[...], small[0:REWARDS, :], 1, 0, HI) * small[8:9, :]
    clip = lax.broadcasted_iota(jnp.int32, (TOK, 8), 1).astype(f32)
    onehot = (clip_of(small, frames((TOK, 8), 0)) == clip).astype(f32)
    scaled = dot(onehot, clip_grad, 1, 0, HI)
    centred = cen_ref[...]
    mixed_grad = (
        scaled
        - jnp.mean(scaled, axis=-1, keepdims=True)
        - centred * jnp.mean(scaled * centred, axis=-1, keepdims=True)
    ) * inv_ref[:, 0:1]
    mixed_grad = mixed_grad.astype(bf16)
    da_ref[...] = dot(mixed_grad, wo_ref[...], 1, 1).astype(bf16)
    dq[...] = jnp.zeros_like(dq)
    dk[...] = jnp.zeros_like(dk)
    dv[...] = jnp.zeros_like(dv)
    for h in range(HEADS):
        a, b = span(h)
        mask = lane_mask(h)
        out_grad = da_ref[:, a:b] * mask
        weights = p_ref[h]
        weight_grad = dot(out_grad, proj_ref[:, 2 * D + a : 2 * D + b], 1, 1)
        inner = jnp.sum(weights * weight_grad, axis=1, keepdims=True)
        logit_grad = (weights * (weight_grad - inner)).astype(bf16)
        dq[:, a:b] += dot(logit_grad, proj_ref[:, D + a : D + b] * mask, 1, 0)
        dk[:, a:b] += dot(logit_grad, proj_ref[:, a:b] * mask, 0, 0)
        dv[:, a:b] += dot(weights.astype(bf16), out_grad, 0, 0)

    def store(ref_qk, ref_vo):
        ref_qk[0] = (dq[...] * SCALE).astype(bf16)
        ref_qk[1] = (dk[...] * SCALE).astype(bf16)
        ref_vo[0] = dv[...].astype(bf16)
        ref_vo[1] = mixed_grad

    core = position()[3]

    @pl.when(core == 0)
    def _():
        store(keep_ref, send_ref)

    @pl.when(core != 0)
    def _():
        store(send_ref, keep_ref)


def backward(totals, small, proj, p, centred, inv, w_out):
    return call(
        backward_kernel,
        (
            shape((CLIPS, REWARDS), f32),
            shape((2, TOK, D), bf16),
            shape((2, TOK, D), bf16),
        ),
        [VMEM] * 10,
        [pltpu.VMEM((TOK, D), f32)] * 3
        + [
            pltpu.VMEM((TOK, D), bf16),
            pltpu.VMEM((8, REWARDS), f32),
        ],
        16,
        "backward",
        flops=1_500_000_000,
        moved=8_000_000,
    )(*totals, small, proj, p, centred, inv, w_out)


def gradient_kernel(lk, lr, rk, rr, *outs):
    for i in range(2):
        right = jnp.concatenate([rk[i], rr[i]], axis=0)
        for k in range(4):
            rows = slice(288 * k, 288 * (k + 1))
            left = jnp.concatenate([lk[i, rows], lr[i, rows]], axis=1)
            outs[SLOT[i][k]][...] = dot(left, right, 1, 0).astype(bf16)


SLOT = ((0, 3, 6, 5), (1, 2, 7, 4))


def gradient(left_keep, left_recv, right_keep, right_recv):
    return call(
        gradient_kernel,
        (shape((288, D), bf16),) * 8,
        [VMEM] * 4,
        [],
        16,
        "gradient",
        flops=1_400_000_000,
        moved=8_000_000,
    )(left_keep, left_recv, right_keep, right_recv)


def total(refs):
    result = refs[0][...].astype(f32)
    for ref in refs[1:]:
        result += ref[...].astype(f32)
    return result


def first_sum_kernel(*refs):
    for i in range(2):
        result = total([refs[SLOT[i][k]] for k in range(4)])
        for k in range(4):
            refs[8 + SLOT[1 - i][k]][...] = result[72 * k : 72 * (k + 1)].astype(bf16)


def first_sum(parts):
    return call(
        first_sum_kernel,
        (shape((72, D), bf16),) * 8,
        [VMEM] * 8,
        [],
        14,
        "first_sum",
        moved=8_000_000,
    )(*parts)


def second_sum_kernel(*refs):
    sums = [total([refs[SLOT[i][k]] for k in range(4)]) for i in (1, 0)]
    rest = jnp.zeros((4, D), f32)
    for k in range(4):
        rows = slice(PIECE * k, PIECE * (k + 1))
        refs[8 + k][...] = jnp.concatenate([sums[0][rows], sums[1][rows], rest], axis=0).astype(
            bf16
        )


def second_sum(parts):
    return call(
        second_sum_kernel,
        (shape((40, D), bf16),) * 4,
        [VMEM] * 8,
        [],
        6,
        "second_sum",
        moved=1_700_000,
    )(*parts)


def sum_kernel(*refs):
    refs[-1][...] = total(refs[:-1]).astype(bf16)


def plain_sum(parts):
    return call(
        sum_kernel,
        shape(parts[0].shape, bf16),
        [VMEM] * len(parts),
        [],
        3,
        "plain_sum",
        moved=500_000,
    )(*parts)


def last_kernel(*refs):
    qkv_ref, out_ref, held = refs[8:]
    _, y_here, _, core = position()
    for k in range(4):
        y = (y_here - k) & 3
        held[core, y] = refs[k][...].astype(f32)
        held[1 - core, y] = refs[4 + k][...].astype(f32)
    for y in range(4):
        rows = slice(PIECE * y, PIECE * (y + 1))
        qkv_ref[rows, 0:D] = held[0, y, 0:PIECE]
        qkv_ref[rows, D : 2 * D] = held[0, y, PIECE : 2 * PIECE]
        qkv_ref[rows, 2 * D : 3 * D] = held[1, y, 0:PIECE]
        out_ref[rows, :] = held[1, y, PIECE : 2 * PIECE]


def last(parts):
    return call(
        last_kernel,
        (shape((72, 3 * D), f32), shape((72, D), f32)),
        [VMEM] * 8,
        [pltpu.VMEM((2, 4, 40, D), f32)],
        10,
        "last",
        moved=2_000_000,
    )(*parts)


def to_core(block):
    return lax.ppermute(block, "tm", [(i, i ^ 1) for i in range(16)])


def to_far(block, core=0):
    return lax.ppermute(block, "tm", [(i, i ^ 8 ^ core) for i in range(16)])


def along_y(block, k):
    return lax.ppermute(block, "tm", [(i, i & 9 | (i + 2 * k) & 6) for i in range(16)])


def along_x(block, k):
    return lax.ppermute(block, "dp", [(i, i & 12 | (i + k) & 3) for i in range(16)])


def around_z(block, k):
    route = []
    for tm in range(16):
        for dp in range(16):
            step = {1: 1, 3: -1, 2: -2 if tm & 1 else 2}[k]
            z = ((tm >> 3) * 4 + (dp >> 2) + step) & 7
            there = (tm & 7 | (z >> 2) << 3) * 16 + ((z & 3) << 2 | dp & 3)
            route.append((tm * 16 + dp, there))
    return lax.ppermute(block, ("tm", "dp"), route)


def exchange(slots):
    moved = list(slots)
    for k in (1, 3, 2):
        moved[SLOT[1][k]] = along_y(slots[SLOT[1][k]], k)
        moved[SLOT[0][k]] = along_x(slots[SLOT[0][k]], k)
    return moved


def small_arrays(clip_frames, teacher, ln_gain, out_gain, reward_head):
    def wide(block):
        return jnp.pad(block, ((0, 0), (0, D - block.shape[1])))

    return jnp.concatenate(
        [
            reward_head.T,
            out_gain[None],
            ln_gain[None],
            wide(clip_frames.astype(f32)),
            jnp.zeros((1, D), f32),
            wide(teacher),
        ],
        axis=0,
    )


def on_device(tokens, clip_frames, teacher_scores, ln_gain, w_qkv, w_out, out_gain, reward_head):
    x = lax.all_to_all(regroup(tokens[0]), "tm", 0, 0, tiled=True).reshape(TOK, D)
    small = small_arrays(clip_frames, teacher_scores[0], ln_gain, out_gain, reward_head)
    normed, attended, proj, p, centred, inv, partial = forward(x, w_qkv, w_out, small)
    near, far, both = to_core(partial), to_far(partial), to_far(partial, 1)
    partial = (partial + near) + (far + both)
    totals = [partial] + [along_y(partial, k) for k in (1, 2, 3)]
    left_keep, left_send = turn(normed, attended)
    left_recv = to_core(left_send)
    scores, right_keep, right_send = backward(totals, small, proj, p, centred, inv, w_out)
    parts = gradient(left_keep, left_recv, right_keep, to_core(right_send))
    parts = second_sum(exchange(first_sum(exchange(parts))))
    part = plain_sum([parts[0]] + [around_z(parts[k], k) for k in (1, 2, 3)])
    part = plain_sum([part, to_far(part)])
    mine = [part] + [along_y(part, k) for k in (1, 2, 3)]
    qkv_total, out_total = last(mine + [to_core(block) for block in mine])
    return (scores[None], qkv_total, out_total)


def solution(mesh):
    return jax.shard_map(
        on_device,
        mesh=mesh,
        in_specs=(
            P("dp", "tm", None, None),
            P("dp", None),
            P("dp", None, None),
            P(),
            P(),
            P(),
            P(),
            P(),
        ),
        out_specs=(P("dp", None, None), P("dp", None), P("dp", None)),
        check_vma=False,
    )
```

```python
import math

import jax
import jax.numpy as jnp
from jax import lax
from jax.experimental import pallas as pl
from jax.experimental.pallas import tpu as pltpu
from jax.sharding import PartitionSpec as P

HEADS = 16
HEAD_DIM = 72
WINDOW = 8
D = 1152
TOK = 128
CLIPS = 4
REWARDS = 8
ROWS = 16
CHUNK = 384
PIECE = 18
EPS = 1e-06
SCALE = 1.0 / math.sqrt(HEAD_DIM)

f32 = jnp.float32
bf16 = jnp.bfloat16
HI = lax.Precision.HIGHEST
VMEM = pl.BlockSpec(memory_space=pltpu.VMEM)
ANY = pl.BlockSpec(memory_space=pl.ANY)


def dot(a, b, ca, cb, precision=None):
    return lax.dot_general(
        a, b, (((ca,), (cb,)), ((), ())), preferred_element_type=f32, precision=precision
    )


def clip_of(small, frame):
    end, clip = small[10:11, 0:1], jnp.zeros_like(frame)
    for c in range(CLIPS):
        clip += (frame >= end).astype(f32)
        if c + 1 < CLIPS:
            end = end + small[10:11, c + 1 : c + 2]
    return clip


def frames(dims, axis):
    return (lax.broadcasted_iota(jnp.int32, dims, axis) >> 2).astype(f32)


def span(h):
    low = HEAD_DIM * h
    return low // 128 * 128, -(-(low + HEAD_DIM) // 128) * 128


def lane_mask(h):
    start, end = span(h)
    lane = lax.broadcasted_iota(jnp.int32, (1, end - start), 1) + (start - HEAD_DIM * h)
    return ((lane >= 0) & (lane < HEAD_DIM)).astype(f32).astype(bf16)


def standard(values):
    centre = values - jnp.mean(values, axis=-1, keepdims=True)
    inv_std = lax.rsqrt(jnp.mean(centre * centre, axis=-1, keepdims=True) + EPS)
    return centre * inv_std, inv_std


def position():
    tm, dp = lax.axis_index("tm"), lax.axis_index("dp")
    return dp & 3, (tm >> 1) & 3, dp >> 2, tm & 1


def shape(dims, kind):
    return jax.ShapeDtypeStruct(dims, kind)


def call(kernel, out_shape, in_specs, scratch, mib, name, flops=0, moved=0):
    return pl.pallas_call(
        kernel,
        out_shape=out_shape,
        in_specs=in_specs,
        out_specs=jax.tree.map(lambda _: VMEM, out_shape),
        scratch_shapes=scratch,
        compiler_params=pltpu.CompilerParams(vmem_limit_bytes=mib << 20),
        cost_estimate=pl.CostEstimate(flops=flops, bytes_accessed=moved, transcendentals=0),
        name=name,
    )


def regroup_kernel(x_ref, out_ref):
    for q in range(4):
        rows = [x_ref[a, 16 * q : 16 * (q + 1)].astype(f32) for a in range(2)]
        for k in range(4):
            piece = slice(4 * k, 4 * (k + 1))
            out_ref[4 * q + k] = jnp.concatenate([r[piece] for r in rows], axis=0).astype(bf16)


def regroup(tokens):
    return call(
        regroup_kernel, shape((16, 8, D), bf16), [VMEM], [], 4, "regroup", moved=600_000
    )(tokens)


def forward_kernel(
    x_ref, wq_any, wo_any, small,
    normed_ref, attended_ref, proj_ref, p_ref, cen_ref, inv_ref, tot_ref,
    acc, wq_ref, wo_ref, sems,
):
    count = 3 * D // CHUNK
    copies = []
    for j in range(count):
        cols = pl.ds(j * CHUNK, CHUNK)
        copies.append(pltpu.make_async_copy(wq_any.at[:, cols], wq_ref.at[:, cols], sems.at[j]))
    copies.append(pltpu.make_async_copy(wo_any, wo_ref, sems.at[count]))
    for copy in copies:
        copy.start()
    x = x_ref[...].astype(f32)
    norm, _ = standard(x)
    normed = (norm * small[9:10, :]).astype(bf16)
    normed_ref[...] = normed
    for j in range(count):
        copies[j].wait()
        cols = slice(j * CHUNK, (j + 1) * CHUNK)
        proj_ref[:, cols] = dot(normed, wq_ref[:, cols], 1, 0).astype(bf16)
    row = lax.broadcasted_iota(jnp.int32, (TOK, TOK), 0)
    col = lax.broadcasted_iota(jnp.int32, (TOK, TOK), 1)
    lag = (col >> 2) - (row >> 2)
    allowed = (
        ((row & 3) == (col & 3))
        & (lag >= -(WINDOW // 2))
        & (lag < WINDOW - WINDOW // 2)
        & (clip_of(small, frames((TOK, TOK), 0)) == clip_of(small, frames((TOK, TOK), 1)))
    )
    acc[...] = jnp.zeros_like(acc)
    for h in range(HEADS):
        a, b = span(h)
        mask = lane_mask(h)
        logits = dot(proj_ref[:, a:b] * mask, proj_ref[:, D + a : D + b], 1, 1) * SCALE
        masked = jnp.where(allowed, logits, -1e30)
        terms = jnp.exp(masked - jnp.max(masked, axis=1, keepdims=True))
        weights = terms / jnp.sum(terms, axis=1, keepdims=True)
        p_ref[h] = weights
        acc[:, a:b] += dot(
            weights.astype(bf16), proj_ref[:, 2 * D + a : 2 * D + b] * mask, 1, 0
        )
    attended = acc[...].astype(bf16)
    attended_ref[...] = attended
    copies[count].wait()
    mixed = x_ref[...].astype(f32) + dot(attended, wo_ref[...], 1, 0)
    centred, inv_std = standard(mixed)
    cen_ref[...] = centred
    inv_ref[...] = jnp.broadcast_to(inv_std, (TOK, 128))
    final = centred * small[8:9, :]
    clip_row = lax.broadcasted_iota(jnp.int32, (8, TOK), 0).astype(f32)
    onehot = (clip_of(small, frames((8, TOK), 1)) == clip_row).astype(f32)
    tot_ref[...] = dot(dot(onehot, final, 1, 0, HI), small[0:REWARDS, :], 1, 1, HI)


def forward(x, w_qkv, w_out, small):
    return call(
        forward_kernel,
        (
            shape((TOK, D), bf16),
            shape((TOK, D), bf16),
            shape((TOK, 3 * D), bf16),
            shape((HEADS, TOK, TOK), f32),
            shape((TOK, D), f32),
            shape((TOK, 128), f32),
            shape((8, REWARDS), f32),
        ),
        [VMEM, ANY, ANY, VMEM],
        [
            pltpu.VMEM((TOK, D), f32),
            pltpu.VMEM((D, 3 * D), bf16),
            pltpu.VMEM((D, D), bf16),
            pltpu.SemaphoreType.DMA((3 * D // CHUNK + 1,)),
        ],
        48,
        "forward",
        flops=2_000_000_000,
        moved=14_000_000,
    )(x, w_qkv, w_out, small)


def place_rows(src, dst, where, x_first):
    x, y, z, _ = where
    for k in range(64):
        first, second, kz = k // 16, k // 4 % 4, k % 4
        kx, ky = (first, second) if x_first else (second, first)
        dp = ((z + kz) & 3) * 4 + ((x + kx) & 3)
        start = dp * 72 + ((y + ky) & 3) * PIECE
        dst[PIECE * k : PIECE * (k + 1), :] = src[pl.ds(start, PIECE), :]


def turn_kernel(normed_ref, attended_ref, keep_ref, send_ref, turned, placed):
    where = position()
    core = where[3]
    turned[0] = normed_ref[...].astype(f32).T
    turned[1] = attended_ref[...].astype(f32).T
    place_rows(turned.at[0], placed, where, True)
    keep_ref[0] = placed[...].astype(bf16)
    send_ref[0] = keep_ref[0]
    place_rows(turned.at[core], placed, where, False)
    keep_ref[1] = placed[...].astype(bf16)
    place_rows(turned.at[1 - core], placed, where, False)
    send_ref[1] = placed[...].astype(bf16)


def turn(normed, attended):
    return call(
        turn_kernel,
        (shape((2, D, TOK), bf16), shape((2, D, TOK), bf16)),
        [VMEM] * 2,
        [pltpu.VMEM((2, D, TOK), f32), pltpu.VMEM((D, TOK), f32)],
        8,
        "turn",
        moved=4_000_000,
    )(normed, attended)


def backward_kernel(
    t0, t1, t2, t3, small, proj_ref, p_ref, cen_ref, inv_ref, wo_ref,
    scores_ref, keep_ref, send_ref,
    dq, dk, dv, da_ref, res_ref,
):
    clip_row = lax.broadcasted_iota(jnp.int32, (8, REWARDS), 0)
    count = jnp.ones((8, REWARDS), f32)
    for c in range(CLIPS):
        count = jnp.where(clip_row == c, small[10:11, c : c + 1] * 64.0, count)
    scores = ((t0[...] + t2[...]) + (t1[...] + t3[...])) / count
    scores_ref[...] = scores[0:CLIPS]
    res_ref[...] = jnp.zeros_like(res_ref)
    res_ref[0:CLIPS] = (scores[0:CLIPS] - small[12:16, 0:REWARDS]) / ROWS
    clip_grad = dot(res_ref[...], small[0:REWARDS, :], 1, 0, HI) * small[8:9, :]
    clip = lax.broadcasted_iota(jnp.int32, (TOK, 8), 1).astype(f32)
    onehot = (clip_of(small, frames((TOK, 8), 0)) == clip).astype(f32)
    scaled = dot(onehot, clip_grad, 1, 0, HI)
    centred = cen_ref[...]
    mixed_grad = (
        scaled
        - jnp.mean(scaled, axis=-1, keepdims=True)
        - centred * jnp.mean(scaled * centred, axis=-1, keepdims=True)
    ) * inv_ref[:, 0:1]
    mixed_grad = mixed_grad.astype(bf16)
    da_ref[...] = dot(mixed_grad, wo_ref[...], 1, 1).astype(bf16)
    dq[...] = jnp.zeros_like(dq)
    dk[...] = jnp.zeros_like(dk)
    dv[...] = jnp.zeros_like(dv)
    for h in range(HEADS):
        a, b = span(h)
        mask = lane_mask(h)
        out_grad = da_ref[:, a:b] * mask
        weights = p_ref[h]
        weight_grad = dot(out_grad, proj_ref[:, 2 * D + a : 2 * D + b], 1, 1)
        inner = jnp.sum(weights * weight_grad, axis=1, keepdims=True)
        logit_grad = (weights * (weight_grad - inner)).astype(bf16)
        dq[:, a:b] += dot(logit_grad, proj_ref[:, D + a : D + b] * mask, 1, 0)
        dk[:, a:b] += dot(logit_grad, proj_ref[:, a:b] * mask, 0, 0)
        dv[:, a:b] += dot(weights.astype(bf16), out_grad, 0, 0)

    def store(ref_qk, ref_vo):
        ref_qk[0] = (dq[...] * SCALE).astype(bf16)
        ref_qk[1] = (dk[...] * SCALE).astype(bf16)
        ref_vo[0] = dv[...].astype(bf16)
        ref_vo[1] = mixed_grad

    core = position()[3]

    @pl.when(core == 0)
    def _():
        store(keep_ref, send_ref)

    @pl.when(core != 0)
    def _():
        store(send_ref, keep_ref)


def backward(totals, small, proj, p, centred, inv, w_out):
    return call(
        backward_kernel,
        (
            shape((CLIPS, REWARDS), f32),
            shape((2, TOK, D), bf16),
            shape((2, TOK, D), bf16),
        ),
        [VMEM] * 10,
        [pltpu.VMEM((TOK, D), f32)] * 3
        + [
            pltpu.VMEM((TOK, D), bf16),
            pltpu.VMEM((8, REWARDS), f32),
        ],
        16,
        "backward",
        flops=1_500_000_000,
        moved=8_000_000,
    )(*totals, small, proj, p, centred, inv, w_out)


PARTS = ((2, 0), (2, 1), (1, 1), (3, 0), (1, 0), (3, 1))


def gradient_kernel(lk, lr, rk, rr, *outs):
    for i in range(2):
        right = jnp.concatenate([rk[i], rr[i]], axis=0)
        for k in (2, 1, 3, 0):
            rows = slice(288 * k, 288 * (k + 1))
            left = jnp.concatenate([lk[i, rows], lr[i, rows]], axis=1)
            part = dot(left, right, 1, 0).astype(bf16)
            if k == 0:
                outs[7 * i + 6][...] = part
            else:
                for j, (distance, piece) in enumerate(PARTS):
                    if distance == k:
                        outs[7 * i + j][...] = part[144 * piece : 144 * (piece + 1)]


def gradient(left_keep, left_recv, right_keep, right_recv):
    parts = call(
        gradient_kernel,
        ((shape((144, D), bf16),) * 6 + (shape((288, D), bf16),)) * 2,
        [VMEM] * 4,
        [],
        16,
        "gradient",
        flops=1_400_000_000,
        moved=8_000_000,
    )(left_keep, left_recv, right_keep, right_recv)
    return parts[:7], parts[7:]


def relay_kernel(*refs):
    for k in range(4):
        refs[8 + k][...] = (refs[k][...].astype(f32) + refs[4 + k][...].astype(f32)).astype(bf16)


def relay(arrived, own):
    return call(
        relay_kernel,
        (shape((144, D), bf16),) * 4,
        [VMEM] * 8,
        [],
        8,
        "relay",
        moved=4_000_000,
    )(*arrived, *own)


def total(refs):
    result = refs[0][...].astype(f32)
    for ref in refs[1:]:
        result += ref[...].astype(f32)
    return result


SLOT = ((0, 3, 6, 5), (1, 2, 7, 4))


def first_sum_kernel(*refs):
    for i in range(2):
        plain_on, plain_back, relayed_on, relayed_back, own = (refs[2 * j + i] for j in range(5))
        result = own[...].astype(f32) + jnp.concatenate(
            [
                plain_back[...].astype(f32) + relayed_on[...].astype(f32),
                plain_on[...].astype(f32) + relayed_back[...].astype(f32),
            ],
            axis=0,
        )
        for k in range(4):
            refs[10 + SLOT[1 - i][k]][...] = result[72 * k : 72 * (k + 1)].astype(bf16)


def first_sum(parts):
    return call(
        first_sum_kernel,
        (shape((72, D), bf16),) * 8,
        [VMEM] * 10,
        [],
        12,
        "first_sum",
        moved=6_000_000,
    )(*parts)


def second_sum_kernel(*refs):
    sums = [total([refs[SLOT[i][k]] for k in range(4)]) for i in (1, 0)]
    rest = jnp.zeros((4, D), f32)
    for k in range(4):
        rows = slice(PIECE * k, PIECE * (k + 1))
        refs[8 + k][...] = jnp.concatenate([sums[0][rows], sums[1][rows], rest], axis=0).astype(
            bf16
        )


def second_sum(parts):
    return call(
        second_sum_kernel,
        (shape((40, D), bf16),) * 4,
        [VMEM] * 8,
        [],
        6,
        "second_sum",
        moved=1_700_000,
    )(*parts)


def sum_kernel(*refs):
    refs[-1][...] = total(refs[:-1]).astype(bf16)


def plain_sum(parts):
    return call(
        sum_kernel,
        shape(parts[0].shape, bf16),
        [VMEM] * len(parts),
        [],
        3,
        "plain_sum",
        moved=500_000,
    )(*parts)


def last_kernel(*refs):
    qkv_ref, out_ref, held = refs[8:]
    _, y_here, _, core = position()
    for k in range(4):
        y = (y_here - k) & 3
        held[core, y] = refs[k][...].astype(f32)
        held[1 - core, y] = refs[4 + k][...].astype(f32)
    for y in range(4):
        rows = slice(PIECE * y, PIECE * (y + 1))
        qkv_ref[rows, 0:D] = held[0, y, 0:PIECE]
        qkv_ref[rows, D : 2 * D] = held[0, y, PIECE : 2 * PIECE]
        qkv_ref[rows, 2 * D : 3 * D] = held[1, y, 0:PIECE]
        out_ref[rows, :] = held[1, y, PIECE : 2 * PIECE]


def last(parts):
    return call(
        last_kernel,
        (shape((72, 3 * D), f32), shape((72, D), f32)),
        [VMEM] * 8,
        [pltpu.VMEM((2, 4, 40, D), f32)],
        10,
        "last",
        moved=2_000_000,
    )(*parts)


def to_core(block):
    return lax.ppermute(block, "tm", [(i, i ^ 1) for i in range(16)])


def to_far(block, core=0):
    return lax.ppermute(block, "tm", [(i, i ^ 8 ^ core) for i in range(16)])


def along_y(block, k):
    return lax.ppermute(block, "tm", [(i, i & 9 | (i + 2 * k) & 6) for i in range(16)])


def along_x(block, k):
    return lax.ppermute(block, "dp", [(i, i & 12 | (i + k) & 3) for i in range(16)])


def around_z(block, k):
    route = []
    for tm in range(16):
        for dp in range(16):
            step = {1: 1, 3: -1, 2: -2 if tm & 1 else 2}[k]
            z = ((tm >> 3) * 4 + (dp >> 2) + step) & 7
            there = (tm & 7 | (z >> 2) << 3) * 16 + ((z & 3) << 2 | dp & 3)
            route.append((tm * 16 + dp, there))
    return lax.ppermute(block, ("tm", "dp"), route)


def exchange(slots):
    moved = list(slots)
    for k in (1, 3, 2):
        moved[SLOT[1][k]] = along_y(slots[SLOT[1][k]], k)
        moved[SLOT[0][k]] = along_x(slots[SLOT[0][k]], k)
    return moved


def around(x_half, y_half):
    on, back = (along_x, along_y), 3
    halves = (x_half, y_half)
    arrived = [on[i](halves[i][j], 1 if j == 0 else back) for j in range(2) for i in range(2)]
    plain = [on[i](halves[i][2 + j], 1 if j == 0 else back) for j in range(2) for i in range(2)]
    own = [halves[i][4 + j] for j in range(2) for i in range(2)]
    sums = relay(arrived, own)
    relayed = [on[i](sums[2 * j + i], 1 if j == 0 else back) for j in range(2) for i in range(2)]
    return first_sum(plain + relayed + [x_half[6], y_half[6]])


def small_arrays(clip_frames, teacher, ln_gain, out_gain, reward_head):
    def wide(block):
        return jnp.pad(block, ((0, 0), (0, D - block.shape[1])))

    return jnp.concatenate(
        [
            reward_head.T,
            out_gain[None],
            ln_gain[None],
            wide(clip_frames.astype(f32)),
            jnp.zeros((1, D), f32),
            wide(teacher),
        ],
        axis=0,
    )


def on_device(tokens, clip_frames, teacher_scores, ln_gain, w_qkv, w_out, out_gain, reward_head):
    x = lax.all_to_all(regroup(tokens[0]), "tm", 0, 0, tiled=True).reshape(TOK, D)
    small = small_arrays(clip_frames, teacher_scores[0], ln_gain, out_gain, reward_head)
    normed, attended, proj, p, centred, inv, partial = forward(x, w_qkv, w_out, small)
    near, far, both = to_core(partial), to_far(partial), to_far(partial, 1)
    partial = (partial + near) + (far + both)
    totals = [partial] + [along_y(partial, k) for k in (1, 2, 3)]
    left_keep, left_send = turn(normed, attended)
    left_recv = to_core(left_send)
    scores, right_keep, right_send = backward(totals, small, proj, p, centred, inv, w_out)
    parts = gradient(left_keep, left_recv, right_keep, to_core(right_send))
    parts = second_sum(exchange(around(*parts)))
    part = plain_sum([parts[0]] + [around_z(parts[k], k) for k in (1, 2, 3)])
    part = plain_sum([part, to_far(part)])
    other = to_core(part)
    mine = [along_y(part, k) for k in (1, 3, 2)]
    mine = [part, mine[0], mine[2], mine[1]]
    qkv_total, out_total = last(mine + [other] + [to_core(block) for block in mine[1:]])
    return (scores[None], qkv_total, out_total)


def solution(mesh):
    return jax.shard_map(
        on_device,
        mesh=mesh,
        in_specs=(
            P("dp", "tm", None, None),
            P("dp", None),
            P("dp", None, None),
            P(),
            P(),
            P(),
            P(),
            P(),
        ),
        out_specs=(P("dp", None, None), P("dp", None), P("dp", None)),
        check_vma=False,
    )
```

```python
import math

import jax
import jax.numpy as jnp
from jax import lax
from jax.experimental import pallas as pl
from jax.experimental.pallas import tpu as pltpu
from jax.sharding import PartitionSpec as P

HEADS = 16
HEAD_DIM = 72
WINDOW = 8
D = 1152
TOK = 128
CLIPS = 4
REWARDS = 8
ROWS = 16
CHUNK = 384
PIECE = 18
GROUP = 4
EPS = 1e-06
SCALE = 1.0 / math.sqrt(HEAD_DIM)

f32 = jnp.float32
bf16 = jnp.bfloat16
HI = lax.Precision.HIGHEST
VMEM = pl.BlockSpec(memory_space=pltpu.VMEM)
ANY = pl.BlockSpec(memory_space=pl.ANY)


def dot(a, b, ca, cb, precision=None):
    return lax.dot_general(
        a, b, (((ca,), (cb,)), ((), ())), preferred_element_type=f32, precision=precision
    )


def clip_of(small, frame):
    end, clip = small[10:11, 0:1], jnp.zeros_like(frame)
    for c in range(CLIPS):
        clip += (frame >= end).astype(f32)
        if c + 1 < CLIPS:
            end = end + small[10:11, c + 1 : c + 2]
    return clip


def frames(dims, axis):
    return (lax.broadcasted_iota(jnp.int32, dims, axis) >> 2).astype(f32)


def span(h):
    low = HEAD_DIM * h
    return low // 128 * 128, -(-(low + HEAD_DIM) // 128) * 128


def lane_mask(h):
    start, end = span(h)
    lane = lax.broadcasted_iota(jnp.int32, (1, end - start), 1) + (start - HEAD_DIM * h)
    return ((lane >= 0) & (lane < HEAD_DIM)).astype(f32).astype(bf16)


def standard(values):
    centre = values - jnp.mean(values, axis=-1, keepdims=True)
    inv_std = lax.rsqrt(jnp.mean(centre * centre, axis=-1, keepdims=True) + EPS)
    return centre * inv_std, inv_std


def position():
    tm, dp = lax.axis_index("tm"), lax.axis_index("dp")
    return dp & 3, (tm >> 1) & 3, dp >> 2, tm & 1


def shape(dims, kind):
    return jax.ShapeDtypeStruct(dims, kind)


def call(kernel, out_shape, in_specs, scratch, mib, name, flops=0, moved=0):
    return pl.pallas_call(
        kernel,
        out_shape=out_shape,
        in_specs=in_specs,
        out_specs=jax.tree.map(lambda _: VMEM, out_shape),
        scratch_shapes=scratch,
        compiler_params=pltpu.CompilerParams(vmem_limit_bytes=mib << 20),
        cost_estimate=pl.CostEstimate(flops=flops, bytes_accessed=moved, transcendentals=0),
        name=name,
    )


def deal_kernel(x_ref, *outs):
    _, y, _, _ = position()
    for k in range(4):
        for a in range(2):
            for z in range(2):
                outs[k][2 * a + z] = x_ref[a, z, (y + k) & 3]


def deal(tokens):
    return call(
        deal_kernel,
        (shape((4, 8, D), bf16),) * 4,
        [VMEM],
        [],
        4,
        "deal",
        moved=600_000,
    )(tokens.reshape(2, 2, 4, 8, D))


def pack_kernel(lens_ref, teacher_ref, ln_ref, og_ref, rh_ref, small):
    small[...] = jnp.zeros_like(small)
    small[0:REWARDS] = rh_ref[...]
    small[8] = og_ref[...]
    small[9] = ln_ref[...]
    small[10:11, 0:CLIPS] = lens_ref[...].astype(f32)
    for c in range(CLIPS):
        small[16 : 16 + REWARDS, c : c + 1] = upright(teacher_ref[c : c + 1])


def upright(row):
    return jnp.sum(jnp.where(eye(), row, 0.0), axis=1, keepdims=True)


def eye():
    side = (REWARDS, REWARDS)
    return lax.broadcasted_iota(jnp.int32, side, 0) == lax.broadcasted_iota(jnp.int32, side, 1)


def pack(clip_frames, teacher, ln_gain, out_gain, reward):
    return call(
        pack_kernel, shape((24, D), f32), [VMEM] * 5, [], 2, "pack", moved=200_000
    )(clip_frames, teacher, ln_gain, out_gain, reward)


def split_kernel(*refs):
    tm = lax.axis_index("tm")
    for kz in range(2):
        for kc in range(2):
            z, core = (tm >> 3) ^ kz, (tm & 1) ^ kc
            for k in range(4):
                rows = [refs[k][2 * a + z].astype(f32) for a in range(2)]
                low = jnp.concatenate([r[0:4] for r in rows], axis=0)
                high = jnp.concatenate([r[4:8] for r in rows], axis=0)
                refs[4 + 2 * kz + kc][k] = jnp.where(core == 0, low, high).astype(bf16)


def split(parts):
    return call(
        split_kernel,
        (shape((4, 8, D), bf16),) * 4,
        [VMEM] * 4,
        [],
        4,
        "split",
        moved=600_000,
    )(*parts)


def load_kernel(wq_any, wo_any, *refs):
    copies = [pltpu.make_async_copy(wo_any, refs[3], refs[4].at[3])]
    for k in range(3):
        cols = pl.ds(D * k, D)
        copies.append(pltpu.make_async_copy(wq_any.at[:, cols], refs[k], refs[4].at[k]))
    for copy in copies:
        copy.start()
    for copy in copies:
        copy.wait()


def load(w_qkv, w_out):
    return call(
        load_kernel,
        (shape((D, D), bf16),) * 4,
        [ANY, ANY],
        [pltpu.SemaphoreType.DMA((4,))],
        40,
        "load",
        moved=21_000_000,
    )(w_qkv, w_out)


def forward_kernel(
    x0, x1, x2, x3, wq_ref, wk_ref, wv_ref, wo_ref, small,
    normed_ref, attended_ref, proj_ref, p_ref, cen_ref, inv_ref, tot_ref,
    acc, xs,
):
    tm = lax.axis_index("tm")
    for t, part in enumerate((x0, x1, x2, x3)):
        for k in range(4):
            y = ((tm >> 1) - k) & 3
            xs[((tm & 9) ^ (8 * (t >> 1) + (t & 1))) | (2 * y)] = part[k].astype(f32)
    x = xs[...].reshape(TOK, D)
    norm, _ = standard(x)
    normed = (norm * small[9:10, :]).astype(bf16)
    normed_ref[...] = normed
    for i, w_ref in enumerate((wq_ref, wk_ref, wv_ref)):
        for j in range(0, D, CHUNK):
            part = dot(normed, w_ref[:, j : j + CHUNK], 1, 0)
            proj_ref[:, i * D + j : i * D + j + CHUNK] = part.astype(bf16)
    row = lax.broadcasted_iota(jnp.int32, (TOK, TOK), 0)
    col = lax.broadcasted_iota(jnp.int32, (TOK, TOK), 1)
    lag = (col >> 2) - (row >> 2)
    allowed = (
        ((row & 3) == (col & 3))
        & (lag >= -(WINDOW // 2))
        & (lag < WINDOW - WINDOW // 2)
        & (clip_of(small, frames((TOK, TOK), 0)) == clip_of(small, frames((TOK, TOK), 1)))
    )
    acc[...] = jnp.zeros_like(acc)
    for h in range(HEADS):
        a, b = span(h)
        mask = lane_mask(h)
        p_ref[h] = dot(proj_ref[:, a:b] * mask, proj_ref[:, D + a : D + b], 1, 1) * SCALE
    for h in range(0, HEADS, GROUP):
        masked = jnp.where(allowed[None], p_ref[h : h + GROUP], -1e30)
        terms = jnp.exp(masked - jnp.max(masked, axis=2, keepdims=True))
        weights = terms / jnp.sum(terms, axis=2, keepdims=True)
        p_ref[h : h + GROUP] = weights
    for h in range(HEADS):
        a, b = span(h)
        acc[:, a:b] += dot(
            p_ref[h].astype(bf16), proj_ref[:, 2 * D + a : 2 * D + b] * lane_mask(h), 1, 0
        )
    attended = acc[...].astype(bf16)
    attended_ref[...] = attended
    mixed = xs[...].reshape(TOK, D) + dot(attended, wo_ref[...], 1, 0)
    centred, inv_std = standard(mixed)
    cen_ref[...] = centred
    inv_ref[...] = jnp.broadcast_to(inv_std, (TOK, 128))
    final = centred * small[8:9, :]
    clip = clip_of(small, frames((TOK, 1), 0))
    tot_ref[...] = jnp.zeros_like(tot_ref)
    for c in range(CLIPS):
        sums = jnp.sum(jnp.where(clip == c, final, 0.0), axis=0, keepdims=True)
        tot_ref[:, c : c + 1] = jnp.sum(small[0:REWARDS, :] * sums, axis=1, keepdims=True)


def forward(x, weights, small):
    return call(
        forward_kernel,
        (
            shape((TOK, D), bf16),
            shape((TOK, D), bf16),
            shape((TOK, 3 * D), bf16),
            shape((HEADS, TOK, TOK), f32),
            shape((TOK, D), f32),
            shape((TOK, 128), f32),
            shape((REWARDS, 8), f32),
        ),
        [VMEM] * 9,
        [pltpu.VMEM((TOK, D), f32), pltpu.VMEM((16, 8, D), f32)],
        24,
        "forward",
        flops=2_000_000_000,
        moved=14_000_000,
    )(*x, *weights, small)


def place_rows(src, dst, where, x_first):
    x, y, z, _ = where
    for k in range(64):
        first, second, kz = k // 16, k // 4 % 4, k % 4
        kx, ky = (first, second) if x_first else (second, first)
        dp = ((z + kz) & 3) * 4 + ((x + kx) & 3)
        start = dp * 72 + ((y + ky) & 3) * PIECE
        dst[PIECE * k : PIECE * (k + 1), :] = src[pl.ds(start, PIECE), :]


def turn_kernel(normed_ref, attended_ref, keep_ref, send_ref, turned, placed):
    where = position()
    core = where[3]
    turned[0] = normed_ref[...].astype(f32).T
    turned[1] = attended_ref[...].astype(f32).T
    place_rows(turned.at[0], placed, where, True)
    keep_ref[0] = placed[...].astype(bf16)
    send_ref[0] = keep_ref[0]
    place_rows(turned.at[core], placed, where, False)
    keep_ref[1] = placed[...].astype(bf16)
    place_rows(turned.at[1 - core], placed, where, False)
    send_ref[1] = placed[...].astype(bf16)


def turn(normed, attended):
    return call(
        turn_kernel,
        (shape((2, D, TOK), bf16), shape((2, D, TOK), bf16)),
        [VMEM] * 2,
        [pltpu.VMEM((2, D, TOK), f32), pltpu.VMEM((D, TOK), f32)],
        8,
        "turn",
        moved=4_000_000,
    )(normed, attended)


def backward_kernel(
    t0, t1, t2, t3, small, proj_ref, p_ref, cen_ref, inv_ref, wo_ref,
    scores_ref, keep_ref, send_ref,
    dq, dk, dv, wg, da_ref,
):
    clip_col = lax.broadcasted_iota(jnp.int32, (REWARDS, 8), 1)
    count = jnp.ones((REWARDS, 8), f32)
    for c in range(CLIPS):
        count = jnp.where(clip_col == c, small[10:11, c : c + 1] * 64.0, count)
    scores = ((t0[...] + t2[...]) + (t1[...] + t3[...])) / count
    scores = scores[:, 0:CLIPS]
    for c in range(CLIPS):
        column = jnp.where(eye(), scores[:, c : c + 1], 0.0)
        scores_ref[c : c + 1, :] = jnp.sum(column, axis=0, keepdims=True)
    residue = (scores - small[16:24, 0:CLIPS]) / ROWS
    clip = clip_of(small, frames((TOK, 1), 0))
    scaled = jnp.zeros((TOK, D), f32)
    for c in range(CLIPS):
        row = jnp.sum(small[0:REWARDS, :] * residue[:, c : c + 1], axis=0, keepdims=True)
        scaled = jnp.where(clip == c, row * small[8:9, :], scaled)
    centred = cen_ref[...]
    mixed_grad = (
        scaled
        - jnp.mean(scaled, axis=-1, keepdims=True)
        - centred * jnp.mean(scaled * centred, axis=-1, keepdims=True)
    ) * inv_ref[:, 0:1]
    mixed_grad = mixed_grad.astype(bf16)
    da_ref[...] = dot(mixed_grad, wo_ref[...], 1, 1).astype(bf16)
    dq[...] = jnp.zeros_like(dq)
    dk[...] = jnp.zeros_like(dk)
    dv[...] = jnp.zeros_like(dv)
    for h in range(HEADS):
        a, b = span(h)
        mask = lane_mask(h)
        wg[h] = dot(da_ref[:, a:b] * mask, proj_ref[:, 2 * D + a : 2 * D + b], 1, 1)
    for h in range(0, HEADS, GROUP):
        weights = p_ref[h : h + GROUP]
        weight_grad = wg[h : h + GROUP]
        inner = jnp.sum(weights * weight_grad, axis=2, keepdims=True)
        wg[h : h + GROUP] = weights * (weight_grad - inner)
    for h in range(HEADS):
        a, b = span(h)
        mask = lane_mask(h)
        logit_grad = wg[h].astype(bf16)
        dq[:, a:b] += dot(logit_grad, proj_ref[:, D + a : D + b] * mask, 1, 0)
        dk[:, a:b] += dot(logit_grad, proj_ref[:, a:b] * mask, 0, 0)
        dv[:, a:b] += dot(p_ref[h].astype(bf16), da_ref[:, a:b] * mask, 0, 0)

    def store(ref_qk, ref_vo):
        ref_qk[0] = (dq[...] * SCALE).astype(bf16)
        ref_qk[1] = (dk[...] * SCALE).astype(bf16)
        ref_vo[0] = dv[...].astype(bf16)
        ref_vo[1] = mixed_grad

    core = position()[3]

    @pl.when(core == 0)
    def _():
        store(keep_ref, send_ref)

    @pl.when(core != 0)
    def _():
        store(send_ref, keep_ref)


def backward(totals, small, proj, p, centred, inv, w_out):
    return call(
        backward_kernel,
        (
            shape((CLIPS, REWARDS), f32),
            shape((2, TOK, D), bf16),
            shape((2, TOK, D), bf16),
        ),
        [VMEM] * 10,
        [pltpu.VMEM((TOK, D), f32)] * 3
        + [
            pltpu.VMEM((HEADS, TOK, TOK), f32),
            pltpu.VMEM((TOK, D), bf16),
        ],
        16,
        "backward",
        flops=1_500_000_000,
        moved=8_000_000,
    )(*totals, small, proj, p, centred, inv, w_out)


PARTS = ((2, 0), (2, 1), (1, 1), (3, 0), (1, 0), (3, 1))


def gradient_kernel(lk, lr, rk, rr, *outs):
    for i in range(2):
        right = jnp.concatenate([rk[i], rr[i]], axis=0)
        for k in (2, 1, 3, 0):
            rows = slice(288 * k, 288 * (k + 1))
            left = jnp.concatenate([lk[i, rows], lr[i, rows]], axis=1)
            part = dot(left, right, 1, 0).astype(bf16)
            if k == 0:
                outs[7 * i + 6][...] = part
            else:
                for j, (distance, piece) in enumerate(PARTS):
                    if distance == k:
                        outs[7 * i + j][...] = part[144 * piece : 144 * (piece + 1)]


def gradient(left_keep, left_recv, right_keep, right_recv):
    parts = call(
        gradient_kernel,
        ((shape((144, D), bf16),) * 6 + (shape((288, D), bf16),)) * 2,
        [VMEM] * 4,
        [],
        16,
        "gradient",
        flops=1_400_000_000,
        moved=8_000_000,
    )(left_keep, left_recv, right_keep, right_recv)
    return parts[:7], parts[7:]


def relay_kernel(*refs):
    for k in range(4):
        refs[8 + k][...] = (refs[k][...].astype(f32) + refs[4 + k][...].astype(f32)).astype(bf16)


def relay(arrived, own):
    return call(
        relay_kernel,
        (shape((144, D), bf16),) * 4,
        [VMEM] * 8,
        [],
        8,
        "relay",
        moved=4_000_000,
    )(*arrived, *own)


def total(refs):
    result = refs[0][...].astype(f32)
    for ref in refs[1:]:
        result += ref[...].astype(f32)
    return result


SLOT = ((0, 3, 6, 5), (1, 2, 7, 4))


def first_sum_kernel(*refs):
    for i in range(2):
        plain_on, plain_back, relayed_on, relayed_back, own = (refs[2 * j + i] for j in range(5))
        result = own[...].astype(f32) + jnp.concatenate(
            [
                plain_back[...].astype(f32) + relayed_on[...].astype(f32),
                plain_on[...].astype(f32) + relayed_back[...].astype(f32),
            ],
            axis=0,
        )
        for k in range(4):
            refs[10 + SLOT[1 - i][k]][...] = result[72 * k : 72 * (k + 1)].astype(bf16)


def first_sum(parts):
    return call(
        first_sum_kernel,
        (shape((72, D), bf16),) * 8,
        [VMEM] * 10,
        [],
        12,
        "first_sum",
        moved=6_000_000,
    )(*parts)


def second_sum_kernel(*refs):
    sums = [total([refs[SLOT[i][k]] for k in range(4)]) for i in (1, 0)]
    rest = jnp.zeros((4, D), f32)
    for k in range(4):
        rows = slice(PIECE * k, PIECE * (k + 1))
        refs[8 + k][...] = jnp.concatenate([sums[0][rows], sums[1][rows], rest], axis=0).astype(
            bf16
        )


def second_sum(parts):
    return call(
        second_sum_kernel,
        (shape((40, D), bf16),) * 4,
        [VMEM] * 8,
        [],
        6,
        "second_sum",
        moved=1_700_000,
    )(*parts)


def sum_kernel(*refs):
    refs[-1][...] = total(refs[:-1]).astype(bf16)


def pair_sum_kernel(a, b, c, d, out):
    out[...] = (a[...] + b[...]) + (c[...] + d[...])


def pair_sum(*parts):
    return call(
        pair_sum_kernel, shape((REWARDS, 8), f32), [VMEM] * 4, [], 1, "pair_sum", moved=20_000
    )(*parts)


def plain_sum(parts):
    return call(
        sum_kernel,
        shape(parts[0].shape, bf16),
        [VMEM] * len(parts),
        [],
        3,
        "plain_sum",
        moved=500_000,
    )(*parts)


def stack_kernel(*refs):
    for k in range(4):
        refs[4][k] = refs[k][...]


def stack(parts):
    return call(
        stack_kernel, shape((4, 40, D), bf16), [VMEM] * 4, [], 3, "stack", moved=800_000
    )(*parts)


def last_kernel(mine, other, qkv_ref, out_ref, held):
    _, y_here, _, core = position()
    for k in range(4):
        y = (y_here - k) & 3
        held[core, y] = mine[k].astype(f32)
        held[1 - core, y] = other[k].astype(f32)
    for y in range(4):
        rows = slice(PIECE * y, PIECE * (y + 1))
        qkv_ref[rows, 0:D] = held[0, y, 0:PIECE]
        qkv_ref[rows, D : 2 * D] = held[0, y, PIECE : 2 * PIECE]
        qkv_ref[rows, 2 * D : 3 * D] = held[1, y, 0:PIECE]
        out_ref[rows, :] = held[1, y, PIECE : 2 * PIECE]


def last(mine, other):
    return call(
        last_kernel,
        (shape((72, 3 * D), f32), shape((72, D), f32)),
        [VMEM] * 2,
        [pltpu.VMEM((2, 4, 40, D), f32)],
        10,
        "last",
        moved=2_000_000,
    )(mine, other)


def to_core(block):
    return lax.ppermute(block, "tm", [(i, i ^ 1) for i in range(16)])


def to_far(block, core=0):
    return lax.ppermute(block, "tm", [(i, i ^ 8 ^ core) for i in range(16)])


def along_y(block, k):
    return lax.ppermute(block, "tm", [(i, i & 9 | (i + 2 * k) & 6) for i in range(16)])


def along_x(block, k):
    return lax.ppermute(block, "dp", [(i, i & 12 | (i + k) & 3) for i in range(16)])


def around_z(block, k):
    route = []
    for tm in range(16):
        for dp in range(16):
            step = {1: 1, 3: -1, 2: -2 if tm & 1 else 2}[k]
            z = ((tm >> 3) * 4 + (dp >> 2) + step) & 7
            there = (tm & 7 | (z >> 2) << 3) * 16 + ((z & 3) << 2 | dp & 3)
            route.append((tm * 16 + dp, there))
    return lax.ppermute(block, ("tm", "dp"), route)


def exchange(slots):
    moved = list(slots)
    for k in (1, 3, 2):
        moved[SLOT[1][k]] = along_y(slots[SLOT[1][k]], k)
        moved[SLOT[0][k]] = along_x(slots[SLOT[0][k]], k)
    return moved


def around(x_half, y_half):
    on, back = (along_x, along_y), 3
    halves = (x_half, y_half)
    arrived = [on[i](halves[i][j], 1 if j == 0 else back) for j in range(2) for i in range(2)]
    plain = [on[i](halves[i][2 + j], 1 if j == 0 else back) for j in range(2) for i in range(2)]
    own = [halves[i][4 + j] for j in range(2) for i in range(2)]
    sums = relay(arrived, own)
    relayed = [on[i](sums[2 * j + i], 1 if j == 0 else back) for j in range(2) for i in range(2)]
    return first_sum(plain + relayed + [x_half[6], y_half[6]])


def on_device(tokens, clip_frames, teacher_scores, ln_gain, w_qkv, w_out, out_gain, reward_head):
    parts = deal(tokens[0])
    small = pack(clip_frames, teacher_scores[0], ln_gain, out_gain, reward_head.T)
    weights = load(w_qkv, w_out)
    parts = split([parts[0]] + [along_y(parts[k], k) for k in (1, 2, 3)])
    x = [parts[0], to_core(parts[1]), to_far(parts[2]), to_far(parts[3], 1)]
    normed, attended, proj, p, centred, inv, partial = forward(x, weights, small)
    near, far, both = to_core(partial), to_far(partial), to_far(partial, 1)
    partial = pair_sum(partial, near, far, both)
    totals = [partial] + [along_y(partial, k) for k in (1, 2, 3)]
    left_keep, left_send = turn(normed, attended)
    left_recv = to_core(left_send)
    scores, right_keep, right_send = backward(totals, small, proj, p, centred, inv, weights[3])
    parts = gradient(left_keep, left_recv, right_keep, to_core(right_send))
    parts = second_sum(exchange(around(*parts)))
    part = plain_sum([parts[0]] + [around_z(parts[k], k) for k in (1, 2, 3)])
    part = plain_sum([part, to_far(part)])
    mine = stack([part] + [along_y(part, k) for k in (1, 2, 3)])
    qkv_total, out_total = last(mine, to_core(mine))
    return (scores[None], qkv_total, out_total)


def solution(mesh):
    return jax.shard_map(
        on_device,
        mesh=mesh,
        in_specs=(
            P("dp", "tm", None, None),
            P("dp", None),
            P("dp", None, None),
            P(),
            P(),
            P(),
            P(),
            P(),
        ),
        out_specs=(P("dp", None, None), P("dp", None), P("dp", None)),
        check_vma=False,
    )
```

```python
import math

import jax
import jax.numpy as jnp
from jax import lax
from jax.experimental import pallas as pl
from jax.experimental.pallas import tpu as pltpu
from jax.sharding import PartitionSpec as P

HEADS = 16
HEAD_DIM = 72
WINDOW = 8
D = 1152
TOK = 128
CLIPS = 4
REWARDS = 8
ROWS = 16
CHUNK = 384
PIECE = 18
GROUP = 4
EPS = 1e-06
SCALE = 1.0 / math.sqrt(HEAD_DIM)

f32 = jnp.float32
bf16 = jnp.bfloat16
HI = lax.Precision.HIGHEST
VMEM = pl.BlockSpec(memory_space=pltpu.VMEM)
ANY = pl.BlockSpec(memory_space=pl.ANY)


def dot(a, b, ca, cb, precision=None):
    return lax.dot_general(
        a, b, (((ca,), (cb,)), ((), ())), preferred_element_type=f32, precision=precision
    )


def clip_of(small, frame):
    end, clip = small[10:11, 0:1], jnp.zeros_like(frame)
    for c in range(CLIPS):
        clip += (frame >= end).astype(f32)
        if c + 1 < CLIPS:
            end = end + small[10:11, c + 1 : c + 2]
    return clip


def frames(dims, axis):
    return (lax.broadcasted_iota(jnp.int32, dims, axis) >> 2).astype(f32)


def span(h):
    low = HEAD_DIM * h
    return low // 128 * 128, -(-(low + HEAD_DIM) // 128) * 128


def lane_mask(h):
    start, end = span(h)
    lane = lax.broadcasted_iota(jnp.int32, (1, end - start), 1) + (start - HEAD_DIM * h)
    return ((lane >= 0) & (lane < HEAD_DIM)).astype(f32).astype(bf16)


def standard(values):
    centre = values - jnp.mean(values, axis=-1, keepdims=True)
    inv_std = lax.rsqrt(jnp.mean(centre * centre, axis=-1, keepdims=True) + EPS)
    return centre * inv_std, inv_std


def position():
    tm, dp = lax.axis_index("tm"), lax.axis_index("dp")
    return dp & 3, (tm >> 1) & 3, dp >> 2, tm & 1


def shape(dims, kind):
    return jax.ShapeDtypeStruct(dims, kind)


def call(kernel, out_shape, in_specs, scratch, mib, name, flops=0, moved=0):
    return pl.pallas_call(
        kernel,
        out_shape=out_shape,
        in_specs=in_specs,
        out_specs=jax.tree.map(lambda _: VMEM, out_shape),
        scratch_shapes=scratch,
        compiler_params=pltpu.CompilerParams(vmem_limit_bytes=mib << 20),
        cost_estimate=pl.CostEstimate(flops=flops, bytes_accessed=moved, transcendentals=0),
        name=name,
    )


def halves_kernel(x_ref, keep_ref, send_ref):
    z = lax.axis_index("tm") >> 3
    for a in range(2):
        keep_ref[a] = x_ref[a, z]
        send_ref[a] = x_ref[a, 1 - z]


def halves(tokens):
    return call(
        halves_kernel,
        (shape((2, 4, 8, D), bf16),) * 2,
        [VMEM],
        [],
        4,
        "halves",
        moved=600_000,
    )(tokens.reshape(2, 2, 4, 8, D))


def deal_kernel(keep_ref, far_ref, small, loaded, *outs):
    _, y, _, _ = position()
    for k in range(4):
        for a in range(2):
            outs[k][a] = keep_ref[a, (y + k) & 3]
            outs[k][2 + a] = far_ref[a, (y + k) & 3]


def deal(keep, far, small, loaded):
    return call(
        deal_kernel,
        (shape((4, 8, D), bf16),) * 4,
        [VMEM] * 4,
        [],
        4,
        "deal",
        moved=600_000,
    )(keep, far, small, loaded)


def pack_kernel(lens_ref, teacher_ref, ln_ref, og_ref, rh_ref, small):
    small[...] = jnp.zeros_like(small)
    small[0:REWARDS] = rh_ref[...]
    small[8] = og_ref[...]
    small[9] = ln_ref[...]
    small[10:11, 0:CLIPS] = lens_ref[...].astype(f32)
    for c in range(CLIPS):
        small[16 : 16 + REWARDS, c : c + 1] = upright(teacher_ref[c : c + 1])


def upright(row):
    return jnp.sum(jnp.where(eye(), row, 0.0), axis=1, keepdims=True)


def eye():
    side = (REWARDS, REWARDS)
    return lax.broadcasted_iota(jnp.int32, side, 0) == lax.broadcasted_iota(jnp.int32, side, 1)


def pack(clip_frames, teacher, ln_gain, out_gain, reward):
    return call(
        pack_kernel, shape((24, D), f32), [VMEM] * 5, [], 2, "pack", moved=200_000
    )(clip_frames, teacher, ln_gain, out_gain, reward)


def split_kernel(*refs):
    core = position()[3]
    for k in range(4):
        for z in range(2):
            rows = [refs[k][2 * z + a].astype(f32) for a in range(2)]
            low = jnp.concatenate([r[0:4] for r in rows], axis=0)
            high = jnp.concatenate([r[4:8] for r in rows], axis=0)
            refs[4][2 * k + z] = jnp.where(core == 0, low, high).astype(bf16)
            refs[5][2 * k + z] = jnp.where(core == 0, high, low).astype(bf16)


def split(parts):
    return call(
        split_kernel,
        (shape((8, 8, D), bf16),) * 2,
        [VMEM] * 4,
        [],
        4,
        "split",
        moved=600_000,
    )(*parts)


def load_kernel(wq_any, wo_any, after, *refs):
    copies = [pltpu.make_async_copy(wo_any, refs[3], refs[5].at[3])]
    for k in range(3):
        cols = pl.ds(D * k, D)
        copies.append(pltpu.make_async_copy(wq_any.at[:, cols], refs[k], refs[5].at[k]))
    for copy in copies:
        copy.start()
    refs[4][...] = jnp.zeros_like(refs[4])
    for copy in copies:
        copy.wait()


def load(w_qkv, w_out, after):
    return call(
        load_kernel,
        (shape((D, D), bf16),) * 4 + (shape((8, 128), f32),),
        [ANY, ANY, ANY],
        [pltpu.SemaphoreType.DMA((4,))],
        40,
        "load",
        moved=21_000_000,
    )(w_qkv, w_out, after)


def forward_kernel(
    x0, x1, wq_ref, wk_ref, wv_ref, wo_ref, small,
    normed_ref, attended_ref, proj_ref, p_ref, cen_ref, inv_ref, tot_ref,
    acc, xs,
):
    tm = lax.axis_index("tm")
    for core, part in enumerate((x0, x1)):
        for k in range(4):
            y = ((tm >> 1) - k) & 3
            for z in range(2):
                xs[((tm & 9) ^ (8 * z + core)) | (2 * y)] = part[2 * k + z].astype(f32)
    x = xs[...].reshape(TOK, D)
    norm, _ = standard(x)
    normed = (norm * small[9:10, :]).astype(bf16)
    normed_ref[...] = normed
    for i, w_ref in enumerate((wq_ref, wk_ref, wv_ref)):
        for j in range(0, D, CHUNK):
            part = dot(normed, w_ref[:, j : j + CHUNK], 1, 0)
            proj_ref[:, i * D + j : i * D + j + CHUNK] = part.astype(bf16)
    row = lax.broadcasted_iota(jnp.int32, (TOK, TOK), 0)
    col = lax.broadcasted_iota(jnp.int32, (TOK, TOK), 1)
    lag = (col >> 2) - (row >> 2)
    allowed = (
        ((row & 3) == (col & 3))
        & (lag >= -(WINDOW // 2))
        & (lag < WINDOW - WINDOW // 2)
        & (clip_of(small, frames((TOK, TOK), 0)) == clip_of(small, frames((TOK, TOK), 1)))
    )
    acc[...] = jnp.zeros_like(acc)
    for h in range(HEADS):
        a, b = span(h)
        mask = lane_mask(h)
        p_ref[h] = dot(proj_ref[:, a:b] * mask, proj_ref[:, D + a : D + b], 1, 1) * SCALE
    for h in range(0, HEADS, GROUP):
        masked = jnp.where(allowed[None], p_ref[h : h + GROUP], -1e30)
        terms = jnp.exp(masked - jnp.max(masked, axis=2, keepdims=True))
        weights = terms / jnp.sum(terms, axis=2, keepdims=True)
        p_ref[h : h + GROUP] = weights
    for h in range(HEADS):
        a, b = span(h)
        acc[:, a:b] += dot(
            p_ref[h].astype(bf16), proj_ref[:, 2 * D + a : 2 * D + b] * lane_mask(h), 1, 0
        )
    attended = acc[...].astype(bf16)
    attended_ref[...] = attended
    mixed = xs[...].reshape(TOK, D) + dot(attended, wo_ref[...], 1, 0)
    centred, inv_std = standard(mixed)
    cen_ref[...] = centred
    inv_ref[...] = jnp.broadcast_to(inv_std, (TOK, 128))
    final = centred * small[8:9, :]
    clip = clip_of(small, frames((TOK, 1), 0))
    tot_ref[...] = jnp.zeros_like(tot_ref)
    for c in range(CLIPS):
        sums = jnp.sum(jnp.where(clip == c, final, 0.0), axis=0, keepdims=True)
        tot_ref[:, c : c + 1] = jnp.sum(small[0:REWARDS, :] * sums, axis=1, keepdims=True)


def forward(x, weights, small):
    return call(
        forward_kernel,
        (
            shape((TOK, D), bf16),
            shape((TOK, D), bf16),
            shape((TOK, 3 * D), bf16),
            shape((HEADS, TOK, TOK), f32),
            shape((TOK, D), f32),
            shape((TOK, 128), f32),
            shape((REWARDS, 8), f32),
        ),
        [VMEM] * 7,
        [pltpu.VMEM((TOK, D), f32), pltpu.VMEM((16, 8, D), f32)],
        24,
        "forward",
        flops=2_000_000_000,
        moved=14_000_000,
    )(*x, *weights, small)


def place_rows(src, dst, where, x_first):
    x, y, z, _ = where
    for k in range(64):
        first, second, kz = k // 16, k // 4 % 4, k % 4
        kx, ky = (first, second) if x_first else (second, first)
        dp = ((z + kz) & 3) * 4 + ((x + kx) & 3)
        start = dp * 72 + ((y + ky) & 3) * PIECE
        dst[PIECE * k : PIECE * (k + 1), :] = src[pl.ds(start, PIECE), :]


def turn_kernel(normed_ref, attended_ref, keep_ref, send_ref, turned, placed):
    where = position()
    core = where[3]
    turned[0] = normed_ref[...].astype(f32).T
    turned[1] = attended_ref[...].astype(f32).T
    place_rows(turned.at[0], placed, where, True)
    keep_ref[0] = placed[...].astype(bf16)
    send_ref[0] = keep_ref[0]
    place_rows(turned.at[core], placed, where, False)
    keep_ref[1] = placed[...].astype(bf16)
    place_rows(turned.at[1 - core], placed, where, False)
    send_ref[1] = placed[...].astype(bf16)


def turn(normed, attended):
    return call(
        turn_kernel,
        (shape((2, D, TOK), bf16), shape((2, D, TOK), bf16)),
        [VMEM] * 2,
        [pltpu.VMEM((2, D, TOK), f32), pltpu.VMEM((D, TOK), f32)],
        8,
        "turn",
        moved=4_000_000,
    )(normed, attended)


def backward_kernel(
    t0, t1, t2, t3, small, proj_ref, p_ref, cen_ref, inv_ref, wo_ref,
    scores_ref, keep_ref, send_ref,
    dq, dk, dv, wg, da_ref,
):
    clip_col = lax.broadcasted_iota(jnp.int32, (REWARDS, 8), 1)
    count = jnp.ones((REWARDS, 8), f32)
    for c in range(CLIPS):
        count = jnp.where(clip_col == c, small[10:11, c : c + 1] * 64.0, count)
    scores = ((t0[...] + t2[...]) + (t1[...] + t3[...])) / count
    scores = scores[:, 0:CLIPS]
    for c in range(CLIPS):
        column = jnp.where(eye(), scores[:, c : c + 1], 0.0)
        scores_ref[c : c + 1, :] = jnp.sum(column, axis=0, keepdims=True)
    residue = (scores - small[16:24, 0:CLIPS]) / ROWS
    clip = clip_of(small, frames((TOK, 1), 0))
    scaled = jnp.zeros((TOK, D), f32)
    for c in range(CLIPS):
        row = jnp.sum(small[0:REWARDS, :] * residue[:, c : c + 1], axis=0, keepdims=True)
        scaled = jnp.where(clip == c, row * small[8:9, :], scaled)
    centred = cen_ref[...]
    mixed_grad = (
        scaled
        - jnp.mean(scaled, axis=-1, keepdims=True)
        - centred * jnp.mean(scaled * centred, axis=-1, keepdims=True)
    ) * inv_ref[:, 0:1]
    mixed_grad = mixed_grad.astype(bf16)
    da_ref[...] = dot(mixed_grad, wo_ref[...], 1, 1).astype(bf16)
    dq[...] = jnp.zeros_like(dq)
    dk[...] = jnp.zeros_like(dk)
    dv[...] = jnp.zeros_like(dv)
    for h in range(HEADS):
        a, b = span(h)
        mask = lane_mask(h)
        wg[h] = dot(da_ref[:, a:b] * mask, proj_ref[:, 2 * D + a : 2 * D + b], 1, 1)
    for h in range(0, HEADS, GROUP):
        weights = p_ref[h : h + GROUP]
        weight_grad = wg[h : h + GROUP]
        inner = jnp.sum(weights * weight_grad, axis=2, keepdims=True)
        wg[h : h + GROUP] = weights * (weight_grad - inner)
    for h in range(HEADS):
        a, b = span(h)
        mask = lane_mask(h)
        logit_grad = wg[h].astype(bf16)
        dq[:, a:b] += dot(logit_grad, proj_ref[:, D + a : D + b] * mask, 1, 0)
        dk[:, a:b] += dot(logit_grad, proj_ref[:, a:b] * mask, 0, 0)
        dv[:, a:b] += dot(p_ref[h].astype(bf16), da_ref[:, a:b] * mask, 0, 0)

    def store(ref_qk, ref_vo):
        ref_qk[0] = (dq[...] * SCALE).astype(bf16)
        ref_qk[1] = (dk[...] * SCALE).astype(bf16)
        ref_vo[0] = dv[...].astype(bf16)
        ref_vo[1] = mixed_grad

    core = position()[3]

    @pl.when(core == 0)
    def _():
        store(keep_ref, send_ref)

    @pl.when(core != 0)
    def _():
        store(send_ref, keep_ref)


def backward(totals, small, proj, p, centred, inv, w_out):
    return call(
        backward_kernel,
        (
            shape((CLIPS, REWARDS), f32),
            shape((2, TOK, D), bf16),
            shape((2, TOK, D), bf16),
        ),
        [VMEM] * 10,
        [pltpu.VMEM((TOK, D), f32)] * 3
        + [
            pltpu.VMEM((HEADS, TOK, TOK), f32),
            pltpu.VMEM((TOK, D), bf16),
        ],
        16,
        "backward",
        flops=1_500_000_000,
        moved=8_000_000,
    )(*totals, small, proj, p, centred, inv, w_out)


PARTS = ((2, 0), (2, 1), (1, 1), (3, 0), (1, 0), (3, 1))


def gradient_kernel(lk, lr, rk, rr, *outs):
    for i in range(2):
        right = jnp.concatenate([rk[i], rr[i]], axis=0)
        for k in (2, 1, 3, 0):
            rows = slice(288 * k, 288 * (k + 1))
            left = jnp.concatenate([lk[i, rows], lr[i, rows]], axis=1)
            part = dot(left, right, 1, 0).astype(bf16)
            if k == 0:
                outs[7 * i + 6][...] = part
            else:
                for j, (distance, piece) in enumerate(PARTS):
                    if distance == k:
                        outs[7 * i + j][...] = part[144 * piece : 144 * (piece + 1)]


def gradient(left_keep, left_recv, right_keep, right_recv):
    parts = call(
        gradient_kernel,
        ((shape((144, D), bf16),) * 6 + (shape((288, D), bf16),)) * 2,
        [VMEM] * 4,
        [],
        16,
        "gradient",
        flops=1_400_000_000,
        moved=8_000_000,
    )(left_keep, left_recv, right_keep, right_recv)
    return parts[:7], parts[7:]


def relay_kernel(*refs):
    for k in range(4):
        refs[8 + k][...] = (refs[k][...].astype(f32) + refs[4 + k][...].astype(f32)).astype(bf16)


def relay(arrived, own):
    return call(
        relay_kernel,
        (shape((144, D), bf16),) * 4,
        [VMEM] * 8,
        [],
        8,
        "relay",
        moved=4_000_000,
    )(*arrived, *own)


def total(refs):
    result = refs[0][...].astype(f32)
    for ref in refs[1:]:
        result += ref[...].astype(f32)
    return result


SLOT = ((0, 3, 6, 5), (1, 2, 7, 4))


def first_sum_kernel(*refs):
    for i in range(2):
        plain_on, plain_back, relayed_on, relayed_back, own = (refs[2 * j + i] for j in range(5))
        result = own[...].astype(f32) + jnp.concatenate(
            [
                plain_back[...].astype(f32) + relayed_on[...].astype(f32),
                plain_on[...].astype(f32) + relayed_back[...].astype(f32),
            ],
            axis=0,
        )
        for k in range(4):
            refs[10 + SLOT[1 - i][k]][...] = result[72 * k : 72 * (k + 1)].astype(bf16)


def first_sum(parts):
    return call(
        first_sum_kernel,
        (shape((72, D), bf16),) * 8,
        [VMEM] * 10,
        [],
        12,
        "first_sum",
        moved=6_000_000,
    )(*parts)


def second_sum_kernel(*refs):
    sums = [total([refs[SLOT[i][k]] for k in range(4)]) for i in (1, 0)]
    rest = jnp.zeros((4, D), f32)
    for k in range(4):
        rows = slice(PIECE * k, PIECE * (k + 1))
        refs[8 + k][...] = jnp.concatenate([sums[0][rows], sums[1][rows], rest], axis=0).astype(
            bf16
        )


def second_sum(parts):
    return call(
        second_sum_kernel,
        (shape((40, D), bf16),) * 4,
        [VMEM] * 8,
        [],
        6,
        "second_sum",
        moved=1_700_000,
    )(*parts)


def sum_kernel(*refs):
    refs[-1][...] = total(refs[:-1]).astype(bf16)


def pair_sum_kernel(a, b, out):
    out[...] = a[...] + b[...]


def pair_sum(*parts):
    return call(
        pair_sum_kernel, shape((REWARDS, 8), f32), [VMEM] * 2, [], 1, "pair_sum", moved=20_000
    )(*parts)


def plain_sum(parts):
    return call(
        sum_kernel,
        shape(parts[0].shape, bf16),
        [VMEM] * len(parts),
        [],
        3,
        "plain_sum",
        moved=500_000,
    )(*parts)


def stack_kernel(*refs):
    for k in range(4):
        refs[4][k] = refs[k][...]


def stack(parts):
    return call(
        stack_kernel, shape((4, 40, D), bf16), [VMEM] * 4, [], 3, "stack", moved=800_000
    )(*parts)


def last_kernel(mine, other, qkv_ref, out_ref, held):
    _, y_here, _, core = position()
    for k in range(4):
        y = (y_here - k) & 3
        held[core, y] = mine[k].astype(f32)
        held[1 - core, y] = other[k].astype(f32)
    for y in range(4):
        rows = slice(PIECE * y, PIECE * (y + 1))
        qkv_ref[rows, 0:D] = held[0, y, 0:PIECE]
        qkv_ref[rows, D : 2 * D] = held[0, y, PIECE : 2 * PIECE]
        qkv_ref[rows, 2 * D : 3 * D] = held[1, y, 0:PIECE]
        out_ref[rows, :] = held[1, y, PIECE : 2 * PIECE]


def last(mine, other):
    return call(
        last_kernel,
        (shape((72, 3 * D), f32), shape((72, D), f32)),
        [VMEM] * 2,
        [pltpu.VMEM((2, 4, 40, D), f32)],
        10,
        "last",
        moved=2_000_000,
    )(mine, other)


def to_core(block):
    return lax.ppermute(block, "tm", [(i, i ^ 1) for i in range(16)])


def to_far(block):
    return lax.ppermute(block, "tm", [(i, i ^ 8) for i in range(16)])


def along_y(block, k):
    return lax.ppermute(block, "tm", [(i, i & 9 | (i + 2 * k) & 6) for i in range(16)])


def along_x(block, k):
    return lax.ppermute(block, "dp", [(i, i & 12 | (i + k) & 3) for i in range(16)])


def around_z(block, k):
    route = []
    for tm in range(16):
        for dp in range(16):
            step = {1: 1, 3: -1, 2: -2 if tm & 1 else 2}[k]
            z = ((tm >> 3) * 4 + (dp >> 2) + step) & 7
            there = (tm & 7 | (z >> 2) << 3) * 16 + ((z & 3) << 2 | dp & 3)
            route.append((tm * 16 + dp, there))
    return lax.ppermute(block, ("tm", "dp"), route)


def exchange(slots):
    moved = list(slots)
    for k in (1, 3, 2):
        moved[SLOT[1][k]] = along_y(slots[SLOT[1][k]], k)
        moved[SLOT[0][k]] = along_x(slots[SLOT[0][k]], k)
    return moved


def around(x_half, y_half):
    on, back = (along_x, along_y), 3
    halves = (x_half, y_half)
    arrived = [on[i](halves[i][j], 1 if j == 0 else back) for j in range(2) for i in range(2)]
    plain = [on[i](halves[i][2 + j], 1 if j == 0 else back) for j in range(2) for i in range(2)]
    own = [halves[i][4 + j] for j in range(2) for i in range(2)]
    sums = relay(arrived, own)
    relayed = [on[i](sums[2 * j + i], 1 if j == 0 else back) for j in range(2) for i in range(2)]
    return first_sum(plain + relayed + [x_half[6], y_half[6]])


def on_device(tokens, clip_frames, teacher_scores, ln_gain, w_qkv, w_out, out_gain, reward_head):
    keep, send = halves(tokens[0])
    small = pack(clip_frames, teacher_scores[0], ln_gain, out_gain, reward_head.T)
    *weights, loaded = load(w_qkv, w_out, keep)
    parts = deal(keep, to_far(send), small, loaded)
    keep, send = split([parts[0]] + [along_y(parts[k], k) for k in (1, 2, 3)])
    x = [keep, to_core(send)]
    normed, attended, proj, p, centred, inv, partial = forward(x, weights, small)
    partial = pair_sum(partial, to_core(partial))
    partial = pair_sum(partial, to_far(partial))
    totals = [partial] + [along_y(partial, k) for k in (1, 2, 3)]
    left_keep, left_send = turn(normed, attended)
    left_recv = to_core(left_send)
    scores, right_keep, right_send = backward(totals, small, proj, p, centred, inv, weights[3])
    parts = gradient(left_keep, left_recv, right_keep, to_core(right_send))
    parts = second_sum(exchange(around(*parts)))
    part = plain_sum([parts[0]] + [around_z(parts[k], k) for k in (1, 2, 3)])
    part = plain_sum([part, to_far(part)])
    mine = stack([part] + [along_y(part, k) for k in (1, 2, 3)])
    qkv_total, out_total = last(mine, to_core(mine))
    return (scores[None], qkv_total, out_total)


def solution(mesh):
    return jax.shard_map(
        on_device,
        mesh=mesh,
        in_specs=(
            P("dp", "tm", None, None),
            P("dp", None),
            P("dp", None, None),
            P(),
            P(),
            P(),
            P(),
            P(),
        ),
        out_specs=(P("dp", None, None), P("dp", None), P("dp", None)),
        check_vma=False,
    )
```

```python
import math

import jax
import jax.numpy as jnp
from jax import lax
from jax.experimental import pallas as pl
from jax.experimental.pallas import tpu as pltpu
from jax.sharding import PartitionSpec as P

HEADS = 16
HEAD_DIM = 72
WINDOW = 8
D = 1152
TOK = 128
CLIPS = 4
REWARDS = 8
ROWS = 16
CHUNK = 384
PIECE = 18
GROUP = 4
EPS = 1e-06
SCALE = 1.0 / math.sqrt(HEAD_DIM)

f32 = jnp.float32
bf16 = jnp.bfloat16
HI = lax.Precision.HIGHEST
VMEM = pl.BlockSpec(memory_space=pltpu.VMEM)
ANY = pl.BlockSpec(memory_space=pl.ANY)


def dot(a, b, ca, cb, precision=None):
    return lax.dot_general(
        a, b, (((ca,), (cb,)), ((), ())), preferred_element_type=f32, precision=precision
    )


def clip_of(small, frame):
    end, clip = small[10:11, 0:1], jnp.zeros_like(frame)
    for c in range(CLIPS):
        clip += (frame >= end).astype(f32)
        if c + 1 < CLIPS:
            end = end + small[10:11, c + 1 : c + 2]
    return clip


def frames(dims, axis):
    return (lax.broadcasted_iota(jnp.int32, dims, axis) >> 2).astype(f32)


def span(h):
    low = HEAD_DIM * h
    return low // 128 * 128, -(-(low + HEAD_DIM) // 128) * 128


def lane_mask(h):
    start, end = span(h)
    lane = lax.broadcasted_iota(jnp.int32, (1, end - start), 1) + (start - HEAD_DIM * h)
    return ((lane >= 0) & (lane < HEAD_DIM)).astype(f32).astype(bf16)


def standard(values):
    centre = values - jnp.mean(values, axis=-1, keepdims=True)
    inv_std = lax.rsqrt(jnp.mean(centre * centre, axis=-1, keepdims=True) + EPS)
    return centre * inv_std, inv_std


def position():
    tm, dp = lax.axis_index("tm"), lax.axis_index("dp")
    return dp & 3, (tm >> 1) & 3, dp >> 2, tm & 1


def shape(dims, kind):
    return jax.ShapeDtypeStruct(dims, kind)


def call(kernel, out_shape, in_specs, scratch, mib, name, flops=0, moved=0):
    return pl.pallas_call(
        kernel,
        out_shape=out_shape,
        in_specs=in_specs,
        out_specs=jax.tree.map(lambda _: VMEM, out_shape),
        scratch_shapes=scratch,
        compiler_params=pltpu.CompilerParams(vmem_limit_bytes=mib << 20),
        cost_estimate=pl.CostEstimate(flops=flops, bytes_accessed=moved, transcendentals=0),
        name=name,
    )


def halves_kernel(x_ref, keep_ref, send_ref):
    z = lax.axis_index("tm") >> 3
    for a in range(2):
        keep_ref[a] = x_ref[a, z]
        send_ref[a] = x_ref[a, 1 - z]


def halves(tokens):
    return call(
        halves_kernel,
        (shape((2, 4, 8, D), bf16),) * 2,
        [VMEM],
        [],
        4,
        "halves",
        moved=600_000,
    )(tokens.reshape(2, 2, 4, 8, D))


def deal_kernel(keep_ref, far_ref, small, loaded, *outs):
    _, y, _, _ = position()
    for k in range(4):
        for a in range(2):
            outs[k][a] = keep_ref[a, (y + k) & 3]
            outs[k][2 + a] = far_ref[a, (y + k) & 3]


def deal(keep, far, small, loaded):
    return call(
        deal_kernel,
        (shape((4, 8, D), bf16),) * 4,
        [VMEM] * 4,
        [],
        4,
        "deal",
        moved=600_000,
    )(keep, far, small, loaded)


def pack_kernel(lens_ref, teacher_ref, ln_ref, og_ref, rh_ref, small):
    small[...] = jnp.zeros_like(small)
    small[0:REWARDS] = rh_ref[...]
    small[8] = og_ref[...]
    small[9] = ln_ref[...]
    small[10:11, 0:CLIPS] = lens_ref[...].astype(f32)
    for c in range(CLIPS):
        small[16 : 16 + REWARDS, c : c + 1] = upright(teacher_ref[c : c + 1])


def upright(row):
    return jnp.sum(jnp.where(eye(), row, 0.0), axis=1, keepdims=True)


def eye():
    side = (REWARDS, REWARDS)
    return lax.broadcasted_iota(jnp.int32, side, 0) == lax.broadcasted_iota(jnp.int32, side, 1)


def pack(clip_frames, teacher, ln_gain, out_gain, reward):
    return call(
        pack_kernel, shape((24, D), f32), [VMEM] * 5, [], 2, "pack", moved=200_000
    )(clip_frames, teacher, ln_gain, out_gain, reward)


def split_kernel(loaded, *refs):
    core = position()[3]
    for k in range(4):
        for z in range(2):
            rows = [refs[k][2 * z + a].astype(f32) for a in range(2)]
            low = jnp.concatenate([r[0:4] for r in rows], axis=0)
            high = jnp.concatenate([r[4:8] for r in rows], axis=0)
            refs[4][2 * k + z] = jnp.where(core == 0, low, high).astype(bf16)
            refs[5][2 * k + z] = jnp.where(core == 0, high, low).astype(bf16)


def split(parts, loaded):
    return call(
        split_kernel,
        (shape((8, 8, D), bf16),) * 2,
        [VMEM] * 5,
        [],
        4,
        "split",
        moved=600_000,
    )(loaded, *parts)


def load(sources, after, mib):
    def kernel(*refs):
        count = len(sources)
        ins, outs, sems = refs[:count], refs[count + 1 : -1], refs[-1]
        copies = []
        for k, (_, column) in enumerate(sources):
            source = ins[k] if column is None else ins[k].at[:, pl.ds(column, D)]
            copies.append(pltpu.make_async_copy(source, outs[k], sems.at[k]))
        for copy in copies:
            copy.start()
        outs[count][...] = jnp.zeros_like(outs[count])
        for copy in copies:
            copy.wait()

    return call(
        kernel,
        (shape((D, D), bf16),) * len(sources) + (shape((8, 128), f32),),
        [ANY] * (len(sources) + 1),
        [pltpu.SemaphoreType.DMA((len(sources),))],
        mib,
        "load",
        moved=10_000_000,
    )(*[array for array, _ in sources], after)


def forward_kernel(
    x0, x1, wq_ref, wk_ref, wv_ref, wo_ref, small,
    normed_ref, attended_ref, proj_ref, p_ref, cen_ref, inv_ref, tot_ref,
    acc, xs,
):
    tm = lax.axis_index("tm")
    for core, part in enumerate((x0, x1)):
        for k in range(4):
            y = ((tm >> 1) - k) & 3
            for z in range(2):
                xs[((tm & 9) ^ (8 * z + core)) | (2 * y)] = part[2 * k + z].astype(f32)
    x = xs[...].reshape(TOK, D)
    norm, _ = standard(x)
    normed = (norm * small[9:10, :]).astype(bf16)
    normed_ref[...] = normed
    for i, w_ref in enumerate((wq_ref, wk_ref, wv_ref)):
        for j in range(0, D, CHUNK):
            part = dot(normed, w_ref[:, j : j + CHUNK], 1, 0)
            proj_ref[:, i * D + j : i * D + j + CHUNK] = part.astype(bf16)
    row = lax.broadcasted_iota(jnp.int32, (TOK, TOK), 0)
    col = lax.broadcasted_iota(jnp.int32, (TOK, TOK), 1)
    lag = (col >> 2) - (row >> 2)
    allowed = (
        ((row & 3) == (col & 3))
        & (lag >= -(WINDOW // 2))
        & (lag < WINDOW - WINDOW // 2)
        & (clip_of(small, frames((TOK, TOK), 0)) == clip_of(small, frames((TOK, TOK), 1)))
    )
    acc[...] = jnp.zeros_like(acc)
    for h in range(HEADS):
        a, b = span(h)
        mask = lane_mask(h)
        p_ref[h] = dot(proj_ref[:, a:b] * mask, proj_ref[:, D + a : D + b], 1, 1) * SCALE
    for h in range(0, HEADS, GROUP):
        masked = jnp.where(allowed[None], p_ref[h : h + GROUP], -1e30)
        terms = jnp.exp(masked - jnp.max(masked, axis=2, keepdims=True))
        weights = terms / jnp.sum(terms, axis=2, keepdims=True)
        p_ref[h : h + GROUP] = weights
    for h in range(HEADS):
        a, b = span(h)
        acc[:, a:b] += dot(
            p_ref[h].astype(bf16), proj_ref[:, 2 * D + a : 2 * D + b] * lane_mask(h), 1, 0
        )
    attended = acc[...].astype(bf16)
    attended_ref[...] = attended
    mixed = xs[...].reshape(TOK, D) + dot(attended, wo_ref[...], 1, 0)
    centred, inv_std = standard(mixed)
    cen_ref[...] = centred
    inv_ref[...] = jnp.broadcast_to(inv_std, (TOK, 128))
    final = centred * small[8:9, :]
    clip = clip_of(small, frames((TOK, 1), 0))
    tot_ref[...] = jnp.zeros_like(tot_ref)
    for c in range(CLIPS):
        sums = jnp.sum(jnp.where(clip == c, final, 0.0), axis=0, keepdims=True)
        tot_ref[:, c : c + 1] = jnp.sum(small[0:REWARDS, :] * sums, axis=1, keepdims=True)


def forward(x, weights, small):
    return call(
        forward_kernel,
        (
            shape((TOK, D), bf16),
            shape((TOK, D), bf16),
            shape((TOK, 3 * D), bf16),
            shape((HEADS, TOK, TOK), f32),
            shape((TOK, D), f32),
            shape((TOK, 128), f32),
            shape((REWARDS, 8), f32),
        ),
        [VMEM] * 7,
        [pltpu.VMEM((TOK, D), f32), pltpu.VMEM((16, 8, D), f32)],
        24,
        "forward",
        flops=2_000_000_000,
        moved=14_000_000,
    )(*x, *weights, small)


def place_rows(src, dst, where, x_first):
    x, y, z, _ = where
    for k in range(64):
        first, second, kz = k // 16, k // 4 % 4, k % 4
        kx, ky = (first, second) if x_first else (second, first)
        dp = ((z + kz) & 3) * 4 + ((x + kx) & 3)
        start = dp * 72 + ((y + ky) & 3) * PIECE
        dst[PIECE * k : PIECE * (k + 1), :] = src[pl.ds(start, PIECE), :]


def turn_kernel(normed_ref, attended_ref, keep_ref, send_ref, turned, placed):
    where = position()
    core = where[3]
    turned[0] = normed_ref[...].astype(f32).T
    turned[1] = attended_ref[...].astype(f32).T
    place_rows(turned.at[0], placed, where, True)
    keep_ref[0] = placed[...].astype(bf16)
    send_ref[0] = keep_ref[0]
    place_rows(turned.at[core], placed, where, False)
    keep_ref[1] = placed[...].astype(bf16)
    place_rows(turned.at[1 - core], placed, where, False)
    send_ref[1] = placed[...].astype(bf16)


def turn(normed, attended):
    return call(
        turn_kernel,
        (shape((2, D, TOK), bf16), shape((2, D, TOK), bf16)),
        [VMEM] * 2,
        [pltpu.VMEM((2, D, TOK), f32), pltpu.VMEM((D, TOK), f32)],
        8,
        "turn",
        moved=4_000_000,
    )(normed, attended)


def backward_kernel(
    t0, t1, t2, t3, small, proj_ref, p_ref, cen_ref, inv_ref, wo_ref,
    scores_ref, keep_ref, send_ref,
    dq, dk, dv, wg, da_ref,
):
    clip_col = lax.broadcasted_iota(jnp.int32, (REWARDS, 8), 1)
    count = jnp.ones((REWARDS, 8), f32)
    for c in range(CLIPS):
        count = jnp.where(clip_col == c, small[10:11, c : c + 1] * 64.0, count)
    scores = ((t0[...] + t2[...]) + (t1[...] + t3[...])) / count
    scores = scores[:, 0:CLIPS]
    for c in range(CLIPS):
        column = jnp.where(eye(), scores[:, c : c + 1], 0.0)
        scores_ref[c : c + 1, :] = jnp.sum(column, axis=0, keepdims=True)
    residue = (scores - small[16:24, 0:CLIPS]) / ROWS
    clip = clip_of(small, frames((TOK, 1), 0))
    scaled = jnp.zeros((TOK, D), f32)
    for c in range(CLIPS):
        row = jnp.sum(small[0:REWARDS, :] * residue[:, c : c + 1], axis=0, keepdims=True)
        scaled = jnp.where(clip == c, row * small[8:9, :], scaled)
    centred = cen_ref[...]
    mixed_grad = (
        scaled
        - jnp.mean(scaled, axis=-1, keepdims=True)
        - centred * jnp.mean(scaled * centred, axis=-1, keepdims=True)
    ) * inv_ref[:, 0:1]
    mixed_grad = mixed_grad.astype(bf16)
    da_ref[...] = dot(mixed_grad, wo_ref[...], 1, 1).astype(bf16)
    dq[...] = jnp.zeros_like(dq)
    dk[...] = jnp.zeros_like(dk)
    dv[...] = jnp.zeros_like(dv)
    for h in range(HEADS):
        a, b = span(h)
        mask = lane_mask(h)
        wg[h] = dot(da_ref[:, a:b] * mask, proj_ref[:, 2 * D + a : 2 * D + b], 1, 1)
    for h in range(0, HEADS, GROUP):
        weights = p_ref[h : h + GROUP]
        weight_grad = wg[h : h + GROUP]
        inner = jnp.sum(weights * weight_grad, axis=2, keepdims=True)
        wg[h : h + GROUP] = weights * (weight_grad - inner)
    for h in range(HEADS):
        a, b = span(h)
        mask = lane_mask(h)
        logit_grad = wg[h].astype(bf16)
        dq[:, a:b] += dot(logit_grad, proj_ref[:, D + a : D + b] * mask, 1, 0)
        dk[:, a:b] += dot(logit_grad, proj_ref[:, a:b] * mask, 0, 0)
        dv[:, a:b] += dot(p_ref[h].astype(bf16), da_ref[:, a:b] * mask, 0, 0)

    def store(ref_qk, ref_vo):
        ref_qk[0] = (dq[...] * SCALE).astype(bf16)
        ref_qk[1] = (dk[...] * SCALE).astype(bf16)
        ref_vo[0] = dv[...].astype(bf16)
        ref_vo[1] = mixed_grad

    core = position()[3]

    @pl.when(core == 0)
    def _():
        store(keep_ref, send_ref)

    @pl.when(core != 0)
    def _():
        store(send_ref, keep_ref)


def backward(totals, small, proj, p, centred, inv, w_out):
    return call(
        backward_kernel,
        (
            shape((CLIPS, REWARDS), f32),
            shape((2, TOK, D), bf16),
            shape((2, TOK, D), bf16),
        ),
        [VMEM] * 10,
        [pltpu.VMEM((TOK, D), f32)] * 3
        + [
            pltpu.VMEM((HEADS, TOK, TOK), f32),
            pltpu.VMEM((TOK, D), bf16),
        ],
        16,
        "backward",
        flops=1_500_000_000,
        moved=8_000_000,
    )(*totals, small, proj, p, centred, inv, w_out)


PARTS = ((2, 0), (2, 1), (1, 1), (3, 0), (1, 0), (3, 1))


def gradient_kernel(lk, lr, rk, rr, *outs):
    for i in range(2):
        right = jnp.concatenate([rk[i], rr[i]], axis=0)
        for k in (2, 1, 3, 0):
            rows = slice(288 * k, 288 * (k + 1))
            left = jnp.concatenate([lk[i, rows], lr[i, rows]], axis=1)
            part = dot(left, right, 1, 0).astype(bf16)
            if k == 0:
                outs[7 * i + 6][...] = part
            else:
                for j, (distance, piece) in enumerate(PARTS):
                    if distance == k:
                        outs[7 * i + j][...] = part[144 * piece : 144 * (piece + 1)]


def gradient(left_keep, left_recv, right_keep, right_recv):
    parts = call(
        gradient_kernel,
        ((shape((144, D), bf16),) * 6 + (shape((288, D), bf16),)) * 2,
        [VMEM] * 4,
        [],
        16,
        "gradient",
        flops=1_400_000_000,
        moved=8_000_000,
    )(left_keep, left_recv, right_keep, right_recv)
    return parts[:7], parts[7:]


def relay_kernel(*refs):
    for k in range(4):
        refs[8 + k][...] = (refs[k][...].astype(f32) + refs[4 + k][...].astype(f32)).astype(bf16)


def relay(arrived, own):
    return call(
        relay_kernel,
        (shape((144, D), bf16),) * 4,
        [VMEM] * 8,
        [],
        8,
        "relay",
        moved=4_000_000,
    )(*arrived, *own)


def total(refs):
    result = refs[0][...].astype(f32)
    for ref in refs[1:]:
        result += ref[...].astype(f32)
    return result


SLOT = ((0, 3, 6, 5), (1, 2, 7, 4))


def first_sum_kernel(*refs):
    for i in range(2):
        plain_on, plain_back, relayed_on, relayed_back, own = (refs[2 * j + i] for j in range(5))
        result = own[...].astype(f32) + jnp.concatenate(
            [
                plain_back[...].astype(f32) + relayed_on[...].astype(f32),
                plain_on[...].astype(f32) + relayed_back[...].astype(f32),
            ],
            axis=0,
        )
        for k in range(4):
            refs[10 + SLOT[1 - i][k]][...] = result[72 * k : 72 * (k + 1)].astype(bf16)


def first_sum(parts):
    return call(
        first_sum_kernel,
        (shape((72, D), bf16),) * 8,
        [VMEM] * 10,
        [],
        12,
        "first_sum",
        moved=6_000_000,
    )(*parts)


def second_sum_kernel(*refs):
    sums = [total([refs[SLOT[i][k]] for k in range(4)]) for i in (1, 0)]
    rest = jnp.zeros((4, D), f32)
    for k in range(4):
        rows = slice(PIECE * k, PIECE * (k + 1))
        refs[8 + k][...] = jnp.concatenate([sums[0][rows], sums[1][rows], rest], axis=0).astype(
            bf16
        )


def second_sum(parts):
    return call(
        second_sum_kernel,
        (shape((40, D), bf16),) * 4,
        [VMEM] * 8,
        [],
        6,
        "second_sum",
        moved=1_700_000,
    )(*parts)


def sum_kernel(*refs):
    refs[-1][...] = total(refs[:-1]).astype(bf16)


def pair_sum_kernel(a, b, out):
    out[...] = a[...] + b[...]


def pair_sum(*parts):
    return call(
        pair_sum_kernel, shape((REWARDS, 8), f32), [VMEM] * 2, [], 1, "pair_sum", moved=20_000
    )(*parts)


def plain_sum(parts):
    return call(
        sum_kernel,
        shape(parts[0].shape, bf16),
        [VMEM] * len(parts),
        [],
        3,
        "plain_sum",
        moved=500_000,
    )(*parts)


GATHER = ((0, 0), (1, 0), (3, 1), (3, 0), (1, 1), (2, 0), (2, 1), (0, 1))


def last_kernel(*refs):
    qkv_ref, out_ref, held = refs[8:]
    _, y_here, _, core = position()
    for j, (k, other) in enumerate(GATHER):
        held[core ^ other, (y_here - k) & 3] = refs[j][...].astype(f32)
    for y in range(4):
        rows = slice(PIECE * y, PIECE * (y + 1))
        qkv_ref[rows, 0:D] = held[0, y, 0:PIECE]
        qkv_ref[rows, D : 2 * D] = held[0, y, PIECE : 2 * PIECE]
        qkv_ref[rows, 2 * D : 3 * D] = held[1, y, 0:PIECE]
        out_ref[rows, :] = held[1, y, PIECE : 2 * PIECE]


def last(parts):
    return call(
        last_kernel,
        (shape((72, 3 * D), f32), shape((72, D), f32)),
        [VMEM] * 8,
        [pltpu.VMEM((2, 4, 40, D), f32)],
        10,
        "last",
        moved=2_000_000,
    )(*parts)


def to_core(block):
    return lax.ppermute(block, "tm", [(i, i ^ 1) for i in range(16)])


def to_far(block):
    return lax.ppermute(block, "tm", [(i, i ^ 8) for i in range(16)])


def along_y(block, k, core=0):
    return lax.ppermute(block, "tm", [(i, (i & 9 | (i + 2 * k) & 6) ^ core) for i in range(16)])


def along_x(block, k):
    return lax.ppermute(block, "dp", [(i, i & 12 | (i + k) & 3) for i in range(16)])


def around_z(block, k):
    route = []
    for tm in range(16):
        for dp in range(16):
            step = {1: 1, 3: -1, 2: -2 if tm & 1 else 2}[k]
            z = ((tm >> 3) * 4 + (dp >> 2) + step) & 7
            there = (tm & 7 | (z >> 2) << 3) * 16 + ((z & 3) << 2 | dp & 3)
            route.append((tm * 16 + dp, there))
    return lax.ppermute(block, ("tm", "dp"), route)


def exchange(slots):
    moved = list(slots)
    for k in (1, 3, 2):
        moved[SLOT[1][k]] = along_y(slots[SLOT[1][k]], k)
        moved[SLOT[0][k]] = along_x(slots[SLOT[0][k]], k)
    return moved


def around(x_half, y_half):
    on, back = (along_x, along_y), 3
    halves = (x_half, y_half)
    arrived = [on[i](halves[i][j], 1 if j == 0 else back) for j in range(2) for i in range(2)]
    plain = [on[i](halves[i][2 + j], 1 if j == 0 else back) for j in range(2) for i in range(2)]
    own = [halves[i][4 + j] for j in range(2) for i in range(2)]
    sums = relay(arrived, own)
    relayed = [on[i](sums[2 * j + i], 1 if j == 0 else back) for j in range(2) for i in range(2)]
    return first_sum(plain + relayed + [x_half[6], y_half[6]])


def on_device(tokens, clip_frames, teacher_scores, ln_gain, w_qkv, w_out, out_gain, reward_head):
    keep, send = halves(tokens[0])
    small = pack(clip_frames, teacher_scores[0], ln_gain, out_gain, reward_head.T)
    wq, wk, loaded = load([(w_qkv, 0), (w_qkv, D)], keep, 44)
    parts = deal(keep, to_far(send), small, loaded)
    wv, wo, loaded = load([(w_qkv, 2 * D), (w_out, None)], parts[0], 42)
    weights = wq, wk, wv, wo
    keep, send = split([parts[0]] + [along_y(parts[k], k) for k in (1, 2, 3)], loaded)
    x = [keep, to_core(send)]
    normed, attended, proj, p, centred, inv, partial = forward(x, weights, small)
    partial = pair_sum(partial, to_core(partial))
    partial = pair_sum(partial, to_far(partial))
    totals = [partial] + [along_y(partial, k) for k in (1, 2, 3)]
    left_keep, left_send = turn(normed, attended)
    left_recv = to_core(left_send)
    scores, right_keep, right_send = backward(totals, small, proj, p, centred, inv, weights[3])
    parts = gradient(left_keep, left_recv, right_keep, to_core(right_send))
    parts = second_sum(exchange(around(*parts)))
    part = plain_sum([parts[0]] + [around_z(parts[k], k) for k in (1, 2, 3)])
    part = plain_sum([part, to_far(part)])
    qkv_total, out_total = last([part] + [along_y(part, k, core) for k, core in GATHER[1:]])
    return (scores[None], qkv_total, out_total)


def solution(mesh):
    return jax.shard_map(
        on_device,
        mesh=mesh,
        in_specs=(
            P("dp", "tm", None, None),
            P("dp", None),
            P("dp", None, None),
            P(),
            P(),
            P(),
            P(),
            P(),
        ),
        out_specs=(P("dp", None, None), P("dp", None), P("dp", None)),
        check_vma=False,
    )
```

```python
import math

import jax
import jax.numpy as jnp
from jax import lax
from jax.experimental import pallas as pl
from jax.experimental.pallas import tpu as pltpu
from jax.sharding import PartitionSpec as P

HEADS = 16
HEAD_DIM = 72
WINDOW = 8
D = 1152
TOK = 128
CLIPS = 4
REWARDS = 8
ROWS = 16
CHUNK = 384
PIECE = 18
GROUP = 4
EPS = 1e-06
SCALE = 1.0 / math.sqrt(HEAD_DIM)

f32 = jnp.float32
bf16 = jnp.bfloat16
HI = lax.Precision.HIGHEST
VMEM = pl.BlockSpec(memory_space=pltpu.VMEM)
ANY = pl.BlockSpec(memory_space=pl.ANY)


def dot(a, b, ca, cb, precision=None):
    return lax.dot_general(
        a, b, (((ca,), (cb,)), ((), ())), preferred_element_type=f32, precision=precision
    )


def clip_of(small, frame):
    end, clip = small[10:11, 0:1], jnp.zeros_like(frame)
    for c in range(CLIPS):
        clip += (frame >= end).astype(f32)
        if c + 1 < CLIPS:
            end = end + small[10:11, c + 1 : c + 2]
    return clip


def frames(dims, axis):
    return (lax.broadcasted_iota(jnp.int32, dims, axis) >> 2).astype(f32)


def span(h):
    low = HEAD_DIM * h
    return low // 128 * 128, -(-(low + HEAD_DIM) // 128) * 128


def lane_mask(h):
    start, end = span(h)
    lane = lax.broadcasted_iota(jnp.int32, (1, end - start), 1) + (start - HEAD_DIM * h)
    return ((lane >= 0) & (lane < HEAD_DIM)).astype(f32).astype(bf16)


def standard(values):
    centre = values - jnp.mean(values, axis=-1, keepdims=True)
    inv_std = lax.rsqrt(jnp.mean(centre * centre, axis=-1, keepdims=True) + EPS)
    return centre * inv_std, inv_std


def position():
    tm, dp = lax.axis_index("tm"), lax.axis_index("dp")
    return dp & 3, (tm >> 1) & 3, dp >> 2, tm & 1


def shape(dims, kind):
    return jax.ShapeDtypeStruct(dims, kind)


def call(kernel, out_shape, in_specs, scratch, mib, name, flops=0, moved=0):
    return pl.pallas_call(
        kernel,
        out_shape=out_shape,
        in_specs=in_specs,
        out_specs=jax.tree.map(lambda _: VMEM, out_shape),
        scratch_shapes=scratch,
        compiler_params=pltpu.CompilerParams(vmem_limit_bytes=mib << 20),
        cost_estimate=pl.CostEstimate(flops=flops, bytes_accessed=moved, transcendentals=0),
        name=name,
    )


def halves_kernel(x_ref, keep_ref, send_ref):
    z = lax.axis_index("tm") >> 3
    for a in range(2):
        keep_ref[a] = x_ref[a, z]
        send_ref[a] = x_ref[a, 1 - z]


def halves(tokens):
    return call(
        halves_kernel,
        (shape((2, 4, 8, D), bf16),) * 2,
        [VMEM],
        [],
        4,
        "halves",
        moved=600_000,
    )(tokens.reshape(2, 2, 4, 8, D))


def deal_kernel(keep_ref, far_ref, small, loaded, *outs):
    _, y, _, _ = position()
    for k in range(4):
        for a in range(2):
            outs[k][a] = keep_ref[a, (y + k) & 3]
            outs[k][2 + a] = far_ref[a, (y + k) & 3]


def deal(keep, far, small, loaded):
    return call(
        deal_kernel,
        (shape((4, 8, D), bf16),) * 4,
        [VMEM] * 4,
        [],
        4,
        "deal",
        moved=600_000,
    )(keep, far, small, loaded)


def pack_kernel(lens_ref, teacher_ref, ln_ref, og_ref, rh_ref, small):
    small[...] = jnp.zeros_like(small)
    small[0:REWARDS] = rh_ref[...]
    small[8] = og_ref[...]
    small[9] = ln_ref[...]
    small[10:11, 0:CLIPS] = lens_ref[...].astype(f32)
    for c in range(CLIPS):
        small[16 : 16 + REWARDS, c : c + 1] = upright(teacher_ref[c : c + 1])


def upright(row):
    return jnp.sum(jnp.where(eye(), row, 0.0), axis=1, keepdims=True)


def eye():
    side = (REWARDS, REWARDS)
    return lax.broadcasted_iota(jnp.int32, side, 0) == lax.broadcasted_iota(jnp.int32, side, 1)


def pack(clip_frames, teacher, ln_gain, out_gain, reward):
    return call(
        pack_kernel, shape((24, D), f32), [VMEM] * 5, [], 2, "pack", moved=200_000
    )(clip_frames, teacher, ln_gain, out_gain, reward)


def split_kernel(loaded, *refs):
    core = position()[3]
    for k in range(4):
        for z in range(2):
            rows = [refs[k][2 * z + a].astype(f32) for a in range(2)]
            low = jnp.concatenate([r[0:4] for r in rows], axis=0)
            high = jnp.concatenate([r[4:8] for r in rows], axis=0)
            refs[4][2 * k + z] = jnp.where(core == 0, low, high).astype(bf16)
            refs[5][2 * k + z] = jnp.where(core == 0, high, low).astype(bf16)


def split(parts, loaded):
    return call(
        split_kernel,
        (shape((8, 8, D), bf16),) * 2,
        [VMEM] * 5,
        [],
        4,
        "split",
        moved=600_000,
    )(loaded, *parts)


def load(sources, after, mib):
    def kernel(*refs):
        count = len(sources)
        ins, outs, sems = refs[:count], refs[count + 1 : -1], refs[-1]
        copies = []
        for k, (_, column) in enumerate(sources):
            source = ins[k] if column is None else ins[k].at[:, pl.ds(column, D)]
            copies.append(pltpu.make_async_copy(source, outs[k], sems.at[k]))
        for copy in copies:
            copy.start()
        outs[count][...] = jnp.zeros_like(outs[count])
        for copy in copies:
            copy.wait()

    return call(
        kernel,
        (shape((D, D), bf16),) * len(sources) + (shape((8, 128), f32),),
        [ANY] * (len(sources) + 1),
        [pltpu.SemaphoreType.DMA((len(sources),))],
        mib,
        "load",
        moved=10_000_000,
    )(*[array for array, _ in sources], after)


def forward_kernel(
    x0, x1, wq_ref, wk_ref, wv_ref, wo_ref, small,
    normed_ref, attended_ref, proj_ref, p_ref, cen_ref, inv_ref, tot_ref,
    acc, xs,
):
    tm = lax.axis_index("tm")
    for core, part in enumerate((x0, x1)):
        for k in range(4):
            y = ((tm >> 1) - k) & 3
            for z in range(2):
                xs[((tm & 9) ^ (8 * z + core)) | (2 * y)] = part[2 * k + z].astype(f32)
    x = xs[...].reshape(TOK, D)
    norm, _ = standard(x)
    normed = (norm * small[9:10, :]).astype(bf16)
    normed_ref[...] = normed
    for i, w_ref in enumerate((wq_ref, wk_ref, wv_ref)):
        for j in range(0, D, CHUNK):
            part = dot(normed, w_ref[:, j : j + CHUNK], 1, 0)
            proj_ref[:, i * D + j : i * D + j + CHUNK] = part.astype(bf16)
    row = lax.broadcasted_iota(jnp.int32, (TOK, TOK), 0)
    col = lax.broadcasted_iota(jnp.int32, (TOK, TOK), 1)
    lag = (col >> 2) - (row >> 2)
    allowed = (
        ((row & 3) == (col & 3))
        & (lag >= -(WINDOW // 2))
        & (lag < WINDOW - WINDOW // 2)
        & (clip_of(small, frames((TOK, TOK), 0)) == clip_of(small, frames((TOK, TOK), 1)))
    )
    acc[...] = jnp.zeros_like(acc)
    for h in range(HEADS):
        a, b = span(h)
        mask = lane_mask(h)
        p_ref[h] = dot(proj_ref[:, a:b] * mask, proj_ref[:, D + a : D + b], 1, 1) * SCALE
    for h in range(0, HEADS, GROUP):
        masked = jnp.where(allowed[None], p_ref[h : h + GROUP], -1e30)
        terms = jnp.exp(masked - jnp.max(masked, axis=2, keepdims=True))
        weights = terms / jnp.sum(terms, axis=2, keepdims=True)
        p_ref[h : h + GROUP] = weights
    for h in range(HEADS):
        a, b = span(h)
        acc[:, a:b] += dot(
            p_ref[h].astype(bf16), proj_ref[:, 2 * D + a : 2 * D + b] * lane_mask(h), 1, 0
        )
    attended = acc[...].astype(bf16)
    attended_ref[...] = attended
    mixed = xs[...].reshape(TOK, D) + dot(attended, wo_ref[...], 1, 0)
    centred, inv_std = standard(mixed)
    cen_ref[...] = centred
    inv_ref[...] = jnp.broadcast_to(inv_std, (TOK, 128))
    final = centred * small[8:9, :]
    clip = clip_of(small, frames((TOK, 1), 0))
    tot_ref[...] = jnp.zeros_like(tot_ref)
    for c in range(CLIPS):
        sums = jnp.sum(jnp.where(clip == c, final, 0.0), axis=0, keepdims=True)
        tot_ref[:, c : c + 1] = jnp.sum(small[0:REWARDS, :] * sums, axis=1, keepdims=True)


def forward(x, weights, small):
    return call(
        forward_kernel,
        (
            shape((TOK, D), bf16),
            shape((TOK, D), bf16),
            shape((TOK, 3 * D), bf16),
            shape((HEADS, TOK, TOK), f32),
            shape((TOK, D), f32),
            shape((TOK, 128), f32),
            shape((REWARDS, 8), f32),
        ),
        [VMEM] * 7,
        [pltpu.VMEM((TOK, D), f32), pltpu.VMEM((16, 8, D), f32)],
        24,
        "forward",
        flops=2_000_000_000,
        moved=14_000_000,
    )(*x, *weights, small)


def place_rows(src, dst, where, x_first):
    x, y, z, _ = where
    for k in range(64):
        first, second, kz = k // 16, k // 4 % 4, k % 4
        kx, ky = (first, second) if x_first else (second, first)
        dp = ((z + kz) & 3) * 4 + ((x + kx) & 3)
        start = dp * 72 + ((y + ky) & 3) * PIECE
        dst[PIECE * k : PIECE * (k + 1), :] = src[pl.ds(start, PIECE), :]


def turn_kernel(normed_ref, attended_ref, keep_ref, send_ref, turned, placed):
    where = position()
    core = where[3]
    turned[0] = normed_ref[...].astype(f32).T
    turned[1] = attended_ref[...].astype(f32).T
    place_rows(turned.at[0], placed, where, True)
    keep_ref[0] = placed[...].astype(bf16)
    send_ref[0] = keep_ref[0]
    place_rows(turned.at[core], placed, where, False)
    keep_ref[1] = placed[...].astype(bf16)
    place_rows(turned.at[1 - core], placed, where, False)
    send_ref[1] = placed[...].astype(bf16)


def turn(normed, attended):
    return call(
        turn_kernel,
        (shape((2, D, TOK), bf16), shape((2, D, TOK), bf16)),
        [VMEM] * 2,
        [pltpu.VMEM((2, D, TOK), f32), pltpu.VMEM((D, TOK), f32)],
        8,
        "turn",
        moved=4_000_000,
    )(normed, attended)


def backward_kernel(
    t0, t1, t2, t3, small, proj_ref, p_ref, cen_ref, inv_ref, wo_ref,
    scores_ref, keep_ref, send_ref,
    dq, dk, dv, wg, da_ref,
):
    clip_col = lax.broadcasted_iota(jnp.int32, (REWARDS, 8), 1)
    count = jnp.ones((REWARDS, 8), f32)
    for c in range(CLIPS):
        count = jnp.where(clip_col == c, small[10:11, c : c + 1] * 64.0, count)
    scores = ((t0[...] + t2[...]) + (t1[...] + t3[...])) / count
    scores = scores[:, 0:CLIPS]
    for c in range(CLIPS):
        column = jnp.where(eye(), scores[:, c : c + 1], 0.0)
        scores_ref[c : c + 1, :] = jnp.sum(column, axis=0, keepdims=True)
    residue = (scores - small[16:24, 0:CLIPS]) / ROWS
    clip = clip_of(small, frames((TOK, 1), 0))
    scaled = jnp.zeros((TOK, D), f32)
    for c in range(CLIPS):
        row = jnp.sum(small[0:REWARDS, :] * residue[:, c : c + 1], axis=0, keepdims=True)
        scaled = jnp.where(clip == c, row * small[8:9, :], scaled)
    centred = cen_ref[...]
    mixed_grad = (
        scaled
        - jnp.mean(scaled, axis=-1, keepdims=True)
        - centred * jnp.mean(scaled * centred, axis=-1, keepdims=True)
    ) * inv_ref[:, 0:1]
    mixed_grad = mixed_grad.astype(bf16)
    da_ref[...] = dot(mixed_grad, wo_ref[...], 1, 1).astype(bf16)
    dq[...] = jnp.zeros_like(dq)
    dk[...] = jnp.zeros_like(dk)
    dv[...] = jnp.zeros_like(dv)
    for h in range(HEADS):
        a, b = span(h)
        mask = lane_mask(h)
        wg[h] = dot(da_ref[:, a:b] * mask, proj_ref[:, 2 * D + a : 2 * D + b], 1, 1)
    for h in range(0, HEADS, GROUP):
        weights = p_ref[h : h + GROUP]
        weight_grad = wg[h : h + GROUP]
        inner = jnp.sum(weights * weight_grad, axis=2, keepdims=True)
        wg[h : h + GROUP] = weights * (weight_grad - inner)
    for h in range(HEADS):
        a, b = span(h)
        mask = lane_mask(h)
        logit_grad = wg[h].astype(bf16)
        dq[:, a:b] += dot(logit_grad, proj_ref[:, D + a : D + b] * mask, 1, 0)
        dk[:, a:b] += dot(logit_grad, proj_ref[:, a:b] * mask, 0, 0)
        dv[:, a:b] += dot(p_ref[h].astype(bf16), da_ref[:, a:b] * mask, 0, 0)

    def store(ref_qk, ref_vo):
        ref_qk[0] = (dq[...] * SCALE).astype(bf16)
        ref_qk[1] = (dk[...] * SCALE).astype(bf16)
        ref_vo[0] = dv[...].astype(bf16)
        ref_vo[1] = mixed_grad

    core = position()[3]

    @pl.when(core == 0)
    def _():
        store(keep_ref, send_ref)

    @pl.when(core != 0)
    def _():
        store(send_ref, keep_ref)


def backward(totals, small, proj, p, centred, inv, w_out):
    return call(
        backward_kernel,
        (
            shape((CLIPS, REWARDS), f32),
            shape((2, TOK, D), bf16),
            shape((2, TOK, D), bf16),
        ),
        [VMEM] * 10,
        [pltpu.VMEM((TOK, D), f32)] * 3
        + [
            pltpu.VMEM((HEADS, TOK, TOK), f32),
            pltpu.VMEM((TOK, D), bf16),
        ],
        16,
        "backward",
        flops=1_500_000_000,
        moved=8_000_000,
    )(*totals, small, proj, p, centred, inv, w_out)


PARTS = ((2, 0), (2, 1), (1, 1), (3, 0), (1, 0), (3, 1))


def gradient_kernel(lk, lr, rk, rr, *outs):
    for i in range(2):
        right = jnp.concatenate([rk[i], rr[i]], axis=0)
        for k in (2, 1, 3, 0):
            rows = slice(288 * k, 288 * (k + 1))
            left = jnp.concatenate([lk[i, rows], lr[i, rows]], axis=1)
            part = dot(left, right, 1, 0).astype(bf16)
            if k == 0:
                outs[7 * i + 6][...] = part
            else:
                for j, (distance, piece) in enumerate(PARTS):
                    if distance == k:
                        outs[7 * i + j][...] = part[144 * piece : 144 * (piece + 1)]


def gradient(left_keep, left_recv, right_keep, right_recv):
    parts = call(
        gradient_kernel,
        ((shape((144, D), bf16),) * 6 + (shape((288, D), bf16),)) * 2,
        [VMEM] * 4,
        [],
        16,
        "gradient",
        flops=1_400_000_000,
        moved=8_000_000,
    )(left_keep, left_recv, right_keep, right_recv)
    return parts[:7], parts[7:]


def relay_kernel(*refs):
    for k in range(4):
        refs[8 + k][...] = (refs[k][...].astype(f32) + refs[4 + k][...].astype(f32)).astype(bf16)


def relay(arrived, own):
    return call(
        relay_kernel,
        (shape((144, D), bf16),) * 4,
        [VMEM] * 8,
        [],
        8,
        "relay",
        moved=4_000_000,
    )(*arrived, *own)


def total(refs):
    result = refs[0][...].astype(f32)
    for ref in refs[1:]:
        result += ref[...].astype(f32)
    return result


SLOT = ((0, 3, 6, 5), (1, 2, 7, 4))


def first_sum_kernel(*refs):
    for i in range(2):
        plain_on, plain_back, relayed_on, relayed_back, own = (refs[2 * j + i] for j in range(5))
        result = own[...].astype(f32) + jnp.concatenate(
            [
                plain_back[...].astype(f32) + relayed_on[...].astype(f32),
                plain_on[...].astype(f32) + relayed_back[...].astype(f32),
            ],
            axis=0,
        )
        for k in range(4):
            refs[10 + SLOT[1 - i][k]][...] = result[72 * k : 72 * (k + 1)].astype(bf16)


def first_sum(parts):
    return call(
        first_sum_kernel,
        (shape((72, D), bf16),) * 8,
        [VMEM] * 10,
        [],
        12,
        "first_sum",
        moved=6_000_000,
    )(*parts)


def second_sum_kernel(*refs):
    sums = [total([refs[SLOT[i][k]] for k in range(4)]) for i in (1, 0)]
    rest = jnp.zeros((4, D), f32)
    for k in range(4):
        rows = slice(PIECE * k, PIECE * (k + 1))
        refs[8 + k][...] = jnp.concatenate([sums[0][rows], sums[1][rows], rest], axis=0).astype(
            bf16
        )


def second_sum(parts):
    return call(
        second_sum_kernel,
        (shape((40, D), bf16),) * 4,
        [VMEM] * 8,
        [],
        6,
        "second_sum",
        moved=1_700_000,
    )(*parts)


def sum_kernel(*refs):
    refs[-1][...] = total(refs[:-1]).astype(bf16)


def pair_sum_kernel(a, b, *rest):
    out = rest[-1]
    out[...] = a[...] + b[...]


def pair_sum(a, b, *after):
    specs = [VMEM] * 2 + [ANY] * len(after)
    return call(
        pair_sum_kernel, shape((REWARDS, 8), f32), specs, [], 1, "pair_sum", moved=20_000
    )(a, b, *after)


def plain_sum(parts):
    return call(
        sum_kernel,
        shape(parts[0].shape, bf16),
        [VMEM] * len(parts),
        [],
        3,
        "plain_sum",
        moved=500_000,
    )(*parts)


def stack_kernel(*refs):
    for k in range(4):
        refs[4][k] = refs[k][...]


def stack(parts):
    return call(
        stack_kernel, shape((4, 40, D), bf16), [VMEM] * 4, [], 3, "stack", moved=800_000
    )(*parts)


def last_kernel(mine, other, qkv_ref, out_ref, held):
    _, y_here, _, core = position()
    for k in range(4):
        y = (y_here - k) & 3
        held[core, y] = mine[k].astype(f32)
        held[1 - core, y] = other[k].astype(f32)
    for y in range(4):
        rows = slice(PIECE * y, PIECE * (y + 1))
        qkv_ref[rows, 0:D] = held[0, y, 0:PIECE]
        qkv_ref[rows, D : 2 * D] = held[0, y, PIECE : 2 * PIECE]
        qkv_ref[rows, 2 * D : 3 * D] = held[1, y, 0:PIECE]
        out_ref[rows, :] = held[1, y, PIECE : 2 * PIECE]


def last(mine, other):
    return call(
        last_kernel,
        (shape((72, 3 * D), f32), shape((72, D), f32)),
        [VMEM] * 2,
        [pltpu.VMEM((2, 4, 40, D), f32)],
        10,
        "last",
        moved=2_000_000,
    )(mine, other)


def to_core(block):
    return lax.ppermute(block, "tm", [(i, i ^ 1) for i in range(16)])


def to_far(block):
    return lax.ppermute(block, "tm", [(i, i ^ 8) for i in range(16)])


def along_y(block, k):
    return lax.ppermute(block, "tm", [(i, i & 9 | (i + 2 * k) & 6) for i in range(16)])


def along_x(block, k):
    return lax.ppermute(block, "dp", [(i, i & 12 | (i + k) & 3) for i in range(16)])


def around_z(block, k):
    route = []
    for tm in range(16):
        for dp in range(16):
            step = {1: 1, 3: -1, 2: -2 if tm & 1 else 2}[k]
            z = ((tm >> 3) * 4 + (dp >> 2) + step) & 7
            there = (tm & 7 | (z >> 2) << 3) * 16 + ((z & 3) << 2 | dp & 3)
            route.append((tm * 16 + dp, there))
    return lax.ppermute(block, ("tm", "dp"), route)


def exchange(slots):
    moved = list(slots)
    for k in (1, 3, 2):
        moved[SLOT[1][k]] = along_y(slots[SLOT[1][k]], k)
        moved[SLOT[0][k]] = along_x(slots[SLOT[0][k]], k)
    return moved


def around(x_half, y_half):
    on, back = (along_x, along_y), 3
    halves = (x_half, y_half)
    arrived = [on[i](halves[i][j], 1 if j == 0 else back) for j in range(2) for i in range(2)]
    plain = []
    for j in range(2):
        for i in range(2):
            block, _ = lax.optimization_barrier((halves[i][2 + j], arrived[2 * j + i]))
            plain.append(on[i](block, 1 if j == 0 else back))
    own = [halves[i][4 + j] for j in range(2) for i in range(2)]
    sums = relay(arrived, own)
    relayed = [on[i](sums[2 * j + i], 1 if j == 0 else back) for j in range(2) for i in range(2)]
    return first_sum(plain + relayed + [x_half[6], y_half[6]])


def on_device(tokens, clip_frames, teacher_scores, ln_gain, w_qkv, w_out, out_gain, reward_head):
    keep, send = halves(tokens[0])
    small = pack(clip_frames, teacher_scores[0], ln_gain, out_gain, reward_head.T)
    wq, wk, loaded = load([(w_qkv, 0), (w_qkv, D)], keep, 44)
    parts = deal(keep, to_far(send), small, loaded)
    wv, wo, loaded = load([(w_qkv, 2 * D), (w_out, None)], parts[0], 42)
    weights = wq, wk, wv, wo
    keep, send = split([parts[0]] + [along_y(parts[k], k) for k in (1, 2, 3)], loaded)
    x = [keep, to_core(send)]
    normed, attended, proj, p, centred, inv, partial = forward(x, weights, small)
    partial = pair_sum(partial, to_core(partial))
    normed, attended, _ = lax.optimization_barrier((normed, attended, partial))
    left_keep, left_send = turn(normed, attended)
    left_recv = to_core(left_send)
    partial = pair_sum(partial, to_far(partial), left_keep)
    totals = [partial] + [along_y(partial, k) for k in (1, 2, 3)]
    scores, right_keep, right_send = backward(totals, small, proj, p, centred, inv, weights[3])
    parts = gradient(left_keep, left_recv, right_keep, to_core(right_send))
    parts = second_sum(exchange(around(*parts)))
    part = plain_sum([parts[0]] + [around_z(parts[k], k) for k in (1, 2, 3)])
    part = plain_sum([part, to_far(part)])
    mine = stack([part] + [along_y(part, k) for k in (1, 2, 3)])
    qkv_total, out_total = last(mine, to_core(mine))
    return (scores[None], qkv_total, out_total)


def solution(mesh):
    return jax.shard_map(
        on_device,
        mesh=mesh,
        in_specs=(
            P("dp", "tm", None, None),
            P("dp", None),
            P("dp", None, None),
            P(),
            P(),
            P(),
            P(),
            P(),
        ),
        out_specs=(P("dp", None, None), P("dp", None), P("dp", None)),
        check_vma=False,
    )
```

```python
import math

import jax
import jax.numpy as jnp
from jax import lax
from jax.experimental import pallas as pl
from jax.experimental.pallas import tpu as pltpu
from jax.sharding import PartitionSpec as P

HEADS = 16
HEAD_DIM = 72
WINDOW = 8
D = 1152
TOK = 128
CLIPS = 4
REWARDS = 8
ROWS = 16
CHUNK = 384
PIECE = 18
GROUP = 4
EPS = 1e-06
SCALE = 1.0 / math.sqrt(HEAD_DIM)

f32 = jnp.float32
bf16 = jnp.bfloat16
HI = lax.Precision.HIGHEST
VMEM = pl.BlockSpec(memory_space=pltpu.VMEM)
ANY = pl.BlockSpec(memory_space=pl.ANY)


def dot(a, b, ca, cb, precision=None):
    return lax.dot_general(
        a, b, (((ca,), (cb,)), ((), ())), preferred_element_type=f32, precision=precision
    )


def clip_of(small, frame):
    end, clip = small[10:11, 0:1], jnp.zeros_like(frame)
    for c in range(CLIPS):
        clip += (frame >= end).astype(f32)
        if c + 1 < CLIPS:
            end = end + small[10:11, c + 1 : c + 2]
    return clip


def frames(dims, axis):
    return (lax.broadcasted_iota(jnp.int32, dims, axis) >> 2).astype(f32)


def span(h):
    low = HEAD_DIM * h
    return low // 128 * 128, -(-(low + HEAD_DIM) // 128) * 128


def lane_mask(h):
    start, end = span(h)
    lane = lax.broadcasted_iota(jnp.int32, (1, end - start), 1) + (start - HEAD_DIM * h)
    return ((lane >= 0) & (lane < HEAD_DIM)).astype(f32).astype(bf16)


def standard(values):
    centre = values - jnp.mean(values, axis=-1, keepdims=True)
    inv_std = lax.rsqrt(jnp.mean(centre * centre, axis=-1, keepdims=True) + EPS)
    return centre * inv_std, inv_std


def position():
    tm, dp = lax.axis_index("tm"), lax.axis_index("dp")
    return dp & 3, (tm >> 1) & 3, dp >> 2, tm & 1


def shape(dims, kind):
    return jax.ShapeDtypeStruct(dims, kind)


def call(kernel, out_shape, in_specs, scratch, mib, name, flops=0, moved=0):
    return pl.pallas_call(
        kernel,
        out_shape=out_shape,
        in_specs=in_specs,
        out_specs=jax.tree.map(lambda _: VMEM, out_shape),
        scratch_shapes=scratch,
        compiler_params=pltpu.CompilerParams(vmem_limit_bytes=mib << 20),
        cost_estimate=pl.CostEstimate(flops=flops, bytes_accessed=moved, transcendentals=0),
        name=name,
    )


def deal_kernel(x_ref, far_ref, small, loaded, *outs):
    _, y, _, _ = position()
    z = lax.axis_index("tm") >> 3
    for k in range(4):
        for a in range(2):
            outs[k][a] = x_ref[a, z, (y + k) & 3]
            outs[k][2 + a] = far_ref[a, (y + k) & 3]


def deal(tokens, far, small, loaded):
    return call(
        deal_kernel,
        (shape((4, 8, D), bf16),) * 4,
        [VMEM] * 4,
        [],
        4,
        "deal",
        moved=600_000,
    )(tokens, far, small, loaded)


def pack_kernel(lens_ref, teacher_ref, ln_ref, og_ref, rh_ref, small):
    small[...] = jnp.zeros_like(small)
    small[0:REWARDS] = rh_ref[...]
    small[8] = og_ref[...]
    small[9] = ln_ref[...]
    small[10:11, 0:CLIPS] = lens_ref[...].astype(f32)
    for c in range(CLIPS):
        small[16 : 16 + REWARDS, c : c + 1] = upright(teacher_ref[c : c + 1])


def upright(row):
    return jnp.sum(jnp.where(eye(), row, 0.0), axis=1, keepdims=True)


def eye():
    side = (REWARDS, REWARDS)
    return lax.broadcasted_iota(jnp.int32, side, 0) == lax.broadcasted_iota(jnp.int32, side, 1)


def pack(clip_frames, teacher, ln_gain, out_gain, reward):
    return call(
        pack_kernel, shape((24, D), f32), [VMEM] * 5, [], 2, "pack", moved=200_000
    )(clip_frames, teacher, ln_gain, out_gain, reward)


def split_kernel(loaded, *refs):
    core = position()[3]
    for k in range(4):
        for z in range(2):
            rows = [refs[k][2 * z + a].astype(f32) for a in range(2)]
            low = jnp.concatenate([r[0:4] for r in rows], axis=0)
            high = jnp.concatenate([r[4:8] for r in rows], axis=0)
            refs[4][2 * k + z] = jnp.where(core == 0, low, high).astype(bf16)
            refs[5][2 * k + z] = jnp.where(core == 0, high, low).astype(bf16)


def split(parts, loaded):
    return call(
        split_kernel,
        (shape((8, 8, D), bf16),) * 2,
        [VMEM] * 5,
        [],
        4,
        "split",
        moved=600_000,
    )(loaded, *parts)


def load(sources, after, mib):
    def kernel(*refs):
        count = len(sources)
        ins, outs, sems = refs[:count], refs[count + 1 : -1], refs[-1]
        copies = []
        for k, (_, column) in enumerate(sources):
            source = ins[k] if column is None else ins[k].at[:, pl.ds(column, D)]
            copies.append(pltpu.make_async_copy(source, outs[k], sems.at[k]))
        for copy in copies:
            copy.start()
        outs[count][...] = jnp.zeros_like(outs[count])
        for copy in copies:
            copy.wait()

    return call(
        kernel,
        (shape((D, D), bf16),) * len(sources) + (shape((8, 128), f32),),
        [ANY] * (len(sources) + 1),
        [pltpu.SemaphoreType.DMA((len(sources),))],
        mib,
        "load",
        moved=10_000_000,
    )(*[array for array, _ in sources], after)


def forward_kernel(
    x0, x1, wq_ref, wk_ref, wv_ref, wo_ref, small,
    normed_ref, attended_ref, proj_ref, p_ref, cen_ref, inv_ref, tot_ref,
    acc, xs,
):
    tm = lax.axis_index("tm")
    for core, part in enumerate((x0, x1)):
        for k in range(4):
            y = ((tm >> 1) - k) & 3
            for z in range(2):
                xs[((tm & 9) ^ (8 * z + core)) | (2 * y)] = part[2 * k + z].astype(f32)
    x = xs[...].reshape(TOK, D)
    norm, _ = standard(x)
    normed = (norm * small[9:10, :]).astype(bf16)
    normed_ref[...] = normed
    for i, w_ref in enumerate((wq_ref, wk_ref, wv_ref)):
        for j in range(0, D, CHUNK):
            part = dot(normed, w_ref[:, j : j + CHUNK], 1, 0)
            proj_ref[:, i * D + j : i * D + j + CHUNK] = part.astype(bf16)
    row = lax.broadcasted_iota(jnp.int32, (TOK, TOK), 0)
    col = lax.broadcasted_iota(jnp.int32, (TOK, TOK), 1)
    lag = (col >> 2) - (row >> 2)
    allowed = (
        ((row & 3) == (col & 3))
        & (lag >= -(WINDOW // 2))
        & (lag < WINDOW - WINDOW // 2)
        & (clip_of(small, frames((TOK, TOK), 0)) == clip_of(small, frames((TOK, TOK), 1)))
    )
    acc[...] = jnp.zeros_like(acc)
    for h in range(HEADS):
        a, b = span(h)
        mask = lane_mask(h)
        p_ref[h] = dot(proj_ref[:, a:b] * mask, proj_ref[:, D + a : D + b], 1, 1) * SCALE
    for h in range(0, HEADS, GROUP):
        masked = jnp.where(allowed[None], p_ref[h : h + GROUP], -1e30)
        terms = jnp.exp(masked - jnp.max(masked, axis=2, keepdims=True))
        weights = terms / jnp.sum(terms, axis=2, keepdims=True)
        p_ref[h : h + GROUP] = weights
    for h in range(HEADS):
        a, b = span(h)
        acc[:, a:b] += dot(
            p_ref[h].astype(bf16), proj_ref[:, 2 * D + a : 2 * D + b] * lane_mask(h), 1, 0
        )
    attended = acc[...].astype(bf16)
    attended_ref[...] = attended
    mixed = xs[...].reshape(TOK, D) + dot(attended, wo_ref[...], 1, 0)
    centred, inv_std = standard(mixed)
    cen_ref[...] = centred
    inv_ref[...] = jnp.broadcast_to(inv_std, (TOK, 128))
    final = centred * small[8:9, :]
    clip = clip_of(small, frames((TOK, 1), 0))
    tot_ref[...] = jnp.zeros_like(tot_ref)
    for c in range(CLIPS):
        sums = jnp.sum(jnp.where(clip == c, final, 0.0), axis=0, keepdims=True)
        tot_ref[:, c : c + 1] = jnp.sum(small[0:REWARDS, :] * sums, axis=1, keepdims=True)


def forward(x, weights, small):
    return call(
        forward_kernel,
        (
            shape((TOK, D), bf16),
            shape((TOK, D), bf16),
            shape((TOK, 3 * D), bf16),
            shape((HEADS, TOK, TOK), f32),
            shape((TOK, D), f32),
            shape((TOK, 128), f32),
            shape((REWARDS, 8), f32),
        ),
        [VMEM] * 7,
        [pltpu.VMEM((TOK, D), f32), pltpu.VMEM((16, 8, D), f32)],
        24,
        "forward",
        flops=2_000_000_000,
        moved=14_000_000,
    )(*x, *weights, small)


def place_rows(src, dst, where, x_first):
    x, y, z, _ = where
    for k in range(64):
        first, second, kz = k // 16, k // 4 % 4, k % 4
        kx, ky = (first, second) if x_first else (second, first)
        dp = ((z + kz) & 3) * 4 + ((x + kx) & 3)
        start = dp * 72 + ((y + ky) & 3) * PIECE
        dst[PIECE * k : PIECE * (k + 1), :] = src[pl.ds(start, PIECE), :]


def turn_kernel(normed_ref, attended_ref, keep_ref, send_ref, turned, placed):
    where = position()
    core = where[3]
    turned[0] = normed_ref[...].astype(f32).T
    turned[1] = attended_ref[...].astype(f32).T
    place_rows(turned.at[0], placed, where, True)
    keep_ref[0] = placed[...].astype(bf16)
    send_ref[0] = keep_ref[0]
    place_rows(turned.at[core], placed, where, False)
    keep_ref[1] = placed[...].astype(bf16)
    place_rows(turned.at[1 - core], placed, where, False)
    send_ref[1] = placed[...].astype(bf16)


def turn(normed, attended):
    return call(
        turn_kernel,
        (shape((2, D, TOK), bf16), shape((2, D, TOK), bf16)),
        [VMEM] * 2,
        [pltpu.VMEM((2, D, TOK), f32), pltpu.VMEM((D, TOK), f32)],
        8,
        "turn",
        moved=4_000_000,
    )(normed, attended)


def backward_kernel(
    t0, t1, t2, t3, small, proj_ref, p_ref, cen_ref, inv_ref, wo_ref,
    scores_ref, keep_ref, send_ref,
    dq, dk, dv, wg, da_ref,
):
    clip_col = lax.broadcasted_iota(jnp.int32, (REWARDS, 8), 1)
    count = jnp.ones((REWARDS, 8), f32)
    for c in range(CLIPS):
        count = jnp.where(clip_col == c, small[10:11, c : c + 1] * 64.0, count)
    scores = ((t0[...] + t2[...]) + (t1[...] + t3[...])) / count
    scores = scores[:, 0:CLIPS]
    for c in range(CLIPS):
        column = jnp.where(eye(), scores[:, c : c + 1], 0.0)
        scores_ref[c : c + 1, :] = jnp.sum(column, axis=0, keepdims=True)
    residue = (scores - small[16:24, 0:CLIPS]) / ROWS
    clip = clip_of(small, frames((TOK, 1), 0))
    scaled = jnp.zeros((TOK, D), f32)
    for c in range(CLIPS):
        row = jnp.sum(small[0:REWARDS, :] * residue[:, c : c + 1], axis=0, keepdims=True)
        scaled = jnp.where(clip == c, row * small[8:9, :], scaled)
    centred = cen_ref[...]
    mixed_grad = (
        scaled
        - jnp.mean(scaled, axis=-1, keepdims=True)
        - centred * jnp.mean(scaled * centred, axis=-1, keepdims=True)
    ) * inv_ref[:, 0:1]
    mixed_grad = mixed_grad.astype(bf16)
    da_ref[...] = dot(mixed_grad, wo_ref[...], 1, 1).astype(bf16)
    dq[...] = jnp.zeros_like(dq)
    dk[...] = jnp.zeros_like(dk)
    dv[...] = jnp.zeros_like(dv)
    for h in range(HEADS):
        a, b = span(h)
        mask = lane_mask(h)
        wg[h] = dot(da_ref[:, a:b] * mask, proj_ref[:, 2 * D + a : 2 * D + b], 1, 1)
    for h in range(0, HEADS, GROUP):
        weights = p_ref[h : h + GROUP]
        weight_grad = wg[h : h + GROUP]
        inner = jnp.sum(weights * weight_grad, axis=2, keepdims=True)
        wg[h : h + GROUP] = weights * (weight_grad - inner)
    for h in range(HEADS):
        a, b = span(h)
        mask = lane_mask(h)
        logit_grad = wg[h].astype(bf16)
        dq[:, a:b] += dot(logit_grad, proj_ref[:, D + a : D + b] * mask, 1, 0)
        dk[:, a:b] += dot(logit_grad, proj_ref[:, a:b] * mask, 0, 0)
        dv[:, a:b] += dot(p_ref[h].astype(bf16), da_ref[:, a:b] * mask, 0, 0)

    def store(ref_qk, ref_vo):
        ref_qk[0] = (dq[...] * SCALE).astype(bf16)
        ref_qk[1] = (dk[...] * SCALE).astype(bf16)
        ref_vo[0] = dv[...].astype(bf16)
        ref_vo[1] = mixed_grad

    core = position()[3]

    @pl.when(core == 0)
    def _():
        store(keep_ref, send_ref)

    @pl.when(core != 0)
    def _():
        store(send_ref, keep_ref)


def backward(totals, small, proj, p, centred, inv, w_out):
    return call(
        backward_kernel,
        (
            shape((CLIPS, REWARDS), f32),
            shape((2, TOK, D), bf16),
            shape((2, TOK, D), bf16),
        ),
        [VMEM] * 10,
        [pltpu.VMEM((TOK, D), f32)] * 3
        + [
            pltpu.VMEM((HEADS, TOK, TOK), f32),
            pltpu.VMEM((TOK, D), bf16),
        ],
        16,
        "backward",
        flops=1_500_000_000,
        moved=8_000_000,
    )(*totals, small, proj, p, centred, inv, w_out)


PARTS = ((2, 0), (2, 1), (1, 1), (3, 0), (1, 0), (3, 1))


def gradient_kernel(lk, lr, rk, rr, *outs):
    for i in range(2):
        right = jnp.concatenate([rk[i], rr[i]], axis=0)
        for k in (2, 1, 3, 0):
            rows = slice(288 * k, 288 * (k + 1))
            left = jnp.concatenate([lk[i, rows], lr[i, rows]], axis=1)
            part = dot(left, right, 1, 0).astype(bf16)
            if k == 0:
                outs[7 * i + 6][...] = part
            else:
                for j, (distance, piece) in enumerate(PARTS):
                    if distance == k:
                        outs[7 * i + j][...] = part[144 * piece : 144 * (piece + 1)]


def gradient(left_keep, left_recv, right_keep, right_recv):
    parts = call(
        gradient_kernel,
        ((shape((144, D), bf16),) * 6 + (shape((288, D), bf16),)) * 2,
        [VMEM] * 4,
        [],
        16,
        "gradient",
        flops=1_400_000_000,
        moved=8_000_000,
    )(left_keep, left_recv, right_keep, right_recv)
    return parts[:7], parts[7:]


def relay_kernel(*refs):
    for k in range(4):
        refs[8 + k][...] = (refs[k][...].astype(f32) + refs[4 + k][...].astype(f32)).astype(bf16)


def relay(arrived, own):
    return call(
        relay_kernel,
        (shape((144, D), bf16),) * 4,
        [VMEM] * 8,
        [],
        8,
        "relay",
        moved=4_000_000,
    )(*arrived, *own)


def total(refs):
    result = refs[0][...].astype(f32)
    for ref in refs[1:]:
        result += ref[...].astype(f32)
    return result


SLOT = ((0, 3, 6, 5), (1, 2, 7, 4))


def first_sum_kernel(*refs):
    for i in range(2):
        plain_on, plain_back, relayed_on, relayed_back, own = (refs[2 * j + i] for j in range(5))
        result = own[...].astype(f32) + jnp.concatenate(
            [
                plain_back[...].astype(f32) + relayed_on[...].astype(f32),
                plain_on[...].astype(f32) + relayed_back[...].astype(f32),
            ],
            axis=0,
        )
        for k in range(4):
            refs[10 + SLOT[1 - i][k]][...] = result[72 * k : 72 * (k + 1)].astype(bf16)


def first_sum(parts):
    return call(
        first_sum_kernel,
        (shape((72, D), bf16),) * 8,
        [VMEM] * 10,
        [],
        12,
        "first_sum",
        moved=6_000_000,
    )(*parts)


def second_sum_kernel(*refs):
    sums = [total([refs[SLOT[i][k]] for k in range(4)]) for i in (1, 0)]
    rest = jnp.zeros((4, D), f32)
    for k in range(4):
        rows = slice(PIECE * k, PIECE * (k + 1))
        refs[8 + k][...] = jnp.concatenate([sums[0][rows], sums[1][rows], rest], axis=0).astype(
            bf16
        )


def second_sum(parts):
    return call(
        second_sum_kernel,
        (shape((40, D), bf16),) * 4,
        [VMEM] * 8,
        [],
        6,
        "second_sum",
        moved=1_700_000,
    )(*parts)


def sum_kernel(*refs):
    refs[-1][...] = total(refs[:-1]).astype(bf16)


def pair_sum_kernel(a, b, *rest):
    out = rest[-1]
    out[...] = a[...] + b[...]


def pair_sum(a, b, *after):
    specs = [VMEM] * 2 + [ANY] * len(after)
    return call(
        pair_sum_kernel, shape((REWARDS, 8), f32), specs, [], 1, "pair_sum", moved=20_000
    )(a, b, *after)


def plain_sum(parts):
    return call(
        sum_kernel,
        shape(parts[0].shape, bf16),
        [VMEM] * len(parts),
        [],
        3,
        "plain_sum",
        moved=500_000,
    )(*parts)


def stack_kernel(*refs):
    for k in range(4):
        refs[4][k] = refs[k][...]


def stack(parts):
    return call(
        stack_kernel, shape((4, 40, D), bf16), [VMEM] * 4, [], 3, "stack", moved=800_000
    )(*parts)


def last_kernel(mine, other, qkv_ref, out_ref, held):
    _, y_here, _, core = position()
    for k in range(4):
        y = (y_here - k) & 3
        held[core, y] = mine[k].astype(f32)
        held[1 - core, y] = other[k].astype(f32)
    for y in range(4):
        rows = slice(PIECE * y, PIECE * (y + 1))
        qkv_ref[rows, 0:D] = held[0, y, 0:PIECE]
        qkv_ref[rows, D : 2 * D] = held[0, y, PIECE : 2 * PIECE]
        qkv_ref[rows, 2 * D : 3 * D] = held[1, y, 0:PIECE]
        out_ref[rows, :] = held[1, y, PIECE : 2 * PIECE]


def last(mine, other):
    return call(
        last_kernel,
        (shape((72, 3 * D), f32), shape((72, D), f32)),
        [VMEM] * 2,
        [pltpu.VMEM((2, 4, 40, D), f32)],
        10,
        "last",
        moved=2_000_000,
    )(mine, other)


def to_core(block):
    return lax.ppermute(block, "tm", [(i, i ^ 1) for i in range(16)])


def to_far(block):
    return lax.ppermute(block, "tm", [(i, i ^ 8) for i in range(16)])


def along_y(block, k):
    return lax.ppermute(block, "tm", [(i, i & 9 | (i + 2 * k) & 6) for i in range(16)])


def along_x(block, k):
    return lax.ppermute(block, "dp", [(i, i & 12 | (i + k) & 3) for i in range(16)])


def around_z(block, k):
    route = []
    for tm in range(16):
        for dp in range(16):
            step = {1: 1, 3: -1, 2: -2 if tm & 1 else 2}[k]
            z = ((tm >> 3) * 4 + (dp >> 2) + step) & 7
            there = (tm & 7 | (z >> 2) << 3) * 16 + ((z & 3) << 2 | dp & 3)
            route.append((tm * 16 + dp, there))
    return lax.ppermute(block, ("tm", "dp"), route)


def exchange(slots):
    moved = list(slots)
    for k in (1, 3, 2):
        moved[SLOT[1][k]] = along_y(slots[SLOT[1][k]], k)
        moved[SLOT[0][k]] = along_x(slots[SLOT[0][k]], k)
    return moved


def around(x_half, y_half):
    on, back = (along_x, along_y), 3
    halves = (x_half, y_half)
    arrived = [on[i](halves[i][j], 1 if j == 0 else back) for j in range(2) for i in range(2)]
    plain = [on[i](halves[i][2 + j], 1 if j == 0 else back) for j in range(2) for i in range(2)]
    own = [halves[i][4 + j] for j in range(2) for i in range(2)]
    sums = relay(arrived, own)
    relayed = [on[i](sums[2 * j + i], 1 if j == 0 else back) for j in range(2) for i in range(2)]
    return first_sum(plain + relayed + [x_half[6], y_half[6]])


def on_device(tokens, clip_frames, teacher_scores, ln_gain, w_qkv, w_out, out_gain, reward_head):
    tokens = tokens.reshape(2, 2, 4, 8, D)
    send = lax.dynamic_index_in_dim(tokens, 1 - (lax.axis_index("tm") >> 3), 1, keepdims=False)
    small = pack(clip_frames, teacher_scores[0], ln_gain, out_gain, reward_head.T)
    wq, wk, loaded = load([(w_qkv, 0), (w_qkv, D)], send, 44)
    parts = deal(tokens, to_far(send), small, loaded)
    wv, wo, loaded = load([(w_qkv, 2 * D), (w_out, None)], parts[0], 42)
    weights = wq, wk, wv, wo
    keep, send = split([parts[0]] + [along_y(parts[k], k) for k in (1, 2, 3)], loaded)
    x = [keep, to_core(send)]
    normed, attended, proj, p, centred, inv, partial = forward(x, weights, small)
    partial = pair_sum(partial, to_core(partial))
    normed, attended, _ = lax.optimization_barrier((normed, attended, partial))
    left_keep, left_send = turn(normed, attended)
    left_recv = to_core(left_send)
    partial = pair_sum(partial, to_far(partial), left_keep)
    totals = [partial] + [along_y(partial, k) for k in (1, 2, 3)]
    scores, right_keep, right_send = backward(totals, small, proj, p, centred, inv, weights[3])
    parts = gradient(left_keep, left_recv, right_keep, to_core(right_send))
    parts = second_sum(exchange(around(*parts)))
    part = plain_sum([parts[0]] + [around_z(parts[k], k) for k in (1, 2, 3)])
    part = plain_sum([part, to_far(part)])
    mine = stack([part] + [along_y(part, k) for k in (1, 2, 3)])
    qkv_total, out_total = last(mine, to_core(mine))
    return (scores[None], qkv_total, out_total)


def solution(mesh):
    return jax.shard_map(
        on_device,
        mesh=mesh,
        in_specs=(
            P("dp", "tm", None, None),
            P("dp", None),
            P("dp", None, None),
            P(),
            P(),
            P(),
            P(),
            P(),
        ),
        out_specs=(P("dp", None, None), P("dp", None), P("dp", None)),
        check_vma=False,
    )
```

```python
import math

import jax
import jax.numpy as jnp
from jax import lax
from jax.experimental import pallas as pl
from jax.experimental.pallas import tpu as pltpu
from jax.sharding import PartitionSpec as P

HEADS = 16
HEAD_DIM = 72
WINDOW = 8
D = 1152
TOK = 128
CLIPS = 4
REWARDS = 8
ROWS = 16
CHUNK = 384
PIECE = 18
GROUP = 4
EPS = 1e-06
SCALE = 1.0 / math.sqrt(HEAD_DIM)

f32 = jnp.float32
bf16 = jnp.bfloat16
HI = lax.Precision.HIGHEST
VMEM = pl.BlockSpec(memory_space=pltpu.VMEM)
ANY = pl.BlockSpec(memory_space=pl.ANY)


def dot(a, b, ca, cb, precision=None):
    return lax.dot_general(
        a, b, (((ca,), (cb,)), ((), ())), preferred_element_type=f32, precision=precision
    )


def clip_of(small, frame):
    end, clip = small[10:11, 0:1], jnp.zeros_like(frame)
    for c in range(CLIPS):
        clip += (frame >= end).astype(f32)
        if c + 1 < CLIPS:
            end = end + small[10:11, c + 1 : c + 2]
    return clip


def frames(dims, axis):
    return (lax.broadcasted_iota(jnp.int32, dims, axis) >> 2).astype(f32)


def span(h):
    low = HEAD_DIM * h
    return low // 128 * 128, -(-(low + HEAD_DIM) // 128) * 128


def lane_mask(h):
    start, end = span(h)
    lane = lax.broadcasted_iota(jnp.int32, (1, end - start), 1) + (start - HEAD_DIM * h)
    return ((lane >= 0) & (lane < HEAD_DIM)).astype(f32).astype(bf16)


def standard(values):
    centre = values - jnp.mean(values, axis=-1, keepdims=True)
    inv_std = lax.rsqrt(jnp.mean(centre * centre, axis=-1, keepdims=True) + EPS)
    return centre * inv_std, inv_std


def position():
    tm, dp = lax.axis_index("tm"), lax.axis_index("dp")
    return dp & 3, (tm >> 1) & 3, dp >> 2, tm & 1


def shape(dims, kind):
    return jax.ShapeDtypeStruct(dims, kind)


def call(kernel, out_shape, in_specs, scratch, mib, name, flops=0, moved=0):
    return pl.pallas_call(
        kernel,
        out_shape=out_shape,
        in_specs=in_specs,
        out_specs=jax.tree.map(lambda _: VMEM, out_shape),
        scratch_shapes=scratch,
        compiler_params=pltpu.CompilerParams(vmem_limit_bytes=mib << 20),
        cost_estimate=pl.CostEstimate(flops=flops, bytes_accessed=moved, transcendentals=0),
        name=name,
    )


def deal_kernel(x_ref, far_ref, small, loaded, *outs):
    _, y, _, _ = position()
    z = lax.axis_index("tm") >> 3
    for k in range(4):
        for a in range(2):
            outs[k][a] = x_ref[a, z, (y + k) & 3]
            outs[k][2 + a] = far_ref[a, (y + k) & 3]


def deal(tokens, far, small, loaded):
    return call(
        deal_kernel,
        (shape((4, 8, D), bf16),) * 4,
        [VMEM] * 4,
        [],
        4,
        "deal",
        moved=600_000,
    )(tokens, far, small, loaded)


def pack_kernel(lens_ref, teacher_ref, ln_ref, og_ref, rh_ref, small):
    small[...] = jnp.zeros_like(small)
    small[0:REWARDS] = rh_ref[...]
    small[8] = og_ref[...]
    small[9] = ln_ref[...]
    small[10:11, 0:CLIPS] = lens_ref[...].astype(f32)
    for c in range(CLIPS):
        small[16 : 16 + REWARDS, c : c + 1] = upright(teacher_ref[c : c + 1])


def upright(row):
    return jnp.sum(jnp.where(eye(), row, 0.0), axis=1, keepdims=True)


def eye():
    side = (REWARDS, REWARDS)
    return lax.broadcasted_iota(jnp.int32, side, 0) == lax.broadcasted_iota(jnp.int32, side, 1)


def pack(clip_frames, teacher, ln_gain, out_gain, reward):
    return call(
        pack_kernel, shape((24, D), f32), [VMEM] * 5, [], 2, "pack", moved=200_000
    )(clip_frames, teacher, ln_gain, out_gain, reward)


def split_kernel(loaded, r0, r2, r1, r3, keep_ref, send_ref):
    core = position()[3]
    for k in range(4):
        for z in range(2):
            rows = [(r0, r1, r2, r3)[k][2 * z + a].astype(f32) for a in range(2)]
            low = jnp.concatenate([r[0:4] for r in rows], axis=0)
            high = jnp.concatenate([r[4:8] for r in rows], axis=0)
            keep_ref[2 * k + z] = jnp.where(core == 0, low, high).astype(bf16)
            send_ref[2 * k + z] = jnp.where(core == 0, high, low).astype(bf16)


def split(parts, loaded):
    return call(
        split_kernel,
        (shape((8, 8, D), bf16),) * 2,
        [VMEM] * 5,
        [],
        4,
        "split",
        moved=600_000,
    )(loaded, *parts)


def load(sources, after, mib):
    def kernel(*refs):
        count = len(sources)
        ins, outs, sems = refs[:count], refs[count + 1 : -1], refs[-1]
        copies = []
        for k, (_, column) in enumerate(sources):
            source = ins[k] if column is None else ins[k].at[:, pl.ds(column, D)]
            copies.append(pltpu.make_async_copy(source, outs[k], sems.at[k]))
        for copy in copies:
            copy.start()
        outs[count][...] = jnp.zeros_like(outs[count])
        for copy in copies:
            copy.wait()

    return call(
        kernel,
        (shape((D, D), bf16),) * len(sources) + (shape((8, 128), f32),),
        [ANY] * (len(sources) + 1),
        [pltpu.SemaphoreType.DMA((len(sources),))],
        mib,
        "load",
        moved=10_000_000,
    )(*[array for array, _ in sources], after)


def forward_kernel(
    x0, x1, wq_ref, wk_ref, wv_ref, wo_ref, small,
    normed_ref, attended_ref, proj_ref, p_ref, cen_ref, inv_ref, tot_ref,
    acc, xs,
):
    tm = lax.axis_index("tm")
    for core, part in enumerate((x0, x1)):
        for k in range(4):
            y = ((tm >> 1) - k) & 3
            for z in range(2):
                xs[((tm & 9) ^ (8 * z + core)) | (2 * y)] = part[2 * k + z].astype(f32)
    x = xs[...].reshape(TOK, D)
    norm, _ = standard(x)
    normed = (norm * small[9:10, :]).astype(bf16)
    normed_ref[...] = normed
    for i, w_ref in enumerate((wq_ref, wk_ref, wv_ref)):
        for j in range(0, D, CHUNK):
            part = dot(normed, w_ref[:, j : j + CHUNK], 1, 0)
            proj_ref[:, i * D + j : i * D + j + CHUNK] = part.astype(bf16)
    row = lax.broadcasted_iota(jnp.int32, (TOK, TOK), 0)
    col = lax.broadcasted_iota(jnp.int32, (TOK, TOK), 1)
    lag = (col >> 2) - (row >> 2)
    allowed = (
        ((row & 3) == (col & 3))
        & (lag >= -(WINDOW // 2))
        & (lag < WINDOW - WINDOW // 2)
        & (clip_of(small, frames((TOK, TOK), 0)) == clip_of(small, frames((TOK, TOK), 1)))
    )
    acc[...] = jnp.zeros_like(acc)
    for h in range(HEADS):
        a, b = span(h)
        mask = lane_mask(h)
        p_ref[h] = dot(proj_ref[:, a:b] * mask, proj_ref[:, D + a : D + b], 1, 1) * SCALE
    for h in range(0, HEADS, GROUP):
        masked = jnp.where(allowed[None], p_ref[h : h + GROUP], -1e30)
        terms = jnp.exp(masked - jnp.max(masked, axis=2, keepdims=True))
        weights = terms / jnp.sum(terms, axis=2, keepdims=True)
        p_ref[h : h + GROUP] = weights
    for h in range(HEADS):
        a, b = span(h)
        acc[:, a:b] += dot(
            p_ref[h].astype(bf16), proj_ref[:, 2 * D + a : 2 * D + b] * lane_mask(h), 1, 0
        )
    attended = acc[...].astype(bf16)
    attended_ref[...] = attended
    mixed = xs[...].reshape(TOK, D) + dot(attended, wo_ref[...], 1, 0)
    centred, inv_std = standard(mixed)
    cen_ref[...] = centred
    inv_ref[...] = jnp.broadcast_to(inv_std, (TOK, 128))
    final = centred * small[8:9, :]
    clip = clip_of(small, frames((TOK, 1), 0))
    tot_ref[...] = jnp.zeros_like(tot_ref)
    for c in range(CLIPS):
        sums = jnp.sum(jnp.where(clip == c, final, 0.0), axis=0, keepdims=True)
        tot_ref[:, c : c + 1] = jnp.sum(small[0:REWARDS, :] * sums, axis=1, keepdims=True)


def forward(x, weights, small):
    return call(
        forward_kernel,
        (
            shape((TOK, D), bf16),
            shape((TOK, D), bf16),
            shape((TOK, 3 * D), bf16),
            shape((HEADS, TOK, TOK), f32),
            shape((TOK, D), f32),
            shape((TOK, 128), f32),
            shape((REWARDS, 8), f32),
        ),
        [VMEM] * 7,
        [pltpu.VMEM((TOK, D), f32), pltpu.VMEM((16, 8, D), f32)],
        24,
        "forward",
        flops=2_000_000_000,
        moved=14_000_000,
    )(*x, *weights, small)


def place_rows(src, dst, where, x_first):
    x, y, z, _ = where
    for k in range(64):
        first, second, kz = k // 16, k // 4 % 4, k % 4
        kx, ky = (first, second) if x_first else (second, first)
        dp = ((z + kz) & 3) * 4 + ((x + kx) & 3)
        start = dp * 72 + ((y + ky) & 3) * PIECE
        dst[PIECE * k : PIECE * (k + 1), :] = src[pl.ds(start, PIECE), :]


def turn_kernel(normed_ref, attended_ref, keep_ref, send_ref, turned, placed):
    where = position()
    core = where[3]
    turned[0] = normed_ref[...].astype(f32).T
    turned[1] = attended_ref[...].astype(f32).T
    place_rows(turned.at[0], placed, where, True)
    keep_ref[0] = placed[...].astype(bf16)
    send_ref[0] = keep_ref[0]
    place_rows(turned.at[core], placed, where, False)
    keep_ref[1] = placed[...].astype(bf16)
    place_rows(turned.at[1 - core], placed, where, False)
    send_ref[1] = placed[...].astype(bf16)


def turn(normed, attended):
    return call(
        turn_kernel,
        (shape((2, D, TOK), bf16), shape((2, D, TOK), bf16)),
        [VMEM] * 2,
        [pltpu.VMEM((2, D, TOK), f32), pltpu.VMEM((D, TOK), f32)],
        8,
        "turn",
        moved=4_000_000,
    )(normed, attended)


def backward_kernel(
    t0, t1, t3, t2, small, proj_ref, p_ref, cen_ref, inv_ref, wo_ref,
    scores_ref, keep_ref, send_ref,
    dq, dk, dv, wg, da_ref,
):
    clip_col = lax.broadcasted_iota(jnp.int32, (REWARDS, 8), 1)
    count = jnp.ones((REWARDS, 8), f32)
    for c in range(CLIPS):
        count = jnp.where(clip_col == c, small[10:11, c : c + 1] * 64.0, count)
    scores = ((t0[...] + t2[...]) + (t1[...] + t3[...])) / count
    scores = scores[:, 0:CLIPS]
    for c in range(CLIPS):
        column = jnp.where(eye(), scores[:, c : c + 1], 0.0)
        scores_ref[c : c + 1, :] = jnp.sum(column, axis=0, keepdims=True)
    residue = (scores - small[16:24, 0:CLIPS]) / ROWS
    clip = clip_of(small, frames((TOK, 1), 0))
    scaled = jnp.zeros((TOK, D), f32)
    for c in range(CLIPS):
        row = jnp.sum(small[0:REWARDS, :] * residue[:, c : c + 1], axis=0, keepdims=True)
        scaled = jnp.where(clip == c, row * small[8:9, :], scaled)
    centred = cen_ref[...]
    mixed_grad = (
        scaled
        - jnp.mean(scaled, axis=-1, keepdims=True)
        - centred * jnp.mean(scaled * centred, axis=-1, keepdims=True)
    ) * inv_ref[:, 0:1]
    mixed_grad = mixed_grad.astype(bf16)
    da_ref[...] = dot(mixed_grad, wo_ref[...], 1, 1).astype(bf16)
    dq[...] = jnp.zeros_like(dq)
    dk[...] = jnp.zeros_like(dk)
    dv[...] = jnp.zeros_like(dv)
    for h in range(HEADS):
        a, b = span(h)
        mask = lane_mask(h)
        wg[h] = dot(da_ref[:, a:b] * mask, proj_ref[:, 2 * D + a : 2 * D + b], 1, 1)
    for h in range(0, HEADS, GROUP):
        weights = p_ref[h : h + GROUP]
        weight_grad = wg[h : h + GROUP]
        inner = jnp.sum(weights * weight_grad, axis=2, keepdims=True)
        wg[h : h + GROUP] = weights * (weight_grad - inner)
    for h in range(HEADS):
        a, b = span(h)
        mask = lane_mask(h)
        logit_grad = wg[h].astype(bf16)
        dq[:, a:b] += dot(logit_grad, proj_ref[:, D + a : D + b] * mask, 1, 0)
        dk[:, a:b] += dot(logit_grad, proj_ref[:, a:b] * mask, 0, 0)
        dv[:, a:b] += dot(p_ref[h].astype(bf16), da_ref[:, a:b] * mask, 0, 0)

    def store(ref_qk, ref_vo):
        ref_qk[0] = (dq[...] * SCALE).astype(bf16)
        ref_qk[1] = (dk[...] * SCALE).astype(bf16)
        ref_vo[0] = dv[...].astype(bf16)
        ref_vo[1] = mixed_grad

    core = position()[3]

    @pl.when(core == 0)
    def _():
        store(keep_ref, send_ref)

    @pl.when(core != 0)
    def _():
        store(send_ref, keep_ref)


def backward(totals, small, proj, p, centred, inv, w_out):
    return call(
        backward_kernel,
        (
            shape((CLIPS, REWARDS), f32),
            shape((2, TOK, D), bf16),
            shape((2, TOK, D), bf16),
        ),
        [VMEM] * 10,
        [pltpu.VMEM((TOK, D), f32)] * 3
        + [
            pltpu.VMEM((HEADS, TOK, TOK), f32),
            pltpu.VMEM((TOK, D), bf16),
        ],
        16,
        "backward",
        flops=1_500_000_000,
        moved=8_000_000,
    )(*totals, small, proj, p, centred, inv, w_out)


PARTS = ((2, 0), (2, 1), (1, 1), (3, 0), (1, 0), (3, 1))


def gradient_kernel(lk, lr, rk, rr, *outs):
    for i in range(2):
        right = jnp.concatenate([rk[i], rr[i]], axis=0)
        for k in (2, 1, 3, 0):
            rows = slice(288 * k, 288 * (k + 1))
            left = jnp.concatenate([lk[i, rows], lr[i, rows]], axis=1)
            part = dot(left, right, 1, 0).astype(bf16)
            if k == 0:
                outs[7 * i + 6][...] = part
            else:
                for j, (distance, piece) in enumerate(PARTS):
                    if distance == k:
                        outs[7 * i + j][...] = part[144 * piece : 144 * (piece + 1)]


def gradient(left_keep, left_recv, right_keep, right_recv):
    parts = call(
        gradient_kernel,
        ((shape((144, D), bf16),) * 6 + (shape((288, D), bf16),)) * 2,
        [VMEM] * 4,
        [],
        16,
        "gradient",
        flops=1_400_000_000,
        moved=8_000_000,
    )(left_keep, left_recv, right_keep, right_recv)
    return parts[:7], parts[7:]


def relay_kernel(*refs):
    for k in range(4):
        refs[8 + k][...] = (refs[k][...].astype(f32) + refs[4 + k][...].astype(f32)).astype(bf16)


def relay(arrived, own):
    return call(
        relay_kernel,
        (shape((144, D), bf16),) * 4,
        [VMEM] * 8,
        [],
        8,
        "relay",
        moved=4_000_000,
    )(*arrived, *own)


def total(refs):
    result = refs[0][...].astype(f32)
    for ref in refs[1:]:
        result += ref[...].astype(f32)
    return result


SLOT = ((0, 5, 3, 7), (1, 4, 2, 6))


def first_sum_kernel(*refs):
    for i in range(2):
        plain_on, plain_back, relayed_on, relayed_back, own = (refs[2 * j + i] for j in range(5))
        result = own[...].astype(f32) + jnp.concatenate(
            [
                plain_back[...].astype(f32) + relayed_on[...].astype(f32),
                plain_on[...].astype(f32) + relayed_back[...].astype(f32),
            ],
            axis=0,
        )
        for k in range(4):
            refs[10 + SLOT[1 - i][k]][...] = result[72 * k : 72 * (k + 1)].astype(bf16)


def first_sum(parts):
    return call(
        first_sum_kernel,
        (shape((72, D), bf16),) * 8,
        [VMEM] * 10,
        [],
        12,
        "first_sum",
        moved=6_000_000,
    )(*parts)


def second_sum_kernel(*refs):
    sums = [total([refs[SLOT[i][k]] for k in range(4)]) for i in (1, 0)]
    rest = jnp.zeros((4, D), f32)
    for k in range(4):
        rows = slice(PIECE * k, PIECE * (k + 1))
        refs[8 + k][...] = jnp.concatenate([sums[0][rows], sums[1][rows], rest], axis=0).astype(
            bf16
        )


def second_sum(parts):
    return call(
        second_sum_kernel,
        (shape((40, D), bf16),) * 4,
        [VMEM] * 8,
        [],
        6,
        "second_sum",
        moved=1_700_000,
    )(*parts)


def sum_kernel(*refs):
    refs[-1][...] = total(refs[:-1]).astype(bf16)


def pair_sum_kernel(a, b, *rest):
    out = rest[-1]
    out[...] = a[...] + b[...]


def pair_sum(a, b, *after):
    specs = [VMEM] * 2 + [ANY] * len(after)
    return call(
        pair_sum_kernel, shape((REWARDS, 8), f32), specs, [], 1, "pair_sum", moved=20_000
    )(a, b, *after)


def plain_sum(parts):
    return call(
        sum_kernel,
        shape(parts[0].shape, bf16),
        [VMEM] * len(parts),
        [],
        3,
        "plain_sum",
        moved=500_000,
    )(*parts)


def stack_kernel(*refs):
    for j, k in enumerate((0, 1, 3, 2)):
        refs[4][k] = refs[j][...]


def stack(parts):
    return call(
        stack_kernel, shape((4, 40, D), bf16), [VMEM] * 4, [], 3, "stack", moved=800_000
    )(*parts)


def last_kernel(mine, other, qkv_ref, out_ref, held):
    _, y_here, _, core = position()
    for k in range(4):
        y = (y_here - k) & 3
        held[core, y] = mine[k].astype(f32)
        held[1 - core, y] = other[k].astype(f32)
    for y in range(4):
        rows = slice(PIECE * y, PIECE * (y + 1))
        qkv_ref[rows, 0:D] = held[0, y, 0:PIECE]
        qkv_ref[rows, D : 2 * D] = held[0, y, PIECE : 2 * PIECE]
        qkv_ref[rows, 2 * D : 3 * D] = held[1, y, 0:PIECE]
        out_ref[rows, :] = held[1, y, PIECE : 2 * PIECE]


def last(mine, other):
    return call(
        last_kernel,
        (shape((72, 3 * D), f32), shape((72, D), f32)),
        [VMEM] * 2,
        [pltpu.VMEM((2, 4, 40, D), f32)],
        10,
        "last",
        moved=2_000_000,
    )(mine, other)


def to_core(block):
    return lax.ppermute(block, "tm", [(i, i ^ 1) for i in range(16)])


def to_far(block):
    return lax.ppermute(block, "tm", [(i, i ^ 8) for i in range(16)])


def along_y(block, k):
    return lax.ppermute(block, "tm", [(i, i & 9 | (i + 2 * k) & 6) for i in range(16)])


def along_x(block, k):
    return lax.ppermute(block, "dp", [(i, i & 12 | (i + k) & 3) for i in range(16)])


def around_z(block, k):
    route = []
    for tm in range(16):
        for dp in range(16):
            step = {1: 1, 3: -1, 2: -2 if tm & 1 else 2}[k]
            z = ((tm >> 3) * 4 + (dp >> 2) + step) & 7
            there = (tm & 7 | (z >> 2) << 3) * 16 + ((z & 3) << 2 | dp & 3)
            route.append((tm * 16 + dp, there))
    return lax.ppermute(block, ("tm", "dp"), route)


def exchange(slots):
    moved = list(slots)
    for k in (2, 1, 3):
        moved[SLOT[1][k]] = along_y(slots[SLOT[1][k]], k)
        moved[SLOT[0][k]] = along_x(slots[SLOT[0][k]], k)
    return moved


def around(x_half, y_half):
    on, back = (along_x, along_y), 3
    halves = (x_half, y_half)
    arrived = [on[i](halves[i][j], 1 if j == 0 else back) for j in range(2) for i in range(2)]
    plain = [on[i](halves[i][2 + j], 1 if j == 0 else back) for j in range(2) for i in range(2)]
    own = [halves[i][4 + j] for j in range(2) for i in range(2)]
    sums = relay(arrived, own)
    relayed = [on[i](sums[2 * j + i], 1 if j == 0 else back) for j in range(2) for i in range(2)]
    return first_sum(plain + relayed + [x_half[6], y_half[6]])


def on_device(tokens, clip_frames, teacher_scores, ln_gain, w_qkv, w_out, out_gain, reward_head):
    tokens = tokens.reshape(2, 2, 4, 8, D)
    send = lax.dynamic_index_in_dim(tokens, 1 - (lax.axis_index("tm") >> 3), 1, keepdims=False)
    small = pack(clip_frames, teacher_scores[0], ln_gain, out_gain, reward_head.T)
    wq, wk, loaded = load([(w_qkv, 0), (w_qkv, D)], send, 44)
    parts = deal(tokens, to_far(send), small, loaded)
    wv, wo, loaded = load([(w_qkv, 2 * D), (w_out, None)], parts[0], 42)
    weights = wq, wk, wv, wo
    keep, send = split([parts[0]] + [along_y(parts[k], k) for k in (2, 1, 3)], loaded)
    x = [keep, to_core(send)]
    normed, attended, proj, p, centred, inv, partial = forward(x, weights, small)
    partial = pair_sum(partial, to_core(partial))
    normed, attended, _ = lax.optimization_barrier((normed, attended, partial))
    left_keep, left_send = turn(normed, attended)
    left_recv = to_core(left_send)
    partial = pair_sum(partial, to_far(partial), left_keep)
    totals = [partial] + [along_y(partial, k) for k in (1, 3, 2)]
    scores, right_keep, right_send = backward(totals, small, proj, p, centred, inv, weights[3])
    parts = gradient(left_keep, left_recv, right_keep, to_core(right_send))
    parts = second_sum(exchange(around(*parts)))
    part = plain_sum([parts[0]] + [around_z(parts[k], k) for k in (2, 1, 3)])
    part = plain_sum([part, to_far(part)])
    mine = stack([part] + [along_y(part, k) for k in (1, 3, 2)])
    qkv_total, out_total = last(mine, to_core(mine))
    return (scores[None], qkv_total, out_total)


def solution(mesh):
    return jax.shard_map(
        on_device,
        mesh=mesh,
        in_specs=(
            P("dp", "tm", None, None),
            P("dp", None),
            P("dp", None, None),
            P(),
            P(),
            P(),
            P(),
            P(),
        ),
        out_specs=(P("dp", None, None), P("dp", None), P("dp", None)),
        check_vma=False,
    )
```

```python
import math

import jax
import jax.numpy as jnp
from jax import lax
from jax.experimental import pallas as pl
from jax.experimental.pallas import tpu as pltpu
from jax.sharding import PartitionSpec as P

HEADS = 16
HEAD_DIM = 72
WINDOW = 8
D = 1152
TOK = 128
CLIPS = 4
REWARDS = 8
ROWS = 16
CHUNK = 384
PIECE = 18
GROUP = 4
EPS = 1e-06
SCALE = 1.0 / math.sqrt(HEAD_DIM)

f32 = jnp.float32
bf16 = jnp.bfloat16
HI = lax.Precision.HIGHEST
VMEM = pl.BlockSpec(memory_space=pltpu.VMEM)
ANY = pl.BlockSpec(memory_space=pl.ANY)


def dot(a, b, ca, cb, precision=None):
    return lax.dot_general(
        a, b, (((ca,), (cb,)), ((), ())), preferred_element_type=f32, precision=precision
    )


def clip_of(small, frame):
    end, clip = small[10:11, 0:1], jnp.zeros_like(frame)
    for c in range(CLIPS):
        clip += (frame >= end).astype(f32)
        if c + 1 < CLIPS:
            end = end + small[10:11, c + 1 : c + 2]
    return clip


def frames(dims, axis):
    return (lax.broadcasted_iota(jnp.int32, dims, axis) >> 2).astype(f32)


def span(h):
    low = HEAD_DIM * h
    return low // 128 * 128, -(-(low + HEAD_DIM) // 128) * 128


def lane_mask(h):
    start, end = span(h)
    lane = lax.broadcasted_iota(jnp.int32, (1, end - start), 1) + (start - HEAD_DIM * h)
    return ((lane >= 0) & (lane < HEAD_DIM)).astype(f32).astype(bf16)


def standard(values):
    centre = values - jnp.mean(values, axis=-1, keepdims=True)
    inv_std = lax.rsqrt(jnp.mean(centre * centre, axis=-1, keepdims=True) + EPS)
    return centre * inv_std, inv_std


def position():
    tm, dp = lax.axis_index("tm"), lax.axis_index("dp")
    return dp & 3, (tm >> 1) & 3, dp >> 2, tm & 1


def shape(dims, kind):
    return jax.ShapeDtypeStruct(dims, kind)


def call(kernel, out_shape, in_specs, scratch, mib, name, flops=0, moved=0):
    return pl.pallas_call(
        kernel,
        out_shape=out_shape,
        in_specs=in_specs,
        out_specs=jax.tree.map(lambda _: VMEM, out_shape),
        scratch_shapes=scratch,
        compiler_params=pltpu.CompilerParams(vmem_limit_bytes=mib << 20),
        cost_estimate=pl.CostEstimate(flops=flops, bytes_accessed=moved, transcendentals=0),
        name=name,
    )


def deal_kernel(x_ref, far_ref, small, loaded, *outs):
    _, y, _, _ = position()
    z = lax.axis_index("tm") >> 3
    for k in range(4):
        for a in range(2):
            outs[k][a] = x_ref[a, z, (y + k) & 3]
            outs[k][2 + a] = far_ref[a, (y + k) & 3]


def deal(tokens, far, small, loaded):
    return call(
        deal_kernel,
        (shape((4, 8, D), bf16),) * 4,
        [VMEM] * 4,
        [],
        4,
        "deal",
        moved=600_000,
    )(tokens, far, small, loaded)


def pack_kernel(lens_ref, teacher_ref, ln_ref, og_ref, rh_ref, small):
    small[...] = jnp.zeros_like(small)
    small[0:REWARDS] = rh_ref[...]
    small[8] = og_ref[...]
    small[9] = ln_ref[...]
    small[10:11, 0:CLIPS] = lens_ref[...].astype(f32)
    for c in range(CLIPS):
        small[16 : 16 + REWARDS, c : c + 1] = upright(teacher_ref[c : c + 1])


def upright(row):
    return jnp.sum(jnp.where(eye(), row, 0.0), axis=1, keepdims=True)


def eye():
    side = (REWARDS, REWARDS)
    return lax.broadcasted_iota(jnp.int32, side, 0) == lax.broadcasted_iota(jnp.int32, side, 1)


def pack(clip_frames, teacher, ln_gain, out_gain, reward):
    return call(
        pack_kernel, shape((24, D), f32), [VMEM] * 5, [], 2, "pack", moved=200_000
    )(clip_frames, teacher, ln_gain, out_gain, reward)


def split_kernel(loaded, r0, r2, r1, r3, keep_ref, send_ref):
    core = position()[3]
    for k in range(4):
        for z in range(2):
            rows = [(r0, r1, r2, r3)[k][2 * z + a].astype(f32) for a in range(2)]
            low = jnp.concatenate([r[0:4] for r in rows], axis=0)
            high = jnp.concatenate([r[4:8] for r in rows], axis=0)
            keep_ref[2 * k + z] = jnp.where(core == 0, low, high).astype(bf16)
            send_ref[2 * k + z] = jnp.where(core == 0, high, low).astype(bf16)


def split(parts, loaded):
    return call(
        split_kernel,
        (shape((8, 8, D), bf16),) * 2,
        [VMEM] * 5,
        [],
        4,
        "split",
        moved=600_000,
    )(loaded, *parts)


def load(sources, after, mib):
    def kernel(*refs):
        count = len(sources)
        ins, outs, sems = refs[:count], refs[count + 1 : -1], refs[-1]
        copies = []
        for k, (_, column) in enumerate(sources):
            source = ins[k] if column is None else ins[k].at[:, pl.ds(column, D)]
            copies.append(pltpu.make_async_copy(source, outs[k], sems.at[k]))
        for copy in copies:
            copy.start()
        outs[count][...] = jnp.zeros_like(outs[count])
        for copy in copies:
            copy.wait()

    return call(
        kernel,
        (shape((D, D), bf16),) * len(sources) + (shape((8, 128), f32),),
        [ANY] * (len(sources) + 1),
        [pltpu.SemaphoreType.DMA((len(sources),))],
        mib,
        "load",
        moved=10_000_000,
    )(*[array for array, _ in sources], after)


def forward_kernel(
    x0, x1, wq_ref, wk_ref, wv_ref, wo_ref, small,
    normed_ref, attended_ref, proj_ref, p_ref, cen_ref, inv_ref, tot_ref,
    acc, xs,
):
    tm = lax.axis_index("tm")
    for core, part in enumerate((x0, x1)):
        for k in range(4):
            y = ((tm >> 1) - k) & 3
            for z in range(2):
                xs[((tm & 9) ^ (8 * z + core)) | (2 * y)] = part[2 * k + z].astype(f32)
    x = xs[...].reshape(TOK, D)
    norm, _ = standard(x)
    normed = (norm * small[9:10, :]).astype(bf16)
    normed_ref[...] = normed
    for i, w_ref in enumerate((wq_ref, wk_ref, wv_ref)):
        for j in range(0, D, CHUNK):
            part = dot(normed, w_ref[:, j : j + CHUNK], 1, 0)
            proj_ref[:, i * D + j : i * D + j + CHUNK] = part.astype(bf16)
    row = lax.broadcasted_iota(jnp.int32, (TOK, TOK), 0)
    col = lax.broadcasted_iota(jnp.int32, (TOK, TOK), 1)
    lag = (col >> 2) - (row >> 2)
    allowed = (
        ((row & 3) == (col & 3))
        & (lag >= -(WINDOW // 2))
        & (lag < WINDOW - WINDOW // 2)
        & (clip_of(small, frames((TOK, TOK), 0)) == clip_of(small, frames((TOK, TOK), 1)))
    )
    acc[...] = jnp.zeros_like(acc)
    for h in range(HEADS):
        a, b = span(h)
        mask = lane_mask(h)
        p_ref[h] = dot(proj_ref[:, a:b] * mask, proj_ref[:, D + a : D + b], 1, 1) * SCALE
    for h in range(0, HEADS, GROUP):
        masked = jnp.where(allowed[None], p_ref[h : h + GROUP], -1e30)
        terms = jnp.exp(masked - jnp.max(masked, axis=2, keepdims=True))
        weights = terms / jnp.sum(terms, axis=2, keepdims=True)
        p_ref[h : h + GROUP] = weights
    for h in range(HEADS):
        a, b = span(h)
        acc[:, a:b] += dot(
            p_ref[h].astype(bf16), proj_ref[:, 2 * D + a : 2 * D + b] * lane_mask(h), 1, 0
        )
    attended = acc[...].astype(bf16)
    attended_ref[...] = attended
    mixed = xs[...].reshape(TOK, D) + dot(attended, wo_ref[...], 1, 0)
    centred, inv_std = standard(mixed)
    cen_ref[...] = centred
    inv_ref[...] = jnp.broadcast_to(inv_std, (TOK, 128))
    final = centred * small[8:9, :]
    clip = clip_of(small, frames((TOK, 1), 0))
    tot_ref[...] = jnp.zeros_like(tot_ref)
    for c in range(CLIPS):
        sums = jnp.sum(jnp.where(clip == c, final, 0.0), axis=0, keepdims=True)
        tot_ref[:, c : c + 1] = jnp.sum(small[0:REWARDS, :] * sums, axis=1, keepdims=True)


def forward(x, weights, small):
    return call(
        forward_kernel,
        (
            shape((TOK, D), bf16),
            shape((TOK, D), bf16),
            shape((TOK, 3 * D), bf16),
            shape((HEADS, TOK, TOK), f32),
            shape((TOK, D), f32),
            shape((TOK, 128), f32),
            shape((REWARDS, 8), f32),
        ),
        [VMEM] * 7,
        [pltpu.VMEM((TOK, D), f32), pltpu.VMEM((16, 8, D), f32)],
        24,
        "forward",
        flops=2_000_000_000,
        moved=14_000_000,
    )(*x, *weights, small)


def place_rows(src, dst, where, x_first):
    x, y, z, _ = where
    for k in range(64):
        first, second, kz = k // 16, k // 4 % 4, k % 4
        kx, ky = (first, second) if x_first else (second, first)
        dp = ((z + kz) & 3) * 4 + ((x + kx) & 3)
        start = dp * 72 + ((y + ky) & 3) * PIECE
        dst[PIECE * k : PIECE * (k + 1), :] = src[pl.ds(start, PIECE), :]


def turn_kernel(normed_ref, attended_ref, keep_ref, send_ref, turned, placed):
    where = position()
    core = where[3]
    turned[0] = normed_ref[...].astype(f32).T
    turned[1] = attended_ref[...].astype(f32).T
    place_rows(turned.at[0], placed, where, True)
    keep_ref[0] = placed[...].astype(bf16)
    send_ref[0] = keep_ref[0]
    place_rows(turned.at[core], placed, where, False)
    keep_ref[1] = placed[...].astype(bf16)
    place_rows(turned.at[1 - core], placed, where, False)
    send_ref[1] = placed[...].astype(bf16)


def turn(normed, attended):
    return call(
        turn_kernel,
        (shape((2, D, TOK), bf16), shape((2, D, TOK), bf16)),
        [VMEM] * 2,
        [pltpu.VMEM((2, D, TOK), f32), pltpu.VMEM((D, TOK), f32)],
        8,
        "turn",
        moved=4_000_000,
    )(normed, attended)


def backward_kernel(
    t0, t1, t3, t2, small, proj_ref, p_ref, cen_ref, inv_ref, wo_ref,
    scores_ref, keep_ref, send_ref,
    dq, dk, dv, wg, da_ref,
):
    clip_col = lax.broadcasted_iota(jnp.int32, (REWARDS, 8), 1)
    count = jnp.ones((REWARDS, 8), f32)
    for c in range(CLIPS):
        count = jnp.where(clip_col == c, small[10:11, c : c + 1] * 64.0, count)
    scores = ((t0[...] + t2[...]) + (t1[...] + t3[...])) / count
    scores = scores[:, 0:CLIPS]
    for c in range(CLIPS):
        column = jnp.where(eye(), scores[:, c : c + 1], 0.0)
        scores_ref[c : c + 1, :] = jnp.sum(column, axis=0, keepdims=True)
    residue = (scores - small[16:24, 0:CLIPS]) / ROWS
    clip = clip_of(small, frames((TOK, 1), 0))
    scaled = jnp.zeros((TOK, D), f32)
    for c in range(CLIPS):
        row = jnp.sum(small[0:REWARDS, :] * residue[:, c : c + 1], axis=0, keepdims=True)
        scaled = jnp.where(clip == c, row * small[8:9, :], scaled)
    centred = cen_ref[...]
    mixed_grad = (
        scaled
        - jnp.mean(scaled, axis=-1, keepdims=True)
        - centred * jnp.mean(scaled * centred, axis=-1, keepdims=True)
    ) * inv_ref[:, 0:1]
    mixed_grad = mixed_grad.astype(bf16)
    da_ref[...] = dot(mixed_grad, wo_ref[...], 1, 1).astype(bf16)
    dq[...] = jnp.zeros_like(dq)
    dk[...] = jnp.zeros_like(dk)
    dv[...] = jnp.zeros_like(dv)
    for h in range(HEADS):
        a, b = span(h)
        mask = lane_mask(h)
        wg[h] = dot(da_ref[:, a:b] * mask, proj_ref[:, 2 * D + a : 2 * D + b], 1, 1)
    for h in range(0, HEADS, GROUP):
        weights = p_ref[h : h + GROUP]
        weight_grad = wg[h : h + GROUP]
        inner = jnp.sum(weights * weight_grad, axis=2, keepdims=True)
        wg[h : h + GROUP] = weights * (weight_grad - inner)
    for h in range(HEADS):
        a, b = span(h)
        mask = lane_mask(h)
        logit_grad = wg[h].astype(bf16)
        dq[:, a:b] += dot(logit_grad, proj_ref[:, D + a : D + b] * mask, 1, 0)
        dk[:, a:b] += dot(logit_grad, proj_ref[:, a:b] * mask, 0, 0)
        dv[:, a:b] += dot(p_ref[h].astype(bf16), da_ref[:, a:b] * mask, 0, 0)

    def store(ref_qk, ref_vo):
        ref_qk[0] = (dq[...] * SCALE).astype(bf16)
        ref_qk[1] = (dk[...] * SCALE).astype(bf16)
        ref_vo[0] = dv[...].astype(bf16)
        ref_vo[1] = mixed_grad

    core = position()[3]

    @pl.when(core == 0)
    def _():
        store(keep_ref, send_ref)

    @pl.when(core != 0)
    def _():
        store(send_ref, keep_ref)


def backward(totals, small, proj, p, centred, inv, w_out):
    return call(
        backward_kernel,
        (
            shape((CLIPS, REWARDS), f32),
            shape((2, TOK, D), bf16),
            shape((2, TOK, D), bf16),
        ),
        [VMEM] * 10,
        [pltpu.VMEM((TOK, D), f32)] * 3
        + [
            pltpu.VMEM((HEADS, TOK, TOK), f32),
            pltpu.VMEM((TOK, D), bf16),
        ],
        16,
        "backward",
        flops=1_500_000_000,
        moved=8_000_000,
    )(*totals, small, proj, p, centred, inv, w_out)


def gradient_kernel(lk, lr, rk, rr, *outs):
    for i in range(2):
        on, back, plain, own_on, own_back, own = outs[6 * i : 6 * i + 6]
        right = jnp.concatenate([rk[i], rr[i]], axis=0)
        for k in (2, 3, 1, 0):
            rows = slice(288 * k, 288 * (k + 1))
            left = jnp.concatenate([lk[i, rows], lr[i, rows]], axis=1)
            part = dot(left, right, 1, 0).astype(bf16)
            if k == 2:
                on[...] = part[:144]
                back[0:144] = part[144:]
            elif k == 3:
                back[144:288] = part[:144]
                own_back[...] = part[144:]
            elif k == 1:
                own_on[...] = part[:144]
                plain[...] = part[144:]
            else:
                own[...] = part


def gradient(left_keep, left_recv, right_keep, right_recv):
    rows = (144, 288, 144, 144, 144, 288)
    parts = call(
        gradient_kernel,
        tuple(shape((r, D), bf16) for r in rows) * 2,
        [VMEM] * 4,
        [],
        16,
        "gradient",
        flops=1_400_000_000,
        moved=8_000_000,
    )(left_keep, left_recv, right_keep, right_recv)
    return parts[:6], parts[6:]


def relay_kernel(*refs):
    for k in range(2):
        arrived = refs[k][0:144].astype(f32)
        refs[4 + k][...] = (arrived + refs[2 + k][...].astype(f32)).astype(bf16)


def relay(arrived, own):
    return call(
        relay_kernel,
        (shape((144, D), bf16),) * 2,
        [VMEM] * 4,
        [],
        6,
        "relay",
        moved=2_000_000,
    )(*arrived, *own)


def total(refs):
    result = refs[0][...].astype(f32)
    for ref in refs[1:]:
        result += ref[...].astype(f32)
    return result


SLOT = ((0, 5, 3, 7), (1, 4, 2, 6))


def first_sum_kernel(*refs):
    for i in range(2):
        plain_on, plain_back, relayed_on, relayed_back, own = (refs[2 * j + i] for j in range(5))
        result = own[...].astype(f32) + jnp.concatenate(
            [
                plain_back[144:288].astype(f32) + relayed_on[...].astype(f32),
                plain_on[...].astype(f32) + relayed_back[...].astype(f32),
            ],
            axis=0,
        )
        for k in range(4):
            refs[10 + SLOT[1 - i][k]][...] = result[72 * k : 72 * (k + 1)].astype(bf16)


def first_sum(parts):
    return call(
        first_sum_kernel,
        (shape((72, D), bf16),) * 8,
        [VMEM] * 10,
        [],
        12,
        "first_sum",
        moved=6_000_000,
    )(*parts)


def second_sum_kernel(*refs):
    sums = [total([refs[SLOT[i][k]] for k in range(4)]) for i in (1, 0)]
    rest = jnp.zeros((4, D), f32)
    for k in range(4):
        rows = slice(PIECE * k, PIECE * (k + 1))
        refs[8 + k][...] = jnp.concatenate([sums[0][rows], sums[1][rows], rest], axis=0).astype(
            bf16
        )


def second_sum(parts):
    return call(
        second_sum_kernel,
        (shape((40, D), bf16),) * 4,
        [VMEM] * 8,
        [],
        6,
        "second_sum",
        moved=1_700_000,
    )(*parts)


def sum_kernel(*refs):
    refs[-1][...] = total(refs[:-1]).astype(bf16)


def pair_sum_kernel(a, b, *rest):
    out = rest[-1]
    out[...] = a[...] + b[...]


def pair_sum(a, b, *after):
    specs = [VMEM] * 2 + [ANY] * len(after)
    return call(
        pair_sum_kernel, shape((REWARDS, 8), f32), specs, [], 1, "pair_sum", moved=20_000
    )(a, b, *after)


def plain_sum(parts):
    return call(
        sum_kernel,
        shape(parts[0].shape, bf16),
        [VMEM] * len(parts),
        [],
        3,
        "plain_sum",
        moved=500_000,
    )(*parts)


def stack_kernel(*refs):
    for j, k in enumerate((0, 1, 3, 2)):
        refs[4][k] = refs[j][...]


def stack(parts):
    return call(
        stack_kernel, shape((4, 40, D), bf16), [VMEM] * 4, [], 3, "stack", moved=800_000
    )(*parts)


def last_kernel(mine, other, qkv_ref, out_ref, held):
    _, y_here, _, core = position()
    for k in range(4):
        y = (y_here - k) & 3
        held[core, y] = mine[k].astype(f32)
        held[1 - core, y] = other[k].astype(f32)
    for y in range(4):
        rows = slice(PIECE * y, PIECE * (y + 1))
        qkv_ref[rows, 0:D] = held[0, y, 0:PIECE]
        qkv_ref[rows, D : 2 * D] = held[0, y, PIECE : 2 * PIECE]
        qkv_ref[rows, 2 * D : 3 * D] = held[1, y, 0:PIECE]
        out_ref[rows, :] = held[1, y, PIECE : 2 * PIECE]


def last(mine, other):
    return call(
        last_kernel,
        (shape((72, 3 * D), f32), shape((72, D), f32)),
        [VMEM] * 2,
        [pltpu.VMEM((2, 4, 40, D), f32)],
        10,
        "last",
        moved=2_000_000,
    )(mine, other)


def to_core(block):
    return lax.ppermute(block, "tm", [(i, i ^ 1) for i in range(16)])


def to_far(block):
    return lax.ppermute(block, "tm", [(i, i ^ 8) for i in range(16)])


def along_y(block, k):
    return lax.ppermute(block, "tm", [(i, i & 9 | (i + 2 * k) & 6) for i in range(16)])


def along_x(block, k):
    return lax.ppermute(block, "dp", [(i, i & 12 | (i + k) & 3) for i in range(16)])


def around_z(block, k):
    route = []
    for tm in range(16):
        for dp in range(16):
            step = {1: 1, 3: -1, 2: -2 if tm & 1 else 2}[k]
            z = ((tm >> 3) * 4 + (dp >> 2) + step) & 7
            there = (tm & 7 | (z >> 2) << 3) * 16 + ((z & 3) << 2 | dp & 3)
            route.append((tm * 16 + dp, there))
    return lax.ppermute(block, ("tm", "dp"), route)


def exchange(slots):
    moved = list(slots)
    for k in (2, 1, 3):
        moved[SLOT[1][k]] = along_y(slots[SLOT[1][k]], k)
        moved[SLOT[0][k]] = along_x(slots[SLOT[0][k]], k)
    return moved


def around(x_half, y_half):
    halves = ((x_half, along_x), (y_half, along_y))
    first = [move(half[0], 1) for half, move in halves]
    back = [move(half[1], 3) for half, move in halves]
    plain = [move(half[2], 1) for half, move in halves]
    sums = relay(first, [half[3] for half, _ in halves])
    relayed_on = [move(block, 1) for block, (_, move) in zip(sums, halves)]
    sums = relay(back, [half[4] for half, _ in halves])
    relayed_back = [move(block, 3) for block, (_, move) in zip(sums, halves)]
    return first_sum(plain + back + relayed_on + relayed_back + [x_half[5], y_half[5]])


def on_device(tokens, clip_frames, teacher_scores, ln_gain, w_qkv, w_out, out_gain, reward_head):
    tokens = tokens.reshape(2, 2, 4, 8, D)
    send = lax.dynamic_index_in_dim(tokens, 1 - (lax.axis_index("tm") >> 3), 1, keepdims=False)
    small = pack(clip_frames, teacher_scores[0], ln_gain, out_gain, reward_head.T)
    wq, wk, loaded = load([(w_qkv, 0), (w_qkv, D)], send, 44)
    parts = deal(tokens, to_far(send), small, loaded)
    wv, wo, loaded = load([(w_qkv, 2 * D), (w_out, None)], parts[0], 42)
    weights = wq, wk, wv, wo
    keep, send = split([parts[0]] + [along_y(parts[k], k) for k in (2, 1, 3)], loaded)
    x = [keep, to_core(send)]
    normed, attended, proj, p, centred, inv, partial = forward(x, weights, small)
    partial = pair_sum(partial, to_core(partial))
    normed, attended, _ = lax.optimization_barrier((normed, attended, partial))
    left_keep, left_send = turn(normed, attended)
    left_recv = to_core(left_send)
    partial = pair_sum(partial, to_far(partial), left_keep)
    totals = [partial] + [along_y(partial, k) for k in (1, 3, 2)]
    scores, right_keep, right_send = backward(totals, small, proj, p, centred, inv, weights[3])
    parts = gradient(left_keep, left_recv, right_keep, to_core(right_send))
    parts = second_sum(exchange(around(*parts)))
    part = plain_sum([parts[0]] + [around_z(parts[k], k) for k in (2, 1, 3)])
    part = plain_sum([part, to_far(part)])
    mine = stack([part] + [along_y(part, k) for k in (1, 3, 2)])
    qkv_total, out_total = last(mine, to_core(mine))
    return (scores[None], qkv_total, out_total)


def solution(mesh):
    return jax.shard_map(
        on_device,
        mesh=mesh,
        in_specs=(
            P("dp", "tm", None, None),
            P("dp", None),
            P("dp", None, None),
            P(),
            P(),
            P(),
            P(),
            P(),
        ),
        out_specs=(P("dp", None, None), P("dp", None), P("dp", None)),
        check_vma=False,
    )
```

```python
import math

import jax
import jax.numpy as jnp
from jax import lax
from jax.experimental import pallas as pl
from jax.experimental.pallas import tpu as pltpu
from jax.sharding import PartitionSpec as P

HEADS = 16
HEAD_DIM = 72
WINDOW = 8
D = 1152
TOK = 128
CLIPS = 4
REWARDS = 8
ROWS = 16
CHUNK = 384
PIECE = 18
GROUP = 4
EPS = 1e-06
SCALE = 1.0 / math.sqrt(HEAD_DIM)

f32 = jnp.float32
bf16 = jnp.bfloat16
HI = lax.Precision.HIGHEST
VMEM = pl.BlockSpec(memory_space=pltpu.VMEM)
ANY = pl.BlockSpec(memory_space=pl.ANY)


def dot(a, b, ca, cb, precision=None):
    return lax.dot_general(
        a, b, (((ca,), (cb,)), ((), ())), preferred_element_type=f32, precision=precision
    )


def clip_of(small, frame):
    end, clip = small[10:11, 0:1], jnp.zeros_like(frame)
    for c in range(CLIPS):
        clip += (frame >= end).astype(f32)
        if c + 1 < CLIPS:
            end = end + small[10:11, c + 1 : c + 2]
    return clip


def frames(dims, axis):
    return (lax.broadcasted_iota(jnp.int32, dims, axis) >> 2).astype(f32)


def span(h):
    low = HEAD_DIM * h
    return low // 128 * 128, -(-(low + HEAD_DIM) // 128) * 128


def lane_mask(h):
    start, end = span(h)
    lane = lax.broadcasted_iota(jnp.int32, (1, end - start), 1) + (start - HEAD_DIM * h)
    return ((lane >= 0) & (lane < HEAD_DIM)).astype(f32).astype(bf16)


def standard(values):
    centre = values - jnp.mean(values, axis=-1, keepdims=True)
    inv_std = lax.rsqrt(jnp.mean(centre * centre, axis=-1, keepdims=True) + EPS)
    return centre * inv_std, inv_std


def position():
    tm, dp = lax.axis_index("tm"), lax.axis_index("dp")
    return dp & 3, (tm >> 1) & 3, dp >> 2, tm & 1


def shape(dims, kind):
    return jax.ShapeDtypeStruct(dims, kind)


def call(kernel, out_shape, in_specs, scratch, mib, name, flops=0, moved=0):
    return pl.pallas_call(
        kernel,
        out_shape=out_shape,
        in_specs=in_specs,
        out_specs=jax.tree.map(lambda _: VMEM, out_shape),
        scratch_shapes=scratch,
        compiler_params=pltpu.CompilerParams(vmem_limit_bytes=mib << 20),
        cost_estimate=pl.CostEstimate(flops=flops, bytes_accessed=moved, transcendentals=0),
        name=name,
    )


def deal_kernel(x_ref, far_ref, small, loaded, *outs):
    _, y, _, _ = position()
    z = lax.axis_index("tm") >> 3
    for k in range(4):
        for a in range(2):
            outs[k][a] = x_ref[a, z, (y + k) & 3]
            outs[k][2 + a] = far_ref[a, (y + k) & 3]


def deal(tokens, far, small, loaded):
    return call(
        deal_kernel,
        (shape((4, 8, D), bf16),) * 4,
        [VMEM] * 4,
        [],
        4,
        "deal",
        moved=600_000,
    )(tokens, far, small, loaded)


def pack_kernel(lens_ref, teacher_ref, ln_ref, og_ref, rh_ref, small):
    small[...] = jnp.zeros_like(small)
    small[0:REWARDS] = rh_ref[...]
    small[8] = og_ref[...]
    small[9] = ln_ref[...]
    small[10:11, 0:CLIPS] = lens_ref[...].astype(f32)
    for c in range(CLIPS):
        small[16 : 16 + REWARDS, c : c + 1] = upright(teacher_ref[c : c + 1])


def upright(row):
    return jnp.sum(jnp.where(eye(), row, 0.0), axis=1, keepdims=True)


def eye():
    side = (REWARDS, REWARDS)
    return lax.broadcasted_iota(jnp.int32, side, 0) == lax.broadcasted_iota(jnp.int32, side, 1)


def pack(clip_frames, teacher, ln_gain, out_gain, reward):
    return call(
        pack_kernel, shape((24, D), f32), [VMEM] * 5, [], 2, "pack", moved=200_000
    )(clip_frames, teacher, ln_gain, out_gain, reward)


def split_kernel(loaded, *refs):
    core = position()[3]
    for k in range(4):
        for z in range(2):
            rows = [refs[k][2 * z + a].astype(f32) for a in range(2)]
            low = jnp.concatenate([r[0:4] for r in rows], axis=0)
            high = jnp.concatenate([r[4:8] for r in rows], axis=0)
            refs[4][2 * k + z] = jnp.where(core == 0, low, high).astype(bf16)
            refs[5][2 * k + z] = jnp.where(core == 0, high, low).astype(bf16)


def split(parts, loaded):
    return call(
        split_kernel,
        (shape((8, 8, D), bf16),) * 2,
        [VMEM] * 5,
        [],
        4,
        "split",
        moved=600_000,
    )(loaded, *parts)


def load(sources, after, mib):
    def kernel(*refs):
        count = len(sources)
        ins, outs, sems = refs[:count], refs[count + 1 : -1], refs[-1]
        copies = []
        for k, (_, column) in enumerate(sources):
            source = ins[k] if column is None else ins[k].at[:, pl.ds(column, D)]
            copies.append(pltpu.make_async_copy(source, outs[k], sems.at[k]))
        for copy in copies:
            copy.start()
        outs[count][...] = jnp.zeros_like(outs[count])
        for copy in copies:
            copy.wait()

    return call(
        kernel,
        (shape((D, D), bf16),) * len(sources) + (shape((8, 128), f32),),
        [ANY] * (len(sources) + 1),
        [pltpu.SemaphoreType.DMA((len(sources),))],
        mib,
        "load",
        moved=10_000_000,
    )(*[array for array, _ in sources], after)


def forward_kernel(
    x0, x1, wq_ref, wk_ref, wv_ref, wo_ref, small,
    normed_ref, attended_ref, proj_ref, p_ref, cen_ref, inv_ref, tot_ref,
    acc, xs,
):
    tm = lax.axis_index("tm")
    for core, part in enumerate((x0, x1)):
        for k in range(4):
            y = ((tm >> 1) - k) & 3
            for z in range(2):
                xs[((tm & 9) ^ (8 * z + core)) | (2 * y)] = part[2 * k + z].astype(f32)
    x = xs[...].reshape(TOK, D)
    norm, _ = standard(x)
    normed = (norm * small[9:10, :]).astype(bf16)
    normed_ref[...] = normed
    for i, w_ref in enumerate((wq_ref, wk_ref, wv_ref)):
        for j in range(0, D, CHUNK):
            part = dot(normed, w_ref[:, j : j + CHUNK], 1, 0)
            proj_ref[:, i * D + j : i * D + j + CHUNK] = part.astype(bf16)
    row = lax.broadcasted_iota(jnp.int32, (TOK, TOK), 0)
    col = lax.broadcasted_iota(jnp.int32, (TOK, TOK), 1)
    lag = (col >> 2) - (row >> 2)
    allowed = (
        ((row & 3) == (col & 3))
        & (lag >= -(WINDOW // 2))
        & (lag < WINDOW - WINDOW // 2)
        & (clip_of(small, frames((TOK, TOK), 0)) == clip_of(small, frames((TOK, TOK), 1)))
    )
    acc[...] = jnp.zeros_like(acc)
    for h in range(HEADS):
        a, b = span(h)
        mask = lane_mask(h)
        p_ref[h] = dot(proj_ref[:, a:b] * mask, proj_ref[:, D + a : D + b], 1, 1) * SCALE
    for h in range(0, HEADS, GROUP):
        masked = jnp.where(allowed[None], p_ref[h : h + GROUP], -1e30)
        terms = jnp.exp(masked - jnp.max(masked, axis=2, keepdims=True))
        weights = terms / jnp.sum(terms, axis=2, keepdims=True)
        p_ref[h : h + GROUP] = weights
    for h in range(HEADS):
        a, b = span(h)
        acc[:, a:b] += dot(
            p_ref[h].astype(bf16), proj_ref[:, 2 * D + a : 2 * D + b] * lane_mask(h), 1, 0
        )
    attended = acc[...].astype(bf16)
    attended_ref[...] = attended
    mixed = xs[...].reshape(TOK, D) + dot(attended, wo_ref[...], 1, 0)
    centred, inv_std = standard(mixed)
    cen_ref[...] = centred
    inv_ref[...] = jnp.broadcast_to(inv_std, (TOK, 128))
    final = centred * small[8:9, :]
    clip = clip_of(small, frames((TOK, 1), 0))
    tot_ref[...] = jnp.zeros_like(tot_ref)
    for c in range(CLIPS):
        sums = jnp.sum(jnp.where(clip == c, final, 0.0), axis=0, keepdims=True)
        tot_ref[:, c : c + 1] = jnp.sum(small[0:REWARDS, :] * sums, axis=1, keepdims=True)


def forward(x, weights, small):
    return call(
        forward_kernel,
        (
            shape((TOK, D), bf16),
            shape((TOK, D), bf16),
            shape((TOK, 3 * D), bf16),
            shape((HEADS, TOK, TOK), f32),
            shape((TOK, D), f32),
            shape((TOK, 128), f32),
            shape((REWARDS, 8), f32),
        ),
        [VMEM] * 7,
        [pltpu.VMEM((TOK, D), f32), pltpu.VMEM((16, 8, D), f32)],
        24,
        "forward",
        flops=2_000_000_000,
        moved=14_000_000,
    )(*x, *weights, small)


def place_rows(src, dst, where, x_first):
    x, y, z, _ = where
    for k in range(64):
        first, second, kz = k // 16, k // 4 % 4, k % 4
        kx, ky = (first, second) if x_first else (second, first)
        dp = ((z + kz) & 3) * 4 + ((x + kx) & 3)
        start = dp * 72 + ((y + ky) & 3) * PIECE
        dst[PIECE * k : PIECE * (k + 1), :] = src[pl.ds(start, PIECE), :]


def turn_kernel(normed_ref, attended_ref, keep_ref, send_ref, turned, placed):
    where = position()
    core = where[3]
    turned[0] = normed_ref[...].astype(f32).T
    turned[1] = attended_ref[...].astype(f32).T
    place_rows(turned.at[0], placed, where, True)
    keep_ref[0] = placed[...].astype(bf16)
    send_ref[0] = keep_ref[0]
    place_rows(turned.at[core], placed, where, False)
    keep_ref[1] = placed[...].astype(bf16)
    place_rows(turned.at[1 - core], placed, where, False)
    send_ref[1] = placed[...].astype(bf16)


def turn(normed, attended):
    return call(
        turn_kernel,
        (shape((2, D, TOK), bf16), shape((2, D, TOK), bf16)),
        [VMEM] * 2,
        [pltpu.VMEM((2, D, TOK), f32), pltpu.VMEM((D, TOK), f32)],
        8,
        "turn",
        moved=4_000_000,
    )(normed, attended)


def backward_kernel(
    total_ref, small, proj_ref, p_ref, cen_ref, inv_ref, wo_ref,
    scores_ref, keep_ref, send_ref,
    dq, dk, dv, wg, da_ref,
):
    clip_col = lax.broadcasted_iota(jnp.int32, (REWARDS, 8), 1)
    count = jnp.ones((REWARDS, 8), f32)
    for c in range(CLIPS):
        count = jnp.where(clip_col == c, small[10:11, c : c + 1] * 64.0, count)
    scores = total_ref[...] / count
    scores = scores[:, 0:CLIPS]
    for c in range(CLIPS):
        column = jnp.where(eye(), scores[:, c : c + 1], 0.0)
        scores_ref[c : c + 1, :] = jnp.sum(column, axis=0, keepdims=True)
    residue = (scores - small[16:24, 0:CLIPS]) / ROWS
    clip = clip_of(small, frames((TOK, 1), 0))
    scaled = jnp.zeros((TOK, D), f32)
    for c in range(CLIPS):
        row = jnp.sum(small[0:REWARDS, :] * residue[:, c : c + 1], axis=0, keepdims=True)
        scaled = jnp.where(clip == c, row * small[8:9, :], scaled)
    centred = cen_ref[...]
    mixed_grad = (
        scaled
        - jnp.mean(scaled, axis=-1, keepdims=True)
        - centred * jnp.mean(scaled * centred, axis=-1, keepdims=True)
    ) * inv_ref[:, 0:1]
    mixed_grad = mixed_grad.astype(bf16)
    da_ref[...] = dot(mixed_grad, wo_ref[...], 1, 1).astype(bf16)
    dq[...] = jnp.zeros_like(dq)
    dk[...] = jnp.zeros_like(dk)
    dv[...] = jnp.zeros_like(dv)
    for h in range(HEADS):
        a, b = span(h)
        mask = lane_mask(h)
        wg[h] = dot(da_ref[:, a:b] * mask, proj_ref[:, 2 * D + a : 2 * D + b], 1, 1)
    for h in range(0, HEADS, GROUP):
        weights = p_ref[h : h + GROUP]
        weight_grad = wg[h : h + GROUP]
        inner = jnp.sum(weights * weight_grad, axis=2, keepdims=True)
        wg[h : h + GROUP] = weights * (weight_grad - inner)
    for h in range(HEADS):
        a, b = span(h)
        mask = lane_mask(h)
        logit_grad = wg[h].astype(bf16)
        dq[:, a:b] += dot(logit_grad, proj_ref[:, D + a : D + b] * mask, 1, 0)
        dk[:, a:b] += dot(logit_grad, proj_ref[:, a:b] * mask, 0, 0)
        dv[:, a:b] += dot(p_ref[h].astype(bf16), da_ref[:, a:b] * mask, 0, 0)

    def store(ref_qk, ref_vo):
        ref_qk[0] = (dq[...] * SCALE).astype(bf16)
        ref_qk[1] = (dk[...] * SCALE).astype(bf16)
        ref_vo[0] = dv[...].astype(bf16)
        ref_vo[1] = mixed_grad

    core = position()[3]

    @pl.when(core == 0)
    def _():
        store(keep_ref, send_ref)

    @pl.when(core != 0)
    def _():
        store(send_ref, keep_ref)


def backward(totals, small, proj, p, centred, inv, w_out):
    return call(
        backward_kernel,
        (
            shape((CLIPS, REWARDS), f32),
            shape((2, TOK, D), bf16),
            shape((2, TOK, D), bf16),
        ),
        [VMEM] * 7,
        [pltpu.VMEM((TOK, D), f32)] * 3
        + [
            pltpu.VMEM((HEADS, TOK, TOK), f32),
            pltpu.VMEM((TOK, D), bf16),
        ],
        16,
        "backward",
        flops=1_500_000_000,
        moved=8_000_000,
    )(totals, small, proj, p, centred, inv, w_out)


PARTS = ((2, 0), (2, 1), (1, 1), (3, 0), (1, 0), (3, 1))


def gradient_kernel(lk, lr, rk, rr, *outs):
    for i in range(2):
        right = jnp.concatenate([rk[i], rr[i]], axis=0)
        for k in (2, 1, 3, 0):
            rows = slice(288 * k, 288 * (k + 1))
            left = jnp.concatenate([lk[i, rows], lr[i, rows]], axis=1)
            part = dot(left, right, 1, 0).astype(bf16)
            if k == 0:
                outs[7 * i + 6][...] = part
            else:
                for j, (distance, piece) in enumerate(PARTS):
                    if distance == k:
                        outs[7 * i + j][...] = part[144 * piece : 144 * (piece + 1)]


def gradient(left_keep, left_recv, right_keep, right_recv):
    parts = call(
        gradient_kernel,
        ((shape((144, D), bf16),) * 6 + (shape((288, D), bf16),)) * 2,
        [VMEM] * 4,
        [],
        16,
        "gradient",
        flops=1_400_000_000,
        moved=8_000_000,
    )(left_keep, left_recv, right_keep, right_recv)
    return parts[:7], parts[7:]


def relay_kernel(*refs):
    for k in range(4):
        refs[8 + k][...] = (refs[k][...].astype(f32) + refs[4 + k][...].astype(f32)).astype(bf16)


def relay(arrived, own):
    return call(
        relay_kernel,
        (shape((144, D), bf16),) * 4,
        [VMEM] * 8,
        [],
        8,
        "relay",
        moved=4_000_000,
    )(*arrived, *own)


def total(refs):
    result = refs[0][...].astype(f32)
    for ref in refs[1:]:
        result += ref[...].astype(f32)
    return result


SLOT = ((0, 3, 6, 5), (1, 2, 7, 4))


def first_sum_kernel(*refs):
    for i in range(2):
        plain_on, plain_back, relayed_on, relayed_back, own = (refs[2 * j + i] for j in range(5))
        result = own[...].astype(f32) + jnp.concatenate(
            [
                plain_back[...].astype(f32) + relayed_on[...].astype(f32),
                plain_on[...].astype(f32) + relayed_back[...].astype(f32),
            ],
            axis=0,
        )
        for k in range(4):
            refs[10 + SLOT[1 - i][k]][...] = result[72 * k : 72 * (k + 1)].astype(bf16)


def first_sum(parts):
    return call(
        first_sum_kernel,
        (shape((72, D), bf16),) * 8,
        [VMEM] * 10,
        [],
        12,
        "first_sum",
        moved=6_000_000,
    )(*parts)


def second_sum_kernel(*refs):
    sums = [total([refs[SLOT[i][k]] for k in range(4)]) for i in (1, 0)]
    rest = jnp.zeros((4, D), f32)
    for k in range(4):
        rows = slice(PIECE * k, PIECE * (k + 1))
        refs[8 + k][...] = jnp.concatenate([sums[0][rows], sums[1][rows], rest], axis=0).astype(
            bf16
        )


def second_sum(parts):
    return call(
        second_sum_kernel,
        (shape((40, D), bf16),) * 4,
        [VMEM] * 8,
        [],
        6,
        "second_sum",
        moved=1_700_000,
    )(*parts)


def sum_kernel(*refs):
    refs[-1][...] = total(refs[:-1]).astype(bf16)


def pair_sum_kernel(a, b, *rest):
    out = rest[-1]
    out[...] = a[...] + b[...]


def pair_sum(a, b, *after):
    specs = [VMEM] * 2 + [ANY] * len(after)
    return call(
        pair_sum_kernel, shape((REWARDS, 8), f32), specs, [], 1, "pair_sum", moved=20_000
    )(a, b, *after)


def plain_sum(parts):
    return call(
        sum_kernel,
        shape(parts[0].shape, bf16),
        [VMEM] * len(parts),
        [],
        3,
        "plain_sum",
        moved=500_000,
    )(*parts)


def stack_kernel(*refs):
    for k in range(4):
        refs[4][k] = refs[k][...]


def stack(parts):
    return call(
        stack_kernel, shape((4, 40, D), bf16), [VMEM] * 4, [], 3, "stack", moved=800_000
    )(*parts)


def last_kernel(mine, other, qkv_ref, out_ref, held):
    _, y_here, _, core = position()
    for k in range(4):
        y = (y_here - k) & 3
        held[core, y] = mine[k].astype(f32)
        held[1 - core, y] = other[k].astype(f32)
    for y in range(4):
        rows = slice(PIECE * y, PIECE * (y + 1))
        qkv_ref[rows, 0:D] = held[0, y, 0:PIECE]
        qkv_ref[rows, D : 2 * D] = held[0, y, PIECE : 2 * PIECE]
        qkv_ref[rows, 2 * D : 3 * D] = held[1, y, 0:PIECE]
        out_ref[rows, :] = held[1, y, PIECE : 2 * PIECE]


def last(mine, other):
    return call(
        last_kernel,
        (shape((72, 3 * D), f32), shape((72, D), f32)),
        [VMEM] * 2,
        [pltpu.VMEM((2, 4, 40, D), f32)],
        10,
        "last",
        moved=2_000_000,
    )(mine, other)


def to_core(block):
    return lax.ppermute(block, "tm", [(i, i ^ 1) for i in range(16)])


def to_partner(block, bit):
    return lax.ppermute(block, "tm", [(i, i ^ bit) for i in range(16)])


def to_far(block):
    return lax.ppermute(block, "tm", [(i, i ^ 8) for i in range(16)])


def along_y(block, k):
    return lax.ppermute(block, "tm", [(i, i & 9 | (i + 2 * k) & 6) for i in range(16)])


def along_x(block, k):
    return lax.ppermute(block, "dp", [(i, i & 12 | (i + k) & 3) for i in range(16)])


def around_z(block, k):
    route = []
    for tm in range(16):
        for dp in range(16):
            step = {1: 1, 3: -1, 2: -2 if tm & 1 else 2}[k]
            z = ((tm >> 3) * 4 + (dp >> 2) + step) & 7
            there = (tm & 7 | (z >> 2) << 3) * 16 + ((z & 3) << 2 | dp & 3)
            route.append((tm * 16 + dp, there))
    return lax.ppermute(block, ("tm", "dp"), route)


def exchange(slots):
    moved = list(slots)
    for k in (1, 3, 2):
        moved[SLOT[1][k]] = along_y(slots[SLOT[1][k]], k)
        moved[SLOT[0][k]] = along_x(slots[SLOT[0][k]], k)
    return moved


def around(x_half, y_half):
    on, back = (along_x, along_y), 3
    halves = (x_half, y_half)
    arrived = [on[i](halves[i][j], 1 if j == 0 else back) for j in range(2) for i in range(2)]
    plain = [on[i](halves[i][2 + j], 1 if j == 0 else back) for j in range(2) for i in range(2)]
    own = [halves[i][4 + j] for j in range(2) for i in range(2)]
    sums = relay(arrived, own)
    relayed = [on[i](sums[2 * j + i], 1 if j == 0 else back) for j in range(2) for i in range(2)]
    return first_sum(plain + relayed + [x_half[6], y_half[6]])


def on_device(tokens, clip_frames, teacher_scores, ln_gain, w_qkv, w_out, out_gain, reward_head):
    tokens = tokens.reshape(2, 2, 4, 8, D)
    send = lax.dynamic_index_in_dim(tokens, 1 - (lax.axis_index("tm") >> 3), 1, keepdims=False)
    small = pack(clip_frames, teacher_scores[0], ln_gain, out_gain, reward_head.T)
    wq, wk, loaded = load([(w_qkv, 0), (w_qkv, D)], send, 44)
    parts = deal(tokens, to_far(send), small, loaded)
    wv, wo, loaded = load([(w_qkv, 2 * D), (w_out, None)], parts[0], 42)
    weights = wq, wk, wv, wo
    keep, send = split([parts[0]] + [along_y(parts[k], k) for k in (1, 2, 3)], loaded)
    x = [keep, to_core(send)]
    normed, attended, proj, p, centred, inv, partial = forward(x, weights, small)
    partial = pair_sum(partial, to_core(partial))
    normed, attended, _ = lax.optimization_barrier((normed, attended, partial))
    left_keep, left_send = turn(normed, attended)
    left_recv = to_core(left_send)
    partial = pair_sum(partial, to_far(partial), left_keep)
    for bit in (2, 4):
        partial = pair_sum(partial, to_partner(partial, bit))
    scores, right_keep, right_send = backward(partial, small, proj, p, centred, inv, weights[3])
    parts = gradient(left_keep, left_recv, right_keep, to_core(right_send))
    parts = second_sum(exchange(around(*parts)))
    part = plain_sum([parts[0]] + [around_z(parts[k], k) for k in (1, 2, 3)])
    part = plain_sum([part, to_far(part)])
    mine = stack([part] + [along_y(part, k) for k in (1, 2, 3)])
    qkv_total, out_total = last(mine, to_core(mine))
    return (scores[None], qkv_total, out_total)


def solution(mesh):
    return jax.shard_map(
        on_device,
        mesh=mesh,
        in_specs=(
            P("dp", "tm", None, None),
            P("dp", None),
            P("dp", None, None),
            P(),
            P(),
            P(),
            P(),
            P(),
        ),
        out_specs=(P("dp", None, None), P("dp", None), P("dp", None)),
        check_vma=False,
    )
```
